32 devices in a mesh: dp: 8 (over z, y), ctx: 4 (over x, core).
Axes of the slice: x: 2, y: 2, z: 4, core: 2. Of those that a mesh axis runs over, the one named last changes fastest.
Arguments:
- tokens: bfloat16 [32, 1024, 1472], P('dp', 'ctx'), may hold values from -6 to 6
- soft_mask: bfloat16 [32, 1024], P('dp', 'ctx'), may hold values from -4 to 0
- segment_ids: int32 [32, 1024], P('dp'), may hold values from 0 to 4, as said below
- buckets: int32 [1024, 1024], P('ctx'), may hold values from 0 to 31
- gain_attn: float32 [1472], replicated, may hold values from 0.5 to 1.5
- gain_ffn: float32 [1472], replicated, may hold values from 0.5 to 1.5
- bias_table: float32 [32, 6], replicated, may hold values from -4 to 4
- w_query: bfloat16 [384, 1472], P(('dp', 'ctx')), may hold values from -0.01953125 to 0.01953125
- w_key: bfloat16 [384, 1472], P(('dp', 'ctx')), may hold values from -0.15625 to 0.15625
- w_value: bfloat16 [384, 1472], P(('dp', 'ctx')), may hold values from -0.15625 to 0.15625
- w_attn_out: bfloat16 [384, 1472], P(('dp', 'ctx')), may hold values from -0.875 to 0.875
- w_gate: bfloat16 [3584, 1472], P(('dp', 'ctx')), may hold values from -0.15625 to 0.15625
- w_up: bfloat16 [3584, 1472], P(('dp', 'ctx')), may hold values from -0.15625 to 0.15625
- w_ffn_out: bfloat16 [3584, 1472], P(('dp', 'ctx')), may hold values from -0.1875 to 0.1875
- cotangent: bfloat16 [32, 1024, 1472], P('dp', 'ctx'), may hold values from -6 to 6
Outputs:
- layer_out: bfloat16 [32, 1024, 1472], P('dp', 'ctx')
- grad_tokens: float32 [32, 1024, 1472], P('dp', 'ctx')
- grad_soft_mask: float32 [32, 1024], P('dp', 'ctx')
- grad_gain_attn: float32 [1472], replicated
- grad_gain_ffn: float32 [1472], replicated
- grad_bias_table: float32 [32, 6], replicated
- grad_query: float32 [384, 1472], P(('dp', 'ctx'))
- grad_key: float32 [384, 1472], P(('dp', 'ctx'))
- grad_value: float32 [384, 1472], P(('dp', 'ctx'))
- grad_attn_out: float32 [384, 1472], P(('dp', 'ctx'))
- grad_gate: float32 [3584, 1472], P(('dp', 'ctx'))
- grad_up: float32 [3584, 1472], P(('dp', 'ctx'))
- grad_ffn_out: float32 [3584, 1472], P(('dp', 'ctx'))
The draws below stay inside these ranges and needn't reach their ends.
Inputs may be any that keep to these rules, and one draw needn't show every extreme that they name: `segment_ids`: each row holds up to five documents numbered from 0 in order of position; in every aligned block of 4 rows one row, drawn from the seed, is one whole document.
All inputs are finite; a program needn't handle non-finite values.
Results may differ from the reference program's by a relative error of at most 0.017.
Values may be sent and summed in bfloat16 or wider, within the bound.
No kernel may reach another device: no remote copies, remote signals or barrier semaphores. Data moves between devices by JAX's collectives and lax.ppermute only.
A program may use at most 256 MiB of HBM per device.

```python
import jax
import jax.numpy as jnp
from jax import lax

D = 1472
FF = 3584
HEADS = 6
HEAD_DIM = 64
NB = 32
L = 1024
ROWS_DEV = 4
ROWS = 32
INNER = 384


def draw_segment_ids(key, part):
    key = jax.random.fold_in(key, 11)
    cuts_key, pick_key = jax.random.split(key)
    cuts = jax.random.randint(cuts_key, (ROWS, 4), 1, L)
    picked = jax.random.randint(pick_key, (ROWS // ROWS_DEV,), 0, ROWS_DEV)
    whole_row = jnp.arange(ROWS) % ROWS_DEV == jnp.repeat(picked, ROWS_DEV)
    cuts = jnp.where(whole_row[:, None], L, cuts)
    places = jnp.arange(L)
    return jnp.sum((places[None, :, None] >= cuts[:, None, :]).astype(jnp.int32), axis=-1).astype(jnp.int32)


def place_ends(drawn, own_key, low, high):
    dims = drawn.shape
    spot = [jax.random.randint(jax.random.fold_in(own_key, axis), (), 0, dims[axis]) for axis in range(len(dims))]
    drawn = drawn.at[tuple(spot)].set(low)
    longest = dims.index(max(dims))
    spot[longest] = (spot[longest] + 1) % dims[longest]
    return drawn.at[tuple(spot)].set(high)


def levels(rng, shape, cuts, smallest, high):
    def one(axis_at, parts):
        draws = jax.random.uniform(jax.random.fold_in(jax.random.fold_in(rng, 6), axis_at), (parts,), jnp.float32, smallest / len(cuts), high / len(cuts))
        return jnp.repeat(jnp.exp(draws), shape[axis_at] // parts).reshape((-1,) + (1,) * (len(shape) - axis_at - 1))

    factor_of = one(*cuts[0])
    for cut in cuts[1:]:
        factor_of = factor_of * one(*cut)
    return factor_of


def noise(own_key, dims, deviation, bound, cuts=(), held_as=jnp.bfloat16):
    entries = jax.random.normal(own_key, dims, jnp.float32) * deviation
    if len(cuts) > 0:
        entries = levels(own_key, dims, cuts, -0.22, 0.18) * entries
    return jnp.clip(entries, min=-bound, max=bound).astype(held_as)


def setup_inputs(seed: int = 0) -> dict:
    keys = jax.random.split(jax.random.key(seed), 16)
    tokens = noise(keys[0], (ROWS, L, D), 1.0, 6.0, ((0, 8), (1, 4)))
    soft_mask = jnp.clip(-4.0 + 4.0 * jax.random.uniform(keys[1], (ROWS, L), jnp.float32) ** levels(keys[1], (ROWS, L), ((0, 8), (1, 4)), -0.2, 0.2), -4.0, 0.0).astype(jnp.bfloat16)
    segment_ids = draw_segment_ids(jax.random.fold_in(keys[15], 71), 0)
    buckets = place_ends(jax.random.randint(keys[3], (L, L), 0, NB), jax.random.fold_in(keys[3], 1), 0, NB - 1).astype(jnp.int32)
    gain_attn = jnp.clip(1.0 + 0.1 * jax.random.normal(keys[4], (D,), jnp.float32), 0.5, 1.5)
    gain_ffn = jnp.clip(1.0 + 0.1 * jax.random.normal(keys[5], (D,), jnp.float32), 0.5, 1.5)
    bias_table = noise(keys[6], (NB, HEADS), 1.0, 4.0, (), jnp.float32)
    w_query = noise(keys[7], (INNER, D), (D * HEAD_DIM) ** -0.5, 0.01953125, ((0, 32),))
    w_key = noise(keys[8], (INNER, D), D ** -0.5, 0.15625, ((0, 32),))
    w_value = noise(keys[9], (INNER, D), D ** -0.5, 0.15625, ((0, 32),))
    w_attn_out = noise(keys[10], (INNER, D), (INNER // 8) ** -0.5, 0.875, ((0, 32),))
    w_gate = noise(keys[11], (FF, D), D ** -0.5, 0.15625, ((0, 32),))
    w_up = noise(keys[12], (FF, D), D ** -0.5, 0.15625, ((0, 32),))
    w_ffn_out = noise(keys[13], (FF, D), (FF // 4) ** -0.5, 0.1875, ((0, 32),))
    cotangent = noise(keys[14], (ROWS, L, D), 1.0, 6.0, ((0, 8), (1, 4)))
    return dict(tokens=tokens, soft_mask=soft_mask, segment_ids=segment_ids, buckets=buckets, gain_attn=gain_attn, gain_ffn=gain_ffn, bias_table=bias_table, w_query=w_query, w_key=w_key, w_value=w_value, w_attn_out=w_attn_out, w_gate=w_gate, w_up=w_up, w_ffn_out=w_ffn_out, cotangent=cotangent)


NORM_EPSILON = 1e-06
MASK_VALUE = -1e+30
HIGHEST = lax.Precision.HIGHEST

@jax.custom_vjp
def low(v):
    return lax.optimization_barrier(v.astype(jnp.bfloat16)).astype(jnp.float32)

@jax.custom_vjp
def low_back(v):
    return v

def low_keep(v):
    return (low(v), None)

def low_pass(kept, grad):
    return (grad,)

def back_keep(v):
    return (v, None)

def back_low(kept, grad):
    return (low(grad),)
low.defvjp(low_keep, low_pass)
low_back.defvjp(back_keep, back_low)

def rms_norm(values, gain):
    return values * lax.rsqrt(lax.optimization_barrier(jnp.mean(values * values, axis=-1, keepdims=True)) + NORM_EPSILON) * gain

def attend_row(query_row, key_row, value_row, pos_bias, mask_row, segs_row):
    scores = low_back(jnp.einsum('qhe,khe->hqk', query_row, key_row, precision=HIGHEST))
    logits = scores + pos_bias + mask_row[None, None, :]
    allowed = segs_row[:, None] == segs_row[None, :]
    logits = jnp.where(allowed[None], logits, MASK_VALUE)
    largest = lax.optimization_barrier(jnp.max(logits, axis=-1, keepdims=True))
    expd_vals = jnp.exp(logits - largest)
    probs = expd_vals / lax.optimization_barrier(jnp.sum(expd_vals, axis=-1, keepdims=True))
    return jnp.einsum('hqk,khe->qhe', low(probs), value_row, precision=HIGHEST)

def layer_block(x_rows, mask_rows, seg_rows, pos_bias, params):
    gain_one, gain_two, w_query, w_key, w_value, w_attn_out, w_gate, w_up, w_ffn_out = params
    row_count = x_rows.shape[0]
    normed = low(rms_norm(x_rows, gain_one))

    def project(matrix):
        product = jnp.einsum('rld,ed->rle', normed, matrix, precision=HIGHEST)
        return low_back(low(product)).reshape(row_count, L, HEADS, HEAD_DIM)
    attended = jax.vmap(attend_row, in_axes=(0, 0, 0, None, 0, 0))(project(w_query), project(w_key), project(w_value), pos_bias, mask_rows, seg_rows)
    attended = low_back(low(attended.reshape(row_count, L, INNER)))
    mixed = x_rows + low_back(jnp.einsum('rle,ed->rld', attended, w_attn_out, precision=HIGHEST))
    normed_two = low(rms_norm(mixed, gain_two))
    gate = low_back(jnp.einsum('rld,fd->rlf', normed_two, w_gate, precision=HIGHEST))
    upward = low_back(jnp.einsum('rld,fd->rlf', normed_two, w_up, precision=HIGHEST))
    hidden = low(jax.nn.gelu(gate, approximate=True) * upward)
    return mixed + low_back(jnp.einsum('rlf,fd->rld', hidden, w_ffn_out, precision=HIGHEST))

def reference(tokens, soft_mask, segment_ids, buckets, gain_attn, gain_ffn, bias_table, w_query, w_key, w_value, w_attn_out, w_gate, w_up, w_ffn_out, cotangent):
    group_count = ROWS // ROWS_DEV

    def forward(tok_vals, mask_vals, gain_one, gain_two, table, wq_vals, wk_vals, wv_vals, wo_vals, wg_vals, wu_vals, wf_vals):
        pos_bias = jnp.transpose(table[buckets], (2, 0, 1))
        params = (gain_one, gain_two, wq_vals, wk_vals, wv_vals, wo_vals, wg_vals, wu_vals, wf_vals)

        def group_step(pieces):
            return layer_block(pieces[0], pieces[1], pieces[2], pos_bias, params)
        result = lax.map(jax.checkpoint(group_step), (tok_vals.reshape(group_count, ROWS_DEV, L, D), mask_vals.reshape(group_count, ROWS_DEV, L), segment_ids.reshape(group_count, ROWS_DEV, L)))
        return result.reshape(ROWS, L, D)
    floats = (tokens.astype(jnp.float32), soft_mask.astype(jnp.float32), gain_attn.astype(jnp.float32), gain_ffn.astype(jnp.float32), bias_table.astype(jnp.float32), w_query.astype(jnp.float32), w_key.astype(jnp.float32), w_value.astype(jnp.float32), w_attn_out.astype(jnp.float32), w_gate.astype(jnp.float32), w_up.astype(jnp.float32), w_ffn_out.astype(jnp.float32))
    output, pullback = jax.vjp(forward, *floats)
    grad_tokens, grad_soft_mask, grad_gain_attn, grad_gain_ffn, grad_bias_table, grad_query, grad_key, grad_value, grad_attn_out, grad_gate, grad_up, grad_ffn_out = pullback(cotangent.astype(jnp.float32))
    return (output.astype(jnp.bfloat16), grad_tokens, grad_soft_mask, grad_gain_attn, grad_gain_ffn, grad_bias_table, grad_query, grad_key, grad_value, grad_attn_out, grad_gate, grad_up, grad_ffn_out)
```

```python
import functools

import jax
import jax.numpy as jnp
import numpy as np
from jax import lax
from jax.experimental import pallas as pl
from jax.experimental.pallas import tpu as pltpu
from jax.sharding import PartitionSpec as P

NORM_EPSILON = 1e-06
MASK_VALUE = -1e30
F32, BF16 = jnp.float32, jnp.bfloat16
HEAD = 64
ROW_TILE = 16
AUG = 16
DOCS = 5
ONES = 1 + DOCS
VMEM_LIMIT = 58 * 1024 * 1024
PARAMS = pltpu.CompilerParams(vmem_limit_bytes=VMEM_LIMIT)


def dot(a, b, ca, cb):
    return lax.dot_general(a, b, (((ca,), (cb,)), ((), ())), preferred_element_type=F32)


def whole(shape):
    return pl.BlockSpec(shape, lambda t: (0,) * len(shape), pipeline_mode=pl.Buffered(1))


def cost(flops, nbytes):
    return pl.CostEstimate(flops=int(flops), bytes_accessed=int(nbytes), transcendentals=0)


def norm_body(x_ref, gain_ref, n_ref):
    x = x_ref[0].astype(F32)
    scale = lax.rsqrt(jnp.mean(x * x, axis=0, keepdims=True) + NORM_EPSILON)
    n_ref[...] = (x * scale * gain_ref[...]).astype(BF16)


def first_norm(x, gain):
    rows, width, size = x.shape
    return pl.pallas_call(
        norm_body,
        grid=(rows,),
        in_specs=[pl.BlockSpec((1, width, size), lambda r: (r, 0, 0)), whole(gain.shape)],
        out_specs=pl.BlockSpec((width, size), lambda r: (0, r)),
        out_shape=jax.ShapeDtypeStruct((width, rows * size), BF16),
        compiler_params=PARAMS,
        name="first_norm",
        cost_estimate=cost(4 * x.size, 4 * x.size),
    )(x, gain)


def key_value_body(inner, n_ref, wk_ref, wv_ref, pk_ref, pv_ref, aug_ref, out_ref):
    n = n_ref[...]
    for start, w_ref, p_ref in ((0, wk_ref, pk_ref), (inner, wv_ref, pv_ref)):
        mixed_up = dot(w_ref[...], n, 1, 0).astype(BF16)
        out_ref[0, start : start + inner] = dot(p_ref[...], mixed_up, 1, 0).astype(BF16)
    out_ref[0, 2 * inner :] = aug_ref[0]


def key_value(n, wk, wv, place_k, place_v, aug):
    rows, _, size = aug.shape
    inner = place_k.shape[0]
    width = n.shape[0]
    return pl.pallas_call(
        functools.partial(key_value_body, inner),
        grid=(rows,),
        in_specs=[
            pl.BlockSpec((width, size), lambda r: (0, r)),
            whole(wk.shape),
            whole(wv.shape),
            whole(place_k.shape),
            whole(place_v.shape),
            pl.BlockSpec((1, AUG, size), lambda r: (r, 0, 0)),
        ],
        out_specs=pl.BlockSpec((1, 2 * inner + AUG, size), lambda r: (r, 0, 0)),
        out_shape=jax.ShapeDtypeStruct((rows, 2 * inner + AUG, size), BF16),
        compiler_params=PARAMS,
        name="key_value",
        cost_estimate=cost(4 * wk.size * rows * size, 4 * wk.size + 2 * n.size),
    )(n, wk, wv, place_k, place_v, aug)


def attend_body(heads, inner, q_ref, u_ref, *refs):
    *blocks, bias_ref, o_ref, lse_ref, s_ref = refs
    for h in range(heads):
        part = slice(h * HEAD, (h + 1) * HEAD)
        q = jnp.concatenate([q_ref[part], u_ref[0]], axis=0)
        top = None
        for s, k_ref in enumerate(blocks):
            k = jnp.concatenate([k_ref[0, part], k_ref[0, 2 * inner :]], axis=0)
            logits = dot(k, q, 0, 0) + bias_ref[h, s]
            s_ref[s] = logits
            peak = jnp.max(logits, axis=0, keepdims=True)
            top = peak if top is None else jnp.maximum(top, peak)
        total, out = None, None
        for s, k_ref in enumerate(blocks):
            e = jnp.exp(s_ref[s] - top)
            part_sum = jnp.sum(e, axis=0, keepdims=True)
            total = part_sum if total is None else total + part_sum
            value = k_ref[0, slice(inner + h * HEAD, inner + (h + 1) * HEAD)]
            term = dot(value, e.astype(BF16), 1, 0)
            out = term if out is None else out + term
        o_ref[part] = (out / total).astype(BF16)
        lse_ref[0, h : h + 1] = top + jnp.log(total)
    pad = lse_ref.shape[1] - heads
    if pad:
        lse_ref[0, heads:] = jnp.zeros((pad, lse_ref.shape[2]), F32)


def attend(qt, u, kv, bias, heads):
    rows, depth, size = kv[0].shape
    inner = heads * HEAD
    pad = -(-heads // 8) * 8
    return pl.pallas_call(
        functools.partial(attend_body, heads, inner),
        grid=(rows,),
        in_specs=[
            pl.BlockSpec((inner, size), lambda r: (0, r)),
            pl.BlockSpec((1, AUG, size), lambda r: (r, 0, 0)),
        ]
        + [pl.BlockSpec((1, depth, size), lambda r: (r, 0, 0))] * len(kv)
        + [whole(bias.shape)],
        out_specs=[
            pl.BlockSpec((inner, size), lambda r: (0, r)),
            pl.BlockSpec((1, pad, size), lambda r: (r, 0, 0)),
        ],
        out_shape=[
            jax.ShapeDtypeStruct((inner, rows * size), BF16),
            jax.ShapeDtypeStruct((rows, pad, size), F32),
        ],
        scratch_shapes=[pltpu.VMEM((len(kv), size, size), F32)],
        compiler_params=PARAMS,
        name="attend",
        cost_estimate=cost(16 * rows * heads * len(kv) * size * size * HEAD, 40_000_000),
    )(qt, u, *kv, bias)


def three(x):
    a = x.astype(BF16).astype(F32)
    rest = x - a
    b = rest.astype(BF16).astype(F32)
    return a, b, rest - b


def attend_back_body(heads, inner, count, q_ref, u_ref, *refs):
    blocks = refs[:count]
    bias_ref, o_ref, do_ref, lse_ref, dq_ref = refs[count : count + 5]
    grads = refs[count + 5 : 2 * count + 5]
    gb_ref = refs[2 * count + 5]
    size = bias_ref.shape[3]
    row = pl.program_id(0)
    mask_grad = [None] * count
    extra = u_ref[0].astype(F32)
    place = lax.broadcasted_iota(jnp.int32, (AUG, size), 0)

    def pick(parts, base):
        for i, value in enumerate(parts):
            base = jnp.where(place == ONES + i, value, base)
        return base.astype(BF16)

    for h in range(heads):
        part = slice(h * HEAD, (h + 1) * HEAD)
        vpart = slice(inner + h * HEAD, inner + (h + 1) * HEAD)
        q = q_ref[part]
        do = do_ref[part]
        delta = jnp.sum(do.astype(F32) * o_ref[part].astype(F32), axis=0, keepdims=True)
        q_aug = jnp.concatenate([q, pick(three(-lse_ref[0, h : h + 1]), extra)], axis=0)
        do_aug = jnp.concatenate([do, pick(three(-delta), jnp.zeros_like(extra))], axis=0)
        dq = None
        for s, k_ref in enumerate(blocks):
            k = k_ref[0, part]
            aug = k_ref[0, 2 * inner :]
            logits = dot(jnp.concatenate([k, aug], axis=0), q_aug, 0, 0) + bias_ref[h, s]
            p = jnp.exp(logits)
            dp = dot(jnp.concatenate([k_ref[0, vpart], aug], axis=0), do_aug, 0, 0)
            ds = p * dp

            @pl.when(row == 0)
            def _():
                gb_ref[h, s] = ds

            @pl.when(row > 0)
            def _():
                gb_ref[h, s] += ds

            low = ds.astype(BF16)
            grads[s][0, vpart] = dot(do, p.astype(BF16), 1, 1).astype(BF16)
            both = dot(q_aug, low, 1, 1)
            grads[s][0, part] = both[:HEAD].astype(BF16)
            g = both[HEAD : HEAD + 1]
            mask_grad[s] = g if mask_grad[s] is None else mask_grad[s] + g
            term = dot(k, low, 1, 0)
            dq = term if dq is None else dq + term
        dq_ref[part] = dq.astype(BF16)
    for s in range(count):
        grads[s][0, 2 * inner :] = jnp.broadcast_to(mask_grad[s], (AUG, size)).astype(BF16)


def attend_back(qt, u, kv, bias, ot, dot_t, lse, heads):
    rows, depth, size = kv[0].shape
    inner = heads * HEAD
    count = len(kv)
    col = pl.BlockSpec((inner, size), lambda r: (0, r))
    block = pl.BlockSpec((1, depth, size), lambda r: (r, 0, 0))
    out = pl.pallas_call(
        functools.partial(attend_back_body, heads, inner, count),
        grid=(rows,),
        in_specs=[col, pl.BlockSpec((1, AUG, size), lambda r: (r, 0, 0))]
        + [block] * count
        + [whole(bias.shape), col, col]
        + [pl.BlockSpec((1,) + lse.shape[1:], lambda r: (r, 0, 0))],
        out_specs=[col] + [block] * count + [whole(bias.shape)],
        out_shape=[jax.ShapeDtypeStruct((inner, rows * size), BF16)]
        + [jax.ShapeDtypeStruct((rows, depth, size), BF16)] * count
        + [jax.ShapeDtypeStruct(bias.shape, F32)],
        compiler_params=PARAMS,
        name="attend_back",
        cost_estimate=cost(40 * rows * heads * count * size * size * HEAD, 60_000_000),
    )(qt, u, *kv, bias, ot, dot_t, lse)
    return out[0], out[1:-1], out[-1]


def bias_body(heads, buckets_ref, table_ref, bias_ref):
    tables = [jnp.broadcast_to(table_ref[h : h + 1], (8, 128)) for h in range(heads)]
    for i in range(buckets_ref.shape[1] // 8):
        for j in range(buckets_ref.shape[2] // 128):
            at = (slice(i * 8, (i + 1) * 8), slice(j * 128, (j + 1) * 128))
            index = buckets_ref[(0,) + at]
            for h in range(heads):
                bias_ref[(h, 0) + at] = jnp.take_along_axis(tables[h], index, axis=1)


def bias_of(table, buckets):
    heads = table.shape[0]
    blocks, size, _ = buckets.shape
    return pl.pallas_call(
        functools.partial(bias_body, heads),
        grid=(blocks,),
        in_specs=[pl.BlockSpec((1, size, size), lambda s: (s, 0, 0)), whole(table.shape)],
        out_specs=pl.BlockSpec((heads, 1, size, size), lambda s: (0, s, 0, 0)),
        out_shape=jax.ShapeDtypeStruct((heads, blocks, size, size), F32),
        compiler_params=PARAMS,
        name="bias_of",
        cost_estimate=cost(16 * buckets.size * heads, 4 * buckets.size * (heads + 1)),
    )(buckets, table)


def sums_body(heads, count, buckets_ref, g_ref, out_ref):
    @pl.when(pl.program_id(0) == 0)
    def _():
        out_ref[...] = jnp.zeros_like(out_ref)

    total = out_ref[...]
    for i in range(buckets_ref.shape[1] // 8):
        at = slice(i * 8, (i + 1) * 8)
        index = buckets_ref[0, at]
        hot = [jnp.where(index == b, 1.0, 0.0) for b in range(count)]
        hot = jnp.concatenate(hot, axis=0).astype(BF16)
        g = jnp.concatenate([g_ref[h, 0, at] for h in range(heads)], axis=0)
        high = g.astype(BF16)
        low = (g - high.astype(F32)).astype(BF16)
        total += dot(jnp.concatenate([high, low], axis=0), hot, 1, 1)
    out_ref[...] = total


def bucket_sums(grad_bias, buckets, count):
    heads, blocks, size, _ = grad_bias.shape
    shape = (2 * heads * 8, count * 8)
    raw = pl.pallas_call(
        functools.partial(sums_body, heads, count),
        grid=(blocks,),
        in_specs=[
            pl.BlockSpec((1, size, size), lambda s: (s, 0, 0)),
            pl.BlockSpec((heads, 1, size, size), lambda s: (0, s, 0, 0)),
        ],
        out_specs=pl.BlockSpec(shape, lambda s: (0, 0)),
        out_shape=jax.ShapeDtypeStruct(shape, F32),
        compiler_params=PARAMS,
        name="bucket_sums",
        cost_estimate=cost(64 * grad_bias.size, 4 * grad_bias.size),
    )(buckets, grad_bias)
    raw = raw.reshape(2, heads, 8, count, 8)
    return jnp.sum(jnp.where(jnp.eye(8, dtype=bool)[None, None, :, None, :], raw, 0.0), (0, 2, 4)).T


def mix_body(x_ref, o_ref, w_ref, place_ref, gain_ref, mixed_ref, n_ref):
    spread = dot(place_ref[...], o_ref[...], 0, 0).astype(BF16)
    mixed = x_ref[0].astype(F32) + dot(w_ref[...], spread, 0, 0)
    mixed_ref[...] = mixed
    scale = lax.rsqrt(jnp.mean(mixed * mixed, axis=0, keepdims=True) + NORM_EPSILON)
    n_ref[...] = (mixed * scale * gain_ref[...]).astype(BF16)


def mix(x, ot, w, place, gain):
    rows, width, size = x.shape
    col = pl.BlockSpec((width, size), lambda r: (0, r))
    return pl.pallas_call(
        mix_body,
        grid=(rows,),
        in_specs=[
            pl.BlockSpec((1, width, size), lambda r: (r, 0, 0)),
            pl.BlockSpec((ot.shape[0], size), lambda r: (0, r)),
            whole(w.shape),
            whole(place.shape),
            whole(gain.shape),
        ],
        out_specs=[col, col],
        out_shape=[
            jax.ShapeDtypeStruct((width, rows * size), F32),
            jax.ShapeDtypeStruct((width, rows * size), BF16),
        ],
        compiler_params=PARAMS,
        name="mix",
        cost_estimate=cost(2 * w.size * rows * size, 8 * x.size + 2 * w.size),
    )(x, ot, w, place, gain)


def mix_back_body(
    mixed_ref, d0_ref, d1_ref, dy_ref, o_ref, w_ref, place_ref, gain_ref,
    dmixed_ref, do_ref, gw_ref, gg_ref, acc,
):
    row = pl.program_id(0)
    mixed = mixed_ref[...]
    dn = d0_ref[...] + d1_ref[...].astype(F32)
    scale = lax.rsqrt(jnp.mean(mixed * mixed, axis=0, keepdims=True) + NORM_EPSILON)
    unit = mixed * scale
    scaled = dn * gain_ref[...]
    inside = jnp.mean(scaled * unit, axis=0, keepdims=True)
    dmixed = dy_ref[0].astype(F32) + scale * (scaled - unit * inside)
    dmixed_ref[...] = dmixed
    low = dmixed.astype(BF16)
    spread = dot(place_ref[...], o_ref[...], 0, 0).astype(BF16)
    mixed_up = dot(w_ref[...], low, 1, 0).astype(BF16)
    do_ref[...] = dot(place_ref[...], mixed_up, 1, 0).astype(BF16)
    both = dn * unit
    gain_part = both[:, :128]
    for j in range(1, both.shape[1] // 128):
        gain_part = gain_part + both[:, j * 128 : (j + 1) * 128]
    product = dot(spread, low, 1, 1)

    @pl.when(row == 0)
    def _():
        acc[...] = product
        gg_ref[...] = gain_part

    @pl.when(row > 0)
    def _():
        acc[...] += product
        gg_ref[...] += gain_part

    @pl.when(row == pl.num_programs(0) - 1)
    def _():
        gw_ref[...] = acc[...].astype(BF16)


def mix_back(mixed, d0, d1, dy, ot, w, place, gain):
    rows, width, size = dy.shape
    inner = ot.shape[0]
    col = pl.BlockSpec((width, size), lambda r: (0, r))
    head_col = pl.BlockSpec((inner, size), lambda r: (0, r))
    return pl.pallas_call(
        mix_back_body,
        grid=(rows,),
        in_specs=[
            col,
            col,
            col,
            pl.BlockSpec((1, width, size), lambda r: (r, 0, 0)),
            head_col,
            whole(w.shape),
            whole(place.shape),
            whole(gain.shape),
        ],
        out_specs=[col, head_col, whole(w.shape), whole((width, 128))],
        out_shape=[
            jax.ShapeDtypeStruct((width, rows * size), F32),
            jax.ShapeDtypeStruct((inner, rows * size), BF16),
            jax.ShapeDtypeStruct(w.shape, BF16),
            jax.ShapeDtypeStruct((width, 128), F32),
        ],
        scratch_shapes=[pltpu.VMEM(w.shape, F32)],
        compiler_params=PARAMS,
        name="mix_back",
        cost_estimate=cost(4 * w.size * rows * size, 16 * dy.size + 4 * w.size),
    )(mixed, d0, d1, dy, ot, w, place, gain)


def ffn_body(count, *refs):
    ws = refs[:count]
    n_ref, dy_ref, act_ref = refs[count : count + 3]
    gs = refs[count + 3 : 2 * count + 3]
    acc = refs[2 * count + 3]
    step = pl.program_id(0)
    norm = n_ref[0]
    dy = dy_ref[0]

    @pl.when(step == 0)
    def _():
        acc[...] = jnp.zeros_like(acc)

    start = 0
    for w_ref in ws:
        owners, _, rows, width = w_ref.shape
        size = owners * rows
        part = slice(start, start + size)
        start += size
        gate = dot(w_ref[:, 0].reshape(size, width), norm, 1, 0)
        up = dot(w_ref[:, 1].reshape(size, width), norm, 1, 0)
        dhid = dot(w_ref[:, 2].reshape(size, width), dy, 1, 0)
        square = gate * gate
        tanh = jnp.tanh(gate * (0.7978845608028654 + 0.035677408136300125 * square))
        half = 0.5 + 0.5 * tanh
        gelu = gate * half
        bend = 0.7978845608028654 + 0.10703222440890037 * square
        slope = half + (0.5 * gate) * (1.0 - tanh * tanh) * bend
        hidden = (gelu * up).astype(BF16)
        dgate = (dhid * up * slope).astype(BF16)
        dup = (dhid * gelu).astype(BF16)
        act_ref[0, part] = dgate
        act_ref[1, part] = dup
        act_ref[2, part] = hidden
        acc[0, part] += dot(dgate, norm, 1, 1)
        acc[1, part] += dot(dup, norm, 1, 1)
        acc[2, part] += dot(hidden, dy, 1, 1)

    @pl.when(step == pl.num_programs(0) - 1)
    def _():
        start = 0
        for g_ref in gs:
            owners, _, rows, width = g_ref.shape
            size = owners * rows
            for j in range(3):
                part = acc[j, start : start + size].astype(BF16)
                g_ref[:, j] = part.reshape(owners, rows, width)
            start += size


def ffn_piece(ws, n, dy, tile):
    halves, width, tokens = n.shape
    size = sum(w.shape[0] * w.shape[2] for w in ws)
    per = tokens // tile
    steps = halves * per
    all_tokens = halves * tokens
    column = pl.BlockSpec((1, width, tile), lambda t: (t // per, 0, t % per))
    out = pl.pallas_call(
        functools.partial(ffn_body, len(ws)),
        grid=(steps,),
        in_specs=[whole(w.shape) for w in ws] + [column, column],
        out_specs=[pl.BlockSpec((3, size, tile), lambda t: (0, 0, t))] + [whole(w.shape) for w in ws],
        out_shape=[jax.ShapeDtypeStruct((3, size, all_tokens), BF16)]
        + [jax.ShapeDtypeStruct(w.shape, BF16) for w in ws],
        scratch_shapes=[pltpu.VMEM((3, size, width), F32)],
        compiler_params=PARAMS,
        name="ffn_piece",
        cost_estimate=cost(
            16 * size * width * all_tokens,
            12 * size * width + 2 * (n.size + dy.size + 3 * size * all_tokens),
        ),
    )(*ws, n, dy)
    return out[0], out[1:]


def ffn_back_body(kinds, layout, *refs):
    count = sum(layout)
    ws, acts, out_ref = refs[:count], refs[count:-1], refs[-1]
    total, at = None, 0
    for a_ref, parts in zip(acts, layout):
        start = 0
        for w_ref in ws[at : at + parts]:
            owners, _, rows, width = w_ref.shape
            size = owners * rows
            for k in range(kinds):
                term = dot(w_ref[:, k].reshape(size, width), a_ref[k, start : start + size], 0, 0)
                total = term if total is None else total + term
            start += size
        at += parts
    out_ref[...] = total.astype(out_ref.dtype)


def ffn_back(pieces, acts, which, kinds, start, count, tile, dtype):
    ws = [w for piece in pieces for w in piece]
    width = ws[0].shape[3]
    first = start // tile
    at = which // kinds
    size = sum(a.shape[1] for a in acts)
    return pl.pallas_call(
        functools.partial(ffn_back_body, kinds, [len(piece) for piece in pieces]),
        grid=(count // tile,),
        in_specs=[
            pl.BlockSpec(
                (w.shape[0], kinds) + w.shape[2:],
                lambda t: (0, at, 0, 0),
                pipeline_mode=pl.Buffered(1),
            )
            for w in ws
        ]
        + [pl.BlockSpec((kinds, a.shape[1], tile), lambda t: (at, 0, first + t)) for a in acts],
        out_specs=pl.BlockSpec((width, tile), lambda t: (0, t)),
        out_shape=jax.ShapeDtypeStruct((width, count), dtype),
        compiler_params=PARAMS,
        name="ffn_back",
        cost_estimate=cost(
            2.6 * kinds * size * width * count, 2 * kinds * size * (width + count) + 4 * width * count
        ),
    )(*ws, *acts)


def last_body(
    x_ref, n_ref, dm_ref, dq_ref, dkv_ref, wq_ref, wk_ref, wv_ref, pq_ref, pk_ref, pv_ref,
    gain_ref, gx_ref, gq_ref, gk_ref, gv_ref, gg_ref, acc,
):
    row = pl.program_id(0)
    inner = dq_ref.shape[0]
    n = n_ref[...]
    dn = None

    @pl.when(row == 0)
    def _():
        acc[...] = jnp.zeros_like(acc)

    sources = (dq_ref[...], dkv_ref[0, :inner], dkv_ref[0, inner : 2 * inner])
    for j, (d, w_ref, p_ref) in enumerate(
        zip(sources, (wq_ref, wk_ref, wv_ref), (pq_ref, pk_ref, pv_ref))
    ):
        spread = dot(p_ref[...], d, 0, 0).astype(BF16)
        term = dot(w_ref[...], spread, 0, 0)
        dn = term if dn is None else dn + term
        acc[j] += dot(spread, n, 1, 1)
    x = x_ref[0].astype(F32)
    scale = lax.rsqrt(jnp.mean(x * x, axis=0, keepdims=True) + NORM_EPSILON)
    unit = x * scale
    scaled = dn * gain_ref[...]
    inside = jnp.mean(scaled * unit, axis=0, keepdims=True)
    gx_ref[0] = dm_ref[...] + scale * (scaled - unit * inside)
    both = dn * unit
    gain_part = both[:, :128]
    for j in range(1, both.shape[1] // 128):
        gain_part = gain_part + both[:, j * 128 : (j + 1) * 128]

    @pl.when(row == 0)
    def _():
        gg_ref[...] = gain_part

    @pl.when(row > 0)
    def _():
        gg_ref[...] += gain_part

    @pl.when(row == pl.num_programs(0) - 1)
    def _():
        for j, g_ref in enumerate((gq_ref, gk_ref, gv_ref)):
            g_ref[...] = acc[j].astype(BF16)


def last_plain(x, n, dmixed, dq, dkv, ws, places, gain):
    rows, width, size = x.shape
    inner = dq.shape[0]
    flat = lambda g: jnp.transpose(g, (1, 0, 2)).reshape(g.shape[1], rows * size)
    sources = (dq, flat(dkv[:, :inner]), flat(dkv[:, inner : 2 * inner]))
    spreads = [dot(p, d, 0, 0).astype(BF16) for p, d in zip(places, sources)]
    grads = [dot(s, n, 1, 1).astype(BF16) for s in spreads]
    dn = sum(dot(w, s, 0, 0) for w, s in zip(ws, spreads))
    values = flat(x).astype(F32)
    scale = lax.rsqrt(jnp.mean(values * values, axis=0, keepdims=True) + NORM_EPSILON)
    unit = values * scale
    scaled = dn * gain
    gx = dmixed + scale * (scaled - unit * jnp.mean(scaled * unit, axis=0, keepdims=True))
    gx = jnp.transpose(gx.reshape(width, rows, size), (1, 0, 2))
    return gx, *grads, jnp.sum(dn * unit, axis=1, keepdims=True)


def last(x, n, dmixed, dq, dkv, ws, places, gain):
    rows, width, size = x.shape
    if ws[0].shape[0] > 1024:
        return last_plain(x, n, dmixed, dq, dkv, ws, places, gain)
    inner = dq.shape[0]
    col = pl.BlockSpec((width, size), lambda r: (0, r))
    block = pl.BlockSpec((1, width, size), lambda r: (r, 0, 0))
    shape = ws[0].shape
    return pl.pallas_call(
        last_body,
        grid=(rows,),
        in_specs=[
            block,
            col,
            col,
            pl.BlockSpec((inner, size), lambda r: (0, r)),
            pl.BlockSpec((1,) + dkv.shape[1:], lambda r: (r, 0, 0)),
        ]
        + [whole(w.shape) for w in ws]
        + [whole(p.shape) for p in places]
        + [whole(gain.shape)],
        out_specs=[block] + [whole(shape)] * 3 + [whole((width, 128))],
        out_shape=[jax.ShapeDtypeStruct(x.shape, F32)]
        + [jax.ShapeDtypeStruct(shape, BF16)] * 3
        + [jax.ShapeDtypeStruct((width, 128), F32)],
        scratch_shapes=[pltpu.VMEM((3,) + shape, F32)],
        compiler_params=PARAMS,
        name="last",
        cost_estimate=cost(12 * ws[0].size * rows * size, 14 * x.size + 12 * ws[0].size),
    )(x, n, dmixed, dq, dkv, *ws, *places, gain)


def make_swap(sizes):
    def swap(x, step):
        axis, bit = step
        return lax.ppermute(x, axis, [(i, i ^ bit) for i in range(sizes[axis])])

    return swap


def pad_rows(w, rows):
    return jnp.pad(w, ((0, rows - w.shape[0]), (0, 0))) if rows > w.shape[0] else w


def per_device(
    dp, ctx,
    tokens, soft_mask, segment_ids, buckets, gain_attn, gain_ffn, bias_table,
    w_query, w_key, w_value, w_attn_out, w_gate, w_up, w_ffn_out, cotangent,
):
    sizes = {"dp": dp, "ctx": ctx}
    swap = make_swap(sizes)
    rows, size, width = tokens.shape
    here = rows * size
    count, heads = bias_table.shape
    inner = heads * HEAD
    my_dp, my_ctx = lax.axis_index("dp"), lax.axis_index("ctx")
    me = my_dp * ctx + my_ctx

    core = ("ctx", 1)
    across = [("ctx", 1 << b) for b in range(1, ctx.bit_length() - 1)]
    near = [("dp", 1)] if dp > 1 else []
    far = [("dp", 1 << b) for b in range(1, dp.bit_length() - 1)]
    order_a = far + near + across
    order_b = far + across + near

    def owners_of(order):
        found = [0]
        for axis, bit in order:
            found = found + [f ^ (bit * ctx if axis == "dp" else bit) for f in found]
        return np.array(found, np.int32)

    def spread_of(order):
        each = w_query.shape[0]
        owners = me ^ jnp.asarray(owners_of(order))
        padded = -(-each // ROW_TILE) * ROW_TILE
        inside = jnp.arange(padded)
        feature = owners[:, None] * each + inside[None, :]
        feature = jnp.where(inside[None, :] < each, feature, -1).reshape(-1)
        return (jnp.arange(inner)[:, None] == feature[None, :]).astype(BF16)

    def gather(w, order):
        for step in order:
            w = jnp.concatenate([w, swap(w, step)], axis=0)
        return w

    def reduce(g, order):
        for step in reversed(order):
            half = g.shape[0] // 2
            g = g[:half] + swap(g[half:], step)
        return g[0]

    each = -(-w_query.shape[0] // ROW_TILE) * ROW_TILE
    order_qa, order_qb = order_a + [core], order_b + [core]
    slot = lambda w: pad_rows(w, each)[None]
    wk = gather(slot(w_key), order_qa)
    wv = gather(slot(w_value), order_qb)
    wq = gather(slot(w_query), order_qa)
    wo = gather(slot(w_attn_out), order_qb)
    flat = lambda w: w.reshape(-1, width)
    place_a, place_b = spread_of(order_qa), spread_of(order_qb)

    units = -(-w_gate.shape[0] // ROW_TILE)
    owners = dp * ctx // 2
    piece_units = max(1, 512 // (owners * ROW_TILE))
    stack = jnp.stack([pad_rows(w, units * ROW_TILE) for w in (w_gate, w_up, w_ffn_out)])
    cuts = []
    at = 0
    while at < units:
        take = min(piece_units, units - at)
        cuts.append((at * ROW_TILE, (at + take) * ROW_TILE))
        at += take
    pieces, piece_orders = [], []
    for i, (low, high) in enumerate(cuts):
        order = order_a if i % 2 == 0 else order_b
        w = stack[None, :, low:high]
        w = gather(w, order[:-1])
        pieces.append([w, swap(w, order[-1])])
        piece_orders.append(order)

    x = jnp.transpose(tokens, (0, 2, 1))
    dy = jnp.transpose(cotangent, (0, 2, 1))
    gain_one, gain_two = gain_attn[:, None], gain_ffn[:, None]
    normed = first_norm(x, gain_one)
    dy_own = jnp.transpose(dy, (1, 0, 2)).reshape(width, here)
    dy_pair = jnp.stack([dy_own, swap(dy_own, core)])

    def slots_of(order):
        found = [0]
        for _, bit in order:
            found = found + [f ^ bit for f in found]
        return found

    ctx_order = across + [core]
    slots = slots_of(ctx_order)
    by_block = buckets.reshape(size, ctx, size)
    buckets_t = jnp.stack(
        [
            lax.dynamic_index_in_dim(by_block, my_ctx ^ s, 1, keepdims=False).T
            for s in slots
        ]
    )
    table = jnp.pad(bias_table.T, ((0, 0), (0, 128 - count)))
    bias = bias_of(table, buckets_t)

    segs = lax.dynamic_slice_in_dim(segment_ids, my_ctx * size, size, 1)
    same = segs[:, None, :] == jnp.arange(DOCS, dtype=segs.dtype)[None, :, None]
    ones = jnp.ones((rows, 1, size), BF16)
    rest = AUG - 1 - DOCS
    aug = jnp.concatenate(
        [soft_mask[:, None, :], same.astype(BF16)] + [ones] * 3
        + [jnp.zeros((rows, rest - 3, size), BF16)],
        axis=1,
    )
    query_aug = jnp.concatenate(
        [ones, jnp.where(same, 0.0, MASK_VALUE).astype(BF16), jnp.zeros((rows, rest, size), BF16)],
        axis=1,
    )
    kv_own = key_value(normed, flat(wk), flat(wv), place_a, place_b, aug)
    kv = [kv_own]
    for step in ctx_order:
        kv = kv + [swap(k, step) for k in kv]

    queries = dot(place_a, dot(flat(wq), normed, 1, 0).astype(BF16), 1, 0).astype(BF16)
    attended, lse = attend(queries, query_aug, kv, bias, heads)
    mixed, normed_two = mix(x, attended, flat(wo), place_b, gain_two)
    n_pair = jnp.stack([normed_two, swap(normed_two, core)])

    acts, piece_grads, act_pieces = [], [], []
    for piece, order in zip(pieces, piece_orders):
        total = sum(w.shape[0] * w.shape[2] for w in piece)
        groups = [piece] if total <= 512 else [[w] for w in piece]
        grads = []
        for group in groups:
            act, g = ffn_piece(group, n_pair, dy_pair, min(512, here))
            acts.append(act)
            act_pieces.append(group)
            grads += g
        g = grads[0] + swap(grads[1], order[-1])
        piece_grads.append(reduce(g, order[:-1]))
    tile = min(512, here)
    dn_other = ffn_back(act_pieces, acts, 0, 2, here, here, tile, BF16)
    dn_own = ffn_back(act_pieces, acts, 0, 2, 0, here, tile, F32)
    dn_got = swap(dn_other, core)
    out_other = ffn_back(act_pieces, acts, 2, 1, here, here, tile, BF16)
    out_own = ffn_back(act_pieces, acts, 2, 1, 0, here, tile, F32)
    out_got = swap(out_other, core)
    out = (mixed + out_own + out_got.astype(F32)).astype(BF16)
    layer_out = jnp.transpose(out.reshape(width, rows, size), (1, 2, 0))
    ffn_grads = jnp.concatenate([g.astype(F32) for g in piece_grads], axis=1)
    grad_gate, grad_up, grad_ffn_out = (ffn_grads[j, : w_gate.shape[0]] for j in range(3))

    dmixed, dattended, gwo, gain_two_part = mix_back(
        mixed, dn_own, dn_got, dy, attended, flat(wo), place_b, gain_two
    )
    dq, dkv, grad_bias = attend_back(
        queries, query_aug, kv, bias, attended, dattended, lse, heads
    )
    dkv = list(dkv)
    for step in reversed(ctx_order):
        half = len(dkv) // 2
        dkv = [a + swap(b, step) for a, b in zip(dkv[:half], dkv[half:])]
    dkv = dkv[0]
    grad_table = bucket_sums(grad_bias, buckets_t, count)
    gx, gwq, gwk, gwv, gain_one_part = last(
        x, normed, dmixed, dq, dkv, (flat(wq), flat(wk), flat(wv)), (place_a, place_a, place_b), gain_one
    )
    unflat = lambda g: g.reshape(-1, each, width)
    grad_attn_out = reduce(unflat(gwo), order_qb)
    grad_query = reduce(unflat(gwq), order_qa)
    grad_key = reduce(unflat(gwk), order_qa)
    grad_value = reduce(unflat(gwv), order_qb)
    real = w_query.shape[0]
    attn_grads = [g[:real].astype(F32) for g in (grad_query, grad_key, grad_value, grad_attn_out)]
    small = jnp.concatenate(
        [jnp.sum(gain_one_part, 1), jnp.sum(gain_two_part, 1), grad_table.reshape(-1)]
    )
    length = small.shape[0]
    small = jnp.pad(small, (0, -length % 1024)).reshape(-1, 128)
    for step in order_qa:
        small = small + swap(small, step)
    small = small.reshape(-1)
    return (
        layer_out,
        jnp.transpose(gx, (0, 2, 1)),
        dkv[:, 2 * inner].astype(F32),
        small[:width],
        small[width : 2 * width],
        small[2 * width : length].reshape(count, heads),
        *attn_grads,
        grad_gate,
        grad_up,
        grad_ffn_out,
    )


def solution(mesh):
    split = P(("dp", "ctx"), None)
    act = P("dp", "ctx", None)
    in_specs = (act, P("dp", "ctx"), P("dp", None), P("ctx", None), P(), P(), P()) + (split,) * 7 + (act,)
    out_specs = (act, act, P("dp", "ctx"), P(), P(), P()) + (split,) * 7
    return jax.shard_map(
        functools.partial(per_device, mesh.shape["dp"], mesh.shape["ctx"]),
        mesh=mesh,
        in_specs=in_specs,
        out_specs=out_specs,
        check_vma=False,
    )
```

```python
import functools

import jax
import jax.numpy as jnp
import numpy as np
from jax import lax
from jax.experimental import pallas as pl
from jax.experimental.pallas import tpu as pltpu
from jax.sharding import Mesh, PartitionSpec as P

NORM_EPSILON = 1e-06
MASK_VALUE = -1e30
F32, BF16 = jnp.float32, jnp.bfloat16
HEAD = 64
ROW_TILE = 16
AUG = 16
DOCS = 5
ONES = 1 + DOCS
VMEM_LIMIT = 58 * 1024 * 1024
PARAMS = pltpu.CompilerParams(vmem_limit_bytes=VMEM_LIMIT)


def dot(a, b, ca, cb):
    return lax.dot_general(a, b, (((ca,), (cb,)), ((), ())), preferred_element_type=F32)


def whole(shape):
    return pl.BlockSpec(shape, lambda t: (0,) * len(shape), pipeline_mode=pl.Buffered(1))


def cost(flops, nbytes):
    return pl.CostEstimate(flops=1, bytes_accessed=1, transcendentals=0)


ANY = pl.BlockSpec(memory_space=pl.ANY)


def join(pairs):
    return [jnp.concatenate(list(pair), axis=0) for pair in pairs]


def cut_join(parts, cuts):
    out = []
    for cut in cuts:
        at = np.s_[:, :, cut[0] : cut[0] + cut[1]] if isinstance(cut, tuple) else np.s_[:, cut]
        out.append(jnp.concatenate([p[at] for p in parts], axis=0))
    return out


def fill(pair, parts):
    start = 0
    for part in parts:
        pair = pair.at[1, start : start + part.shape[0]].set(part)
        start += part.shape[0]
    return pair


def add_halves(keep, got):
    out = []
    for k, r in zip(keep, got):
        part = k.shape[0] // 2
        out.append((k[:part] + r[:part], k[part:] + r[part:]))
    return out


def add_merge(keep, got, edges):
    part = keep[0].shape[0] // 2
    ends = [slice(None, part), slice(part, None)]
    return [jnp.concatenate([k[e] + r[e] for k, r in zip(keep, got)], axis=-2) for e in ends]


def add_last(keep, got, edges):
    total = keep[0].astype(F32) + got[0].astype(F32)
    return [total[..., a:b, :] for a, b in zip(edges, edges[1:])]


def add_pairs(pairs):
    return [a + b for a, b in pairs]


PIECES = 4


def pieces_of(shape, tile, first=0):
    rows, columns = shape
    piece = (rows // PIECES, columns)
    specs = [pl.BlockSpec((piece[0], tile), lambda t: (0, first + t)) for _ in range(PIECES)]
    return specs, [jax.ShapeDtypeStruct(piece, BF16)] * PIECES


def put_pieces(refs, value):
    step = refs[0].shape[0]
    for k, ref in enumerate(refs):
        ref[...] = value[k * step : (k + 1) * step]


def norm_body(x_ref, dy_ref, gain_ref, n_ref, pair_ref, *piece_refs):
    x = x_ref[0].astype(F32)
    scale = lax.rsqrt(jnp.mean(x * x, axis=0, keepdims=True) + NORM_EPSILON)
    n_ref[...] = (x * scale * gain_ref[...]).astype(BF16)
    pair_ref[0] = dy_ref[0]
    put_pieces(piece_refs, dy_ref[0])


def first_norm(x, dy, gain):
    rows, width, size = x.shape
    block = pl.BlockSpec((1, width, size), lambda r: (r, 0, 0))
    col = pl.BlockSpec((width, size), lambda r: (0, r))
    here = rows * size
    piece_specs, piece_shapes = pieces_of((width, here), size)
    return pl.pallas_call(
        norm_body,
        grid=(rows,),
        in_specs=[block, block, whole(gain.shape)],
        out_specs=[col, pl.BlockSpec((1, width, size), lambda r: (0, 0, r))] + piece_specs,
        out_shape=[
            jax.ShapeDtypeStruct((width, here), BF16),
            jax.ShapeDtypeStruct((2, width, here), BF16),
        ]
        + piece_shapes,
        compiler_params=PARAMS,
        name="first_norm",
        cost_estimate=cost(4 * x.size, 10 * x.size),
    )(x, dy, gain)


def key_value_body(inner, n_ref, wk_ref, wv_ref, pk_ref, pv_ref, aug_ref, out_ref):
    n = n_ref[...]
    for start, w_ref, p_ref in ((0, wk_ref, pk_ref), (inner, wv_ref, pv_ref)):
        mixed_up = dot(w_ref[...], n, 1, 0).astype(BF16)
        out_ref[0, start : start + inner] = dot(p_ref[...], mixed_up, 1, 0).astype(BF16)
    out_ref[0, 2 * inner :] = aug_ref[0]


def key_value(n, wk, wv, place_k, place_v, aug, first, rows):
    size = aug.shape[2]
    inner = place_k.shape[0]
    width = n.shape[0]
    return pl.pallas_call(
        functools.partial(key_value_body, inner),
        grid=(rows,),
        in_specs=[
            pl.BlockSpec((width, size), lambda r: (0, first + r)),
            whole(wk.shape),
            whole(wv.shape),
            whole(place_k.shape),
            whole(place_v.shape),
            pl.BlockSpec((1, AUG, size), lambda r: (first + r, 0, 0)),
        ],
        out_specs=pl.BlockSpec((1, 2 * inner + AUG, size), lambda r: (r, 0, 0)),
        out_shape=jax.ShapeDtypeStruct((rows, 2 * inner + AUG, size), BF16),
        compiler_params=PARAMS,
        name="key_value",
        cost_estimate=cost(4 * wk.size * rows * size, 4 * wk.size + 2 * n.size),
    )(n, wk, wv, place_k, place_v, aug)


def project_body(n_ref, w_ref, p_ref, out_ref):
    mixed_up = dot(w_ref[...], n_ref[...], 1, 0).astype(BF16)
    out_ref[...] = dot(p_ref[...], mixed_up, 1, 0).astype(BF16)


def project(n, w, place, tile):
    width, here = n.shape
    inner = place.shape[0]
    return pl.pallas_call(
        project_body,
        grid=(here // tile,),
        in_specs=[pl.BlockSpec((width, tile), lambda t: (0, t)), whole(w.shape), whole(place.shape)],
        out_specs=pl.BlockSpec((inner, tile), lambda t: (0, t)),
        out_shape=jax.ShapeDtypeStruct((inner, here), BF16),
        compiler_params=PARAMS,
        name="project",
        cost_estimate=cost(1, 1),
    )(n, w, place)


def attend_body(heads, inner, q_ref, u_ref, *refs):
    *blocks, bias_ref, o_ref, lse_ref, s_ref = refs
    for h in range(heads):
        part = slice(h * HEAD, (h + 1) * HEAD)
        q = jnp.concatenate([q_ref[part], u_ref[0]], axis=0)
        top = None
        for s, k_ref in enumerate(blocks):
            k = jnp.concatenate([k_ref[0, part], k_ref[0, 2 * inner :]], axis=0)
            logits = dot(k, q, 0, 0) + bias_ref[h, s]
            s_ref[s] = logits
            peak = jnp.max(logits, axis=0, keepdims=True)
            top = peak if top is None else jnp.maximum(top, peak)
        total, out = None, None
        for s, k_ref in enumerate(blocks):
            e = jnp.exp(s_ref[s] - top)
            part_sum = jnp.sum(e, axis=0, keepdims=True)
            total = part_sum if total is None else total + part_sum
            value = k_ref[0, slice(inner + h * HEAD, inner + (h + 1) * HEAD)]
            term = dot(value, e.astype(BF16), 1, 0)
            out = term if out is None else out + term
        o_ref[part] = (out / total).astype(BF16)
        lse_ref[0, h : h + 1] = top + jnp.log(total)
    pad = lse_ref.shape[1] - heads
    if pad:
        lse_ref[0, heads:] = jnp.zeros((pad, lse_ref.shape[2]), F32)


def attend(qt, u, kv, bias, heads, first):
    rows, depth, size = kv[0].shape
    inner = heads * HEAD
    pad = -(-heads // 8) * 8
    return pl.pallas_call(
        functools.partial(attend_body, heads, inner),
        grid=(rows,),
        in_specs=[
            pl.BlockSpec((inner, size), lambda r: (0, first + r)),
            pl.BlockSpec((1, AUG, size), lambda r: (first + r, 0, 0)),
        ]
        + [pl.BlockSpec((1, depth, size), lambda r: (r, 0, 0))] * len(kv)
        + [whole(bias.shape)],
        out_specs=[
            pl.BlockSpec((inner, size), lambda r: (0, r)),
            pl.BlockSpec((1, pad, size), lambda r: (r, 0, 0)),
        ],
        out_shape=[
            jax.ShapeDtypeStruct((inner, rows * size), BF16),
            jax.ShapeDtypeStruct((rows, pad, size), F32),
        ],
        scratch_shapes=[pltpu.VMEM((len(kv), size, size), F32)],
        compiler_params=PARAMS,
        name="attend",
        cost_estimate=cost(16 * rows * heads * len(kv) * size * size * HEAD, 40_000_000),
    )(qt, u, *kv, bias)


def three(x):
    a = x.astype(BF16).astype(F32)
    rest = x - a
    b = rest.astype(BF16).astype(F32)
    return a, b, rest - b


def attend_back_body(heads, inner, count, more, q_ref, u_ref, *refs):
    blocks = refs[:count]
    bias_ref, o_ref, do_ref, lse_ref = refs[count : count + 4]
    refs = refs[count + 4 :]
    before_ref, refs = (refs[0], refs[1:]) if more else (None, refs)
    dq_ref = refs[0]
    grads = refs[1 : count + 1]
    gb_ref = refs[count + 1]
    size = bias_ref.shape[3]
    row = pl.program_id(0)
    mask_grad = [None] * count
    extra = u_ref[0].astype(F32)
    place = lax.broadcasted_iota(jnp.int32, (AUG, size), 0)

    def pick(parts, base):
        for i, value in enumerate(parts):
            base = jnp.where(place == ONES + i, value, base)
        return base.astype(BF16)

    for h in range(heads):
        part = slice(h * HEAD, (h + 1) * HEAD)
        vpart = slice(inner + h * HEAD, inner + (h + 1) * HEAD)
        q = q_ref[part]
        do = do_ref[part]
        delta = jnp.sum(do.astype(F32) * o_ref[part].astype(F32), axis=0, keepdims=True)
        q_aug = jnp.concatenate([q, pick(three(-lse_ref[0, h : h + 1]), extra)], axis=0)
        do_aug = jnp.concatenate([do, pick(three(-delta), jnp.zeros_like(extra))], axis=0)
        dq = None
        for s, k_ref in enumerate(blocks):
            k = k_ref[0, part]
            aug = k_ref[0, 2 * inner :]
            logits = dot(jnp.concatenate([k, aug], axis=0), q_aug, 0, 0) + bias_ref[h, s]
            p = jnp.exp(logits)
            dp = dot(jnp.concatenate([k_ref[0, vpart], aug], axis=0), do_aug, 0, 0)
            ds = p * dp

            @pl.when(row == 0)
            def _():
                gb_ref[h, s] = before_ref[h, s] + ds if more else ds

            @pl.when(row > 0)
            def _():
                gb_ref[h, s] += ds

            low = ds.astype(BF16)
            grads[s][0, vpart] = dot(do, p.astype(BF16), 1, 1).astype(BF16)
            both = dot(q_aug, low, 1, 1)
            grads[s][0, part] = both[:HEAD].astype(BF16)
            g = both[HEAD : HEAD + 1]
            mask_grad[s] = g if mask_grad[s] is None else mask_grad[s] + g
            term = dot(k, low, 1, 0)
            dq = term if dq is None else dq + term
        dq_ref[part] = dq.astype(BF16)
    for s in range(count):
        grads[s][0, 2 * inner :] = jnp.broadcast_to(mask_grad[s], (AUG, size)).astype(BF16)


def attend_back(qt, u, kv, bias, ot, dot_t, lse, heads, first, before):
    rows, depth, size = kv[0].shape
    inner = heads * HEAD
    count = len(kv)
    own = pl.BlockSpec((inner, size), lambda r: (0, r))
    col = pl.BlockSpec((inner, size), lambda r: (0, first + r))
    block = pl.BlockSpec((1, depth, size), lambda r: (r, 0, 0))
    out = pl.pallas_call(
        functools.partial(attend_back_body, heads, inner, count, len(before)),
        grid=(rows,),
        in_specs=[col, pl.BlockSpec((1, AUG, size), lambda r: (first + r, 0, 0))]
        + [block] * count
        + [whole(bias.shape), own, col]
        + [pl.BlockSpec((1,) + lse.shape[1:], lambda r: (r, 0, 0))]
        + [whole(b.shape) for b in before],
        out_specs=[own] + [block] * count + [whole(bias.shape)],
        out_shape=[jax.ShapeDtypeStruct((inner, rows * size), BF16)]
        + [jax.ShapeDtypeStruct((rows, depth, size), BF16)] * count
        + [jax.ShapeDtypeStruct(bias.shape, F32)],
        compiler_params=PARAMS,
        name="attend_back",
        cost_estimate=cost(40 * rows * heads * count * size * size * HEAD, 60_000_000),
    )(qt, u, *kv, bias, ot, dot_t, lse, *before)
    return out[0], out[1:-1], out[-1]


def bias_body(heads, slots_ref, buckets_ref, table_ref, bias_ref, buckets_t_ref):
    tables = [jnp.broadcast_to(table_ref[h : h + 1], (8, 128)) for h in range(heads)]
    buckets_t_ref[0] = buckets_ref[...].T
    for i in range(buckets_ref.shape[1] // 8):
        for j in range(buckets_ref.shape[0] // 128):
            at = (slice(i * 8, (i + 1) * 8), slice(j * 128, (j + 1) * 128))
            index = buckets_t_ref[(0,) + at]
            for h in range(heads):
                bias_ref[(h, 0) + at] = jnp.take_along_axis(tables[h], index, axis=1)


def bias_of(slots, buckets, table):
    heads = table.shape[0]
    size, blocks = buckets.shape[0], slots.shape[0]
    spec = pltpu.PrefetchScalarGridSpec(
        num_scalar_prefetch=1,
        grid=(blocks,),
        in_specs=[
            pl.BlockSpec((size, size), lambda s, slots: (0, slots[s])),
            pl.BlockSpec(table.shape, lambda s, slots: (0, 0)),
        ],
        out_specs=[
            pl.BlockSpec((heads, 1, size, size), lambda s, slots: (0, s, 0, 0)),
            pl.BlockSpec((1, size, size), lambda s, slots: (s, 0, 0)),
        ],
    )
    return pl.pallas_call(
        functools.partial(bias_body, heads),
        grid_spec=spec,
        out_shape=[
            jax.ShapeDtypeStruct((heads, blocks, size, size), F32),
            jax.ShapeDtypeStruct((blocks, size, size), jnp.int32),
        ],
        compiler_params=PARAMS,
        name="bias_of",
        cost_estimate=cost(1, 1),
    )(slots, buckets, table)


def sums_body(heads, count, buckets_ref, g_ref, out_ref):
    @pl.when(pl.program_id(0) == 0)
    def _():
        out_ref[...] = jnp.zeros_like(out_ref)

    total = out_ref[...]
    for i in range(buckets_ref.shape[1] // 8):
        at = slice(i * 8, (i + 1) * 8)
        index = buckets_ref[0, at]
        hot = [jnp.where(index == b, 1.0, 0.0) for b in range(count)]
        hot = jnp.concatenate(hot, axis=0).astype(BF16)
        g = jnp.concatenate([g_ref[h, 0, at] for h in range(heads)], axis=0)
        high = g.astype(BF16)
        low = (g - high.astype(F32)).astype(BF16)
        total += dot(jnp.concatenate([high, low], axis=0), hot, 1, 1)
    out_ref[...] = total


def bucket_sums(grad_bias, buckets, count):
    heads, blocks, size, _ = grad_bias.shape
    shape = (2 * heads * 8, count * 8)
    raw = pl.pallas_call(
        functools.partial(sums_body, heads, count),
        grid=(blocks,),
        in_specs=[
            pl.BlockSpec((1, size, size), lambda s: (s, 0, 0)),
            pl.BlockSpec((heads, 1, size, size), lambda s: (0, s, 0, 0)),
        ],
        out_specs=pl.BlockSpec(shape, lambda s: (0, 0)),
        out_shape=jax.ShapeDtypeStruct(shape, F32),
        compiler_params=PARAMS,
        name="bucket_sums",
        cost_estimate=cost(64 * grad_bias.size, 4 * grad_bias.size),
    )(buckets, grad_bias)
    raw = raw.reshape(2, heads, 8, count, 8)
    return jnp.sum(jnp.where(jnp.eye(8, dtype=bool)[None, None, :, None, :], raw, 0.0), (0, 2, 4)).T


def mix_body(x_ref, o_ref, w_ref, place_ref, gain_ref, mixed_ref, pair_ref, *piece_refs):
    spread = dot(place_ref[...], o_ref[...], 0, 0).astype(BF16)
    mixed = x_ref[0].astype(F32) + dot(w_ref[...], spread, 0, 0)
    mixed_ref[...] = mixed
    scale = lax.rsqrt(jnp.mean(mixed * mixed, axis=0, keepdims=True) + NORM_EPSILON)
    n = (mixed * scale * gain_ref[...]).astype(BF16)
    pair_ref[0] = n
    put_pieces(piece_refs, n)


def group_specs(shape, count, per, rank):
    def place(g):
        def index(r):
            inside = jnp.clip(r - g * per, 0, per - 1)
            return (0, inside) if rank == 2 else (inside, 0, 0)

        return index

    return [pl.BlockSpec(shape, place(g)) for g in range(count)]


def mix(x, ot, w, place, gain):
    rows, width, size = x.shape
    inner = ot.shape[0]
    here = rows * size
    piece_specs, piece_shapes = pieces_of((width, here), size)
    return pl.pallas_call(
        mix_body,
        grid=(rows,),
        in_specs=[
            pl.BlockSpec((1, width, size), lambda r: (r, 0, 0)),
            pl.BlockSpec((inner, size), lambda r: (0, r)),
            whole(w.shape),
            whole(place.shape),
            whole(gain.shape),
        ],
        out_specs=[
            pl.BlockSpec((width, size), lambda r: (0, r)),
            pl.BlockSpec((1, width, size), lambda r: (0, 0, r)),
        ]
        + piece_specs,
        out_shape=[
            jax.ShapeDtypeStruct((width, here), F32),
            jax.ShapeDtypeStruct((2, width, here), BF16),
        ]
        + piece_shapes,
        compiler_params=PARAMS,
        name="mix",
        cost_estimate=cost(1, 1),
    )(x, ot, w, place, gain)


def units_of(ws):
    return sum(w.shape[0] * w.shape[2] for w in ws)


def entries_of(ws):
    return sum(w.shape[0] for w in ws)


def loads_of(refs, buf, sems, kinds):
    copies, start = [], 0
    for a, ref in enumerate(refs):
        for k, kind in enumerate(kinds):
            inside = buf.at[k, pl.ds(start, ref.shape[0])]
            copies.append(pltpu.make_async_copy(ref.at[:, kind], inside, sems.at[a, k]))
        start += ref.shape[0]
    return copies


def ffn_body(count, masks, me_ref, *refs):
    ws, (n_ref, dy_ref, act_ref), refs = refs[:count], refs[count : count + 3], refs[count + 3 :]
    gs, (buf, acc, in_sems, out_sems) = refs[:-4], refs[-4:]
    t = pl.program_id(0)
    entries, rows, width = buf.shape[1:]
    size = entries * rows
    loads = loads_of(ws, buf, in_sems, range(3))

    @pl.when(t == 0)
    def _():
        for copy in loads:
            copy.start()
        acc[...] = jnp.zeros_like(acc)
        for copy in loads:
            copy.wait()

    norm = n_ref[0]
    dy = dy_ref[0]
    gate = dot(buf[0].reshape(size, width), norm, 1, 0)
    up = dot(buf[1].reshape(size, width), norm, 1, 0)
    dhid = dot(buf[2].reshape(size, width), dy, 1, 0)
    inside = gate * (0.7978845608028654 + 0.035677408136300125 * (gate * gate))
    half = 0.5 + 0.5 * jnp.tanh(inside)
    gelu = gate * half
    slope = half * (1.0 + (1.0 - half) * (6.0 * inside - 3.1915382432114616 * gate))
    dgate = (dhid * up * slope).astype(BF16)
    dup = (dhid * gelu).astype(BF16)
    hidden = (gelu * up).astype(BF16)
    act_ref[0] = dgate
    act_ref[1] = dup
    act_ref[2] = hidden
    acc[0] += dot(dgate, norm, 1, 1)
    acc[1] += dot(dup, norm, 1, 1)
    acc[2] += dot(hidden, dy, 1, 1)

    @pl.when(t == pl.num_programs(0) - 1)
    def _():
        for k in range(3):
            buf[k] = acc[k].astype(BF16).reshape(entries, rows, width)
        stores = []
        if masks is None:
            start = 0
            for g, out in enumerate(gs):
                for k in range(3):
                    inside = buf.at[k, pl.ds(start, out.shape[0])]
                    stores.append(pltpu.make_async_copy(inside, out.at[:, k], out_sems.at[g, k]))
                start += out.shape[0]
        else:
            part = len(masks) // 2
            for s, mask in enumerate(masks):
                for k in range(3):
                    inside, out = buf.at[k, me_ref[0] ^ mask], gs[s // part].at[s % part, k]
                    stores.append(pltpu.make_async_copy(inside, out, out_sems.at[s, k]))
        for copy in stores:
            copy.start()
        for copy in stores:
            copy.wait()


def ffn_group(me, ws, n, dy, tile, masks=None):
    halves, width, tokens = n.shape
    per = tokens // tile
    all_tokens = halves * tokens
    size = units_of(ws)
    inner = (entries_of(ws),) + ws[0].shape[2:]
    column = pl.BlockSpec((1, width, tile), lambda t, me: (t // per, 0, t % per))
    stores = len(ws) if masks is None else len(masks)
    shapes = [w.shape for w in ws]
    if masks is not None:
        shapes = [(inner[0] // 2, 3) + inner[1:]] * 2
    spec = pltpu.PrefetchScalarGridSpec(
        num_scalar_prefetch=1,
        grid=(halves * per,),
        in_specs=[ANY] * len(ws) + [column, column],
        out_specs=[pl.BlockSpec((3, size, tile), lambda t, me: (0, 0, t))] + [ANY] * len(shapes),
        scratch_shapes=[
            pltpu.VMEM((3,) + inner, BF16),
            pltpu.VMEM((3, size, width), F32),
            pltpu.SemaphoreType.DMA((len(ws), 3)),
            pltpu.SemaphoreType.DMA((stores, 3)),
        ],
    )
    out = pl.pallas_call(
        functools.partial(ffn_body, len(ws), masks),
        grid_spec=spec,
        out_shape=[jax.ShapeDtypeStruct((3, size, all_tokens), BF16)]
        + [jax.ShapeDtypeStruct(shape, BF16) for shape in shapes],
        compiler_params=PARAMS,
        name="ffn_group",
        cost_estimate=cost(1, 1),
    )(me, *ws, n, dy)
    return out[0], out[1:]


def ffn_terms(layout, kinds, refs):
    count, total = len(layout), sum(layout)
    ws, acts, refs = refs[:total], refs[total : total + count], refs[total + count :]
    bufs, sems = refs[:count], refs[count]

    @pl.when(pl.program_id(0) == 0)
    def _():
        copies, start = [], 0
        for p, arrays in enumerate(layout):
            copies += loads_of(ws[start : start + arrays], bufs[p], sems.at[p], kinds)
            start += arrays
        for copy in copies:
            copy.start()
        for copy in copies:
            copy.wait()

    out = None
    for act, buf in zip(acts, bufs):
        _, entries, rows, width = buf.shape
        for k in range(len(kinds)):
            term = dot(buf[k].reshape(entries * rows, width), act[k], 0, 0)
            out = term if out is None else out + term
    return out


def layout_of(groups):
    return tuple(len(ws) for ws in groups)


def flat_of(groups):
    return [w for ws in groups for w in ws]


def ffn_specs(groups, acts, kinds, tile, first):
    at = kinds[0] // len(kinds)
    return [ANY] * len(flat_of(groups)) + [
        pl.BlockSpec((len(kinds), a.shape[1], tile), lambda t: (at, 0, first + t)) for a in acts
    ]


def ffn_scratch(groups, kinds):
    return [
        pltpu.VMEM((len(kinds), entries_of(ws)) + ws[0].shape[2:], BF16) for ws in groups
    ] + [pltpu.SemaphoreType.DMA((len(groups), max(layout_of(groups)), len(kinds)))]


def ffn_back_body(layout, kinds, *refs):
    ins = sum(layout) + len(layout)
    total = ffn_terms(layout, kinds, refs[:ins] + refs[ins + PIECES :])
    put_pieces(refs[ins : ins + PIECES], total.astype(BF16))


def ffn_back(groups, acts, kinds, start, count, tile):
    width = groups[0][0].shape[3]
    piece_specs, piece_shapes = pieces_of((width, count), tile)
    return pl.pallas_call(
        functools.partial(ffn_back_body, layout_of(groups), kinds),
        grid=(count // tile,),
        in_specs=ffn_specs(groups, acts, kinds, tile, start // tile),
        out_specs=piece_specs,
        out_shape=piece_shapes,
        scratch_shapes=ffn_scratch(groups, kinds),
        compiler_params=PARAMS,
        name="ffn_back",
        cost_estimate=cost(1, 1),
    )(*flat_of(groups), *acts)


def layer_out_body(layout, *refs):
    ins = sum(layout) + len(layout)
    mixed_ref, out_ref = refs[ins], refs[ins + 1 + PIECES]
    got = jnp.concatenate([r[...] for r in refs[ins + 1 : ins + 1 + PIECES]], axis=0)
    total = ffn_terms(layout, [2], refs[:ins] + refs[ins + 2 + PIECES :])
    out_ref[0] = (mixed_ref[...] + total + got.astype(F32)).astype(BF16)


def layer_out_of(groups, acts, mixed, got, rows):
    width, here = mixed.shape
    size = here // rows
    col = pl.BlockSpec((width, size), lambda t: (0, t))
    return pl.pallas_call(
        functools.partial(layer_out_body, layout_of(groups)),
        grid=(rows,),
        in_specs=ffn_specs(groups, acts, [2], size, 0) + [col] + pieces_of(mixed.shape, size)[0],
        out_specs=pl.BlockSpec((1, width, size), lambda t: (t, 0, 0)),
        out_shape=jax.ShapeDtypeStruct((rows, width, size), BF16),
        scratch_shapes=ffn_scratch(groups, [2]),
        compiler_params=PARAMS,
        name="layer_out_of",
        cost_estimate=cost(1, 1),
    )(*flat_of(groups), *acts, mixed, *got)


def mix_back_body(layout, *refs):
    ins = sum(layout) + len(layout)
    weights, refs = refs[:ins], refs[ins:]
    pieces, refs = refs[:PIECES], refs[PIECES:]
    mixed_ref, dy_ref, o_ref, w_ref, place_ref, gain_ref = refs[:6]
    refs = refs[6:]
    inside_grad = len(refs) == 6 + len(layout) + 1
    dmixed_ref, do_ref, gg_ref = refs[:3]
    low_ref, high_ref, acc = refs[3:6] if inside_grad else (None, None, None)
    row = pl.program_id(0)
    got = jnp.concatenate([r[...] for r in pieces], axis=0)
    dn = ffn_terms(layout, [0, 1], weights + refs[-len(layout) - 1 :]) + got.astype(F32)
    mixed = mixed_ref[...]
    scale = lax.rsqrt(jnp.mean(mixed * mixed, axis=0, keepdims=True) + NORM_EPSILON)
    unit = mixed * scale
    scaled = dn * gain_ref[...]
    inside = jnp.mean(scaled * unit, axis=0, keepdims=True)
    dmixed = dy_ref[0].astype(F32) + scale * (scaled - unit * inside)
    dmixed_ref[...] = dmixed
    low = dmixed.astype(BF16)
    spread = dot(place_ref[...], o_ref[...], 0, 0).astype(BF16)
    mixed_up = dot(w_ref[...], low, 1, 0).astype(BF16)
    do_ref[...] = dot(place_ref[...], mixed_up, 1, 0).astype(BF16)
    both = dn * unit
    gain_part = both[:, :128]
    for j in range(1, both.shape[1] // 128):
        gain_part = gain_part + both[:, j * 128 : (j + 1) * 128]

    @pl.when(row == 0)
    def _():
        gg_ref[...] = gain_part

    @pl.when(row > 0)
    def _():
        gg_ref[...] += gain_part

    if inside_grad:
        product = dot(spread, low, 1, 1)

        @pl.when(row == 0)
        def _():
            acc[...] = product

        @pl.when(row > 0)
        def _():
            acc[...] += product

        @pl.when(row == pl.num_programs(0) - 1)
        def _():
            half = low_ref.shape[0]
            low_ref[...] = acc[:half].astype(BF16)
            high_ref[...] = acc[half:].astype(BF16)


def mix_back(groups, acts, mixed, d1, dy, ot, w, place, gain):
    rows, width, size = dy.shape
    inner = ot.shape[0]
    here = rows * size
    col = pl.BlockSpec((width, size), lambda r: (0, r))
    head_col = pl.BlockSpec((inner, size), lambda r: (0, r))
    fits = w.shape[0] <= 1024
    half = (w.shape[0] // 2, width)
    out = pl.pallas_call(
        functools.partial(mix_back_body, layout_of(groups)),
        grid=(rows,),
        in_specs=ffn_specs(groups, acts, [0, 1], size, 0)
        + pieces_of(mixed.shape, size)[0]
        + [col, pl.BlockSpec((1, width, size), lambda r: (r, 0, 0)), head_col]
        + [whole(w.shape), whole(place.shape), whole(gain.shape)],
        out_specs=[col, head_col, whole((width, 128))] + [whole(half)] * (2 * fits),
        out_shape=[
            jax.ShapeDtypeStruct((width, here), F32),
            jax.ShapeDtypeStruct((inner, here), BF16),
            jax.ShapeDtypeStruct((width, 128), F32),
        ]
        + [jax.ShapeDtypeStruct(half, BF16)] * (2 * fits),
        scratch_shapes=[pltpu.VMEM(w.shape, F32)] * fits + ffn_scratch(groups, [0, 1]),
        compiler_params=PARAMS,
        name="mix_back",
        cost_estimate=cost(1, 1),
    )(*flat_of(groups), *acts, *d1, mixed, dy, ot, w, place, gain)
    if not fits:
        spread = dot(place, ot, 0, 0).astype(BF16)
        product = dot(spread, out[0].astype(BF16), 1, 1).astype(BF16)
        out = [*out, product[: half[0]], product[half[0] :]]
    return out


def grads_body(per, groups, parts, n_ref, *refs):
    d_refs, refs = refs[:groups], refs[groups:]
    places, refs = refs[: len(parts)], refs[len(parts) :]
    outs, (acc, d_scr) = refs[: 2 * len(parts)], refs[2 * len(parts) :]
    row = pl.program_id(0)
    n = n_ref[...]
    for g, d_ref in enumerate(d_refs):

        @pl.when(row // per == g)
        def _():
            d_scr[...] = d_ref[...].reshape(d_scr.shape)

    products = []
    for (start, stop), p_ref in zip(parts, places):
        spread = dot(p_ref[...], d_scr[start:stop], 0, 0).astype(BF16)
        products.append(dot(spread, n, 1, 1))

    @pl.when(row == 0)
    def _():
        for j, product in enumerate(products):
            acc[j] = product

    @pl.when(row > 0)
    def _():
        for j, product in enumerate(products):
            acc[j] += product

    @pl.when(row == pl.num_programs(0) - 1)
    def _():
        half = acc.shape[1] // 2
        for j in range(len(parts)):
            outs[2 * j][...] = acc[j, :half].astype(BF16)
            outs[2 * j + 1][...] = acc[j, half:].astype(BF16)


def projection_grads(n, groups, parts, places, rows):
    if len(parts) > 1 and places[0].shape[1] > 1024:
        return [
            half
            for part, p in zip(parts, places)
            for half in projection_grads(n, groups, [part], [p], rows)
        ]
    width, here = n.shape
    size = here // rows
    per = rows // len(groups)
    rank = groups[0].ndim
    depth = groups[0].shape[-2]
    shape = (depth, size) if rank == 2 else (1, depth, size)
    wide = (places[0].shape[1], width)
    return pl.pallas_call(
        functools.partial(grads_body, per, len(groups), parts),
        grid=(rows,),
        in_specs=[pl.BlockSpec((width, size), lambda r: (0, r))]
        + group_specs(shape, len(groups), per, rank)
        + [whole(p.shape) for p in places],
        out_specs=[whole((wide[0] // 2, width))] * (2 * len(parts)),
        out_shape=[jax.ShapeDtypeStruct((wide[0] // 2, width), BF16)] * (2 * len(parts)),
        scratch_shapes=[pltpu.VMEM((len(parts),) + wide, F32), pltpu.VMEM((depth, size), BF16)],
        compiler_params=PARAMS,
        name="projection_grads",
        cost_estimate=cost(
            2 * len(parts) * wide[0] * width * here, 2 * n.size + 2 * len(parts) * wide[0] * width
        ),
    )(n, *groups, *places)


def last_body(per, groups, x_ref, dm_ref, *refs):
    dq_refs, dkv_refs, refs = refs[:groups], refs[groups : 2 * groups], refs[2 * groups :]
    ws, places, refs = refs[:3], refs[3:6], refs[6:]
    gain_ref, gx_ref, gg_ref, d_scr = refs
    row = pl.program_id(0)
    inner = dq_refs[0].shape[0]
    for g in range(groups):

        @pl.when(row // per == g)
        def _():
            d_scr[:inner] = dq_refs[g][...]
            d_scr[inner:] = dkv_refs[g][0, : 2 * inner]

    dn = None
    for j in range(3):
        spread = dot(places[j][...], d_scr[j * inner : (j + 1) * inner], 0, 0).astype(BF16)
        term = dot(ws[j][...], spread, 0, 0)
        dn = term if dn is None else dn + term
    x = x_ref[0].astype(F32)
    scale = lax.rsqrt(jnp.mean(x * x, axis=0, keepdims=True) + NORM_EPSILON)
    unit = x * scale
    scaled = dn * gain_ref[...]
    inside = jnp.mean(scaled * unit, axis=0, keepdims=True)
    gx_ref[0] = dm_ref[...] + scale * (scaled - unit * inside)
    both = dn * unit
    gain_part = both[:, :128]
    for j in range(1, both.shape[1] // 128):
        gain_part = gain_part + both[:, j * 128 : (j + 1) * 128]

    @pl.when(row == 0)
    def _():
        gg_ref[...] = gain_part

    @pl.when(row > 0)
    def _():
        gg_ref[...] += gain_part


def last(x, dmixed, dqs, dkvs, ws, places, gain):
    rows, width, size = x.shape
    inner = dqs[0].shape[0]
    per = rows // len(dqs)
    col = pl.BlockSpec((width, size), lambda r: (0, r))
    block = pl.BlockSpec((1, width, size), lambda r: (r, 0, 0))
    return pl.pallas_call(
        functools.partial(last_body, per, len(dqs)),
        grid=(rows,),
        in_specs=[block, col]
        + group_specs((inner, size), len(dqs), per, 2)
        + group_specs((1,) + dkvs[0].shape[1:], len(dkvs), per, 3)
        + [whole(w.shape) for w in ws]
        + [whole(p.shape) for p in places]
        + [whole(gain.shape)],
        out_specs=[block, whole((width, 128))],
        out_shape=[jax.ShapeDtypeStruct(x.shape, F32), jax.ShapeDtypeStruct((width, 128), F32)],
        scratch_shapes=[pltpu.VMEM((3 * inner, size), BF16)],
        compiler_params=PARAMS,
        name="last",
        cost_estimate=cost(6 * ws[0].size * rows * size, 14 * x.size + 6 * ws[0].size),
    )(x, dmixed, *dqs, *dkvs, *ws, *places, gain)


def after(value, *markers):
    return lax.optimization_barrier((value, markers))[0]


def pad_rows(w, rows):
    return jnp.pad(w, ((0, rows - w.shape[0]), (0, 0))) if rows > w.shape[0] else w


class Links:
    def __init__(self, dp, pairs):
        self.sizes = {"dp": dp, "x": pairs, "core": 2}
        self.strides = {"dp": 2 * pairs, "x": 2, "core": 1}
        self.core = ("core", 1)
        self.across = ("x", 1)
        self.near = ("dp", 1)
        self.far_count = dp // 2

    def swap(self, x, step):
        axis, mask = step
        return lax.ppermute(x, axis, [(i, i ^ mask) for i in range(self.sizes[axis])])

    def far_steps(self):
        return [("dp", k << 1) for k in range(1, self.far_count)]

    def far_bits(self):
        return [("dp", 2 << b) for b in range(self.far_count.bit_length() - 1)]

    def masks(self, steps):
        found = [(k << 1) * self.strides["dp"] for k in range(self.far_count)]
        for axis, mask in steps:
            found = found + [f ^ (mask * self.strides[axis]) for f in found]
        return found


def per_device(
    dp, ctx,
    tokens, soft_mask, segment_ids, buckets, gain_attn, gain_ffn, bias_table,
    w_query, w_key, w_value, w_attn_out, w_gate, w_up, w_ffn_out, cotangent,
):
    links = Links(dp, ctx // 2)
    swap, core, across, near = links.swap, links.core, links.across, links.near
    far = links.far_steps()
    rows, size, width = tokens.shape
    here = rows * size
    count, heads = bias_table.shape
    inner = heads * HEAD
    my_dp, my_ctx = lax.axis_index("dp"), lax.axis_index("x") * 2 + lax.axis_index("core")
    me = my_dp * ctx + my_ctx
    tile = min(512, here)
    order_a, order_b = [near, across], [across, near]

    def spread_of(steps):
        real = w_query.shape[0]
        owners = me ^ jnp.asarray(links.masks(steps), dtype=jnp.int32)
        inside = jnp.arange(each)
        feature = owners[:, None] * real + inside[None, :]
        feature = jnp.where(inside[None, :] < real, feature, -1).reshape(-1)
        return (jnp.arange(inner)[:, None] == feature[None, :]).astype(BF16)

    token = []

    def run(work, *args):
        if token:
            args = lax.optimization_barrier((args, tuple(token)))[0]
        out = work(*args)
        token[:] = jax.tree.leaves(out)[:1]
        return out

    each = -(-w_query.shape[0] // ROW_TILE) * ROW_TILE
    slot = lambda w: pad_rows(w, each)[None]
    flat = lambda w: w.reshape(-1, width)
    far_bits = links.far_bits()
    ab, ba = (near, across), (across, near)

    def exchange(arrays, steps):
        return [(a, swap(a, step)) for a, step in zip(arrays, steps)]

    def swap_core(value):
        return [swap(v, core) for v in value]

    def close(value):
        return run(lambda v: v, value)

    class Gather:
        def __init__(self, array, cuts, direct=False, mark=None, paths=(ab, ba)):
            if mark is not None:
                array = after(array, mark)
            self.cuts, self.stage, self.paths = cuts, 0, paths
            self.hops = 1 if direct else len(far_bits)
            steps = far if direct else far_bits[:1]
            self.held = [array] + [swap(array, step) for step in steps]

        def go(self):
            self.stage += 1
            if self.stage < self.hops:
                (array,) = run(lambda *p: join([p]), *self.held)
                self.held = [array, swap(array, far_bits[self.stage])]
            elif self.stage == self.hops:
                parts = run(lambda *p: cut_join(list(p), self.cuts), *self.held)
                self.held = exchange(parts, self.paths[0])
            elif self.stage == self.hops + 1:
                self.held = exchange(run(join, self.held), self.paths[1])

        def start_of(self):
            first = self.held[0]
            return first[0] if isinstance(first, tuple) else first

        def core_go(self):
            self.held = exchange(run(join, self.held), (core, core))

        def core_end(self):
            return run(join, self.held)

    units = -(-w_gate.shape[0] // ROW_TILE)
    padded = [pad_rows(w, units * ROW_TILE) for w in (w_gate, w_up, w_ffn_out)]
    marks = [0, 3, 5, 7] if units == 7 else list(range(units + 1))
    shards = [
        jnp.stack([w[low * ROW_TILE : high * ROW_TILE] for w in padded])
        for low, high in zip(marks, marks[1:])
    ]
    attn_w = Gather(
        jnp.concatenate([slot(w) for w in (w_key, w_attn_out, w_value, w_query)], axis=1)[:, None],
        [(0, 2 * each), (2 * each, 2 * each)],
        direct=True,
    )
    same_core = ("dp", "x")
    by_hops = units == 7
    last_group = len(shards) - 1

    x = jnp.transpose(tokens, (0, 2, 1))
    dy = jnp.transpose(cotangent, (0, 2, 1))
    gain_one, gain_two = gain_attn[:, None], gain_ffn[:, None]
    place_a, place_b = spread_of(order_a + [core]), spread_of(order_b + [core])
    segs = lax.dynamic_slice_in_dim(segment_ids, my_ctx * size, size, 1)
    same = segs[:, None, :] == jnp.arange(DOCS, dtype=segs.dtype)[None, :, None]
    ones = jnp.ones((rows, 1, size), BF16)
    rest = AUG - 1 - DOCS
    aug = jnp.concatenate(
        [soft_mask[:, None, :], same.astype(BF16)] + [ones] * 3
        + [jnp.zeros((rows, rest - 3, size), BF16)],
        axis=1,
    )
    query_aug = jnp.concatenate(
        [ones, jnp.where(same, 0.0, MASK_VALUE).astype(BF16), jnp.zeros((rows, rest, size), BF16)],
        axis=1,
    )
    normed, dy_pair, *dy_own = run(first_norm, x, dy, gain_one)

    attn_w.go()
    ffn_w = [
        [lax.all_gather(after(shard, attn_w.start_of()), same_core)]
        for shard in (shards[:-1] if by_hops else shards)
    ]
    slots = jnp.array([0, 2, 1, 3], jnp.int32) ^ my_ctx
    bias, buckets_t = run(
        bias_of, slots, buckets, jnp.pad(bias_table.T, ((0, 0), (0, 128 - count)))
    )
    dy_parts = swap_core(dy_own)
    attn_w.go()
    dy_pair = run(fill, dy_pair, dy_parts)
    attn_w.core_go()
    wko, wvq = attn_w.core_end()
    pick = lambda w, k: w[:, 0, k * each : (k + 1) * each].reshape(-1, width)
    wk, wo, wv, wq = run(lambda a, b: [pick(a, 0), pick(a, 1), pick(b, 0), pick(b, 1)], wko, wvq)
    kv_own = run(lambda *a: key_value(*a, 0, rows), normed, wk, wv, place_a, place_b, aug)
    kv_across = swap(kv_own, across)
    kv_core = swap(kv_own, core)
    if by_hops:
        last_w = Gather(
            shards[-1][None], [(0, shards[-1].shape[1])], mark=kv_own, paths=((across,), (near,))
        )
    queries = run(lambda n, w, p: project(n, w, p, tile), normed, wq, place_b)
    kv_core = close(kv_core)
    if by_hops:
        last_w.go()

    kv = run(lambda *k: list(k), kv_own, kv_across, kv_core)
    kv.append(close(jnp.concatenate([swap(k, core) for k in jnp.split(kv[1], rows)])))
    attended, lse = run(lambda *a: attend(*a, heads, 0), queries, query_aug, kv, bias)
    if by_hops:
        last_w.go()
    mixed, n_pair, *normed_two = run(mix, x, attended, wo, place_a, gain_two)
    n_parts = close(swap_core(normed_two))
    if by_hops:
        last_w.go()
    n_pair = run(fill, n_pair, n_parts)

    class Sums:
        def __init__(self, grads, paths):
            self.paths = paths[: len(grads)]
            self.stage = 0
            self.send(grads)

        def send(self, halves):
            self.keep = [h[0] for h in halves]
            self.got = [swap(h[1], p[self.stage]) for h, p in zip(halves, self.paths)]

        def go(self):
            near_hops = len(self.paths[0])
            hops = near_hops + len(far_bits)
            self.stage += 1
            if self.stage > hops:
                return
            if self.stage < near_hops:
                self.send(run(add_halves, self.keep, self.got))
                return
            if self.stage == near_hops:
                rows_of = [k.shape[-2] for k in self.keep]
                self.edges = [sum(rows_of[:k]) for k in range(len(rows_of) + 1)]
                halves = run(lambda k, r: add_merge(k, r, self.edges), self.keep, self.got)
            elif self.stage < hops:
                halves = run(add_halves, self.keep, self.got)[0]
            else:
                self.out = run(lambda k, r: add_last(k[0], r[0], self.edges), self.keep, self.got)
                return
            self.keep = [halves[0]]
            self.got = [swap(halves[1], far_bits[hops - 1 - self.stage])]

    acts, sums = [], []
    me_same = (my_dp * (ctx // 2) + lax.axis_index("x")).reshape(1)
    masks = [[m >> 1 for m in links.masks(steps)] for steps in (ab, ba)]
    ffn_grads = []
    if by_hops:
        ffn_w.append(last_w.held[0])
    for i, ws in enumerate(ffn_w):
        some = tile if units_of(ws) <= 768 else tile // 2
        mask = masks[0] if by_hops and i == last_group - 1 else None
        if i == last_group and by_hops:
            ws = ffn_w[i] = close(list(ws))
        act, grads = run(
            lambda m, w, n, d: ffn_group(m, w, n, d, some, mask), me_same, ws, n_pair, dy_pair
        )
        acts.append(act)
        if by_hops and i >= last_group - 1:
            ffn_grads.append(grads)
        else:
            ffn_grads.append(lax.psum_scatter(grads[0], same_core))
    if by_hops:
        sums = [Sums(ffn_grads[-2:], [ba, ab])]

    def tick():
        for s in sums:
            s.go()

    back = run(lambda p, a: ffn_back(p, a, [0, 1], here, here, tile), ffn_w, acts)
    dn_parts = swap_core(back)
    out_other = run(lambda p, a: ffn_back(p, a, [2], here, here, tile), ffn_w, acts)
    dn_got = close(dn_parts)
    dmixed, dattended, gain_two_part, *gwo = run(
        mix_back, ffn_w, acts, mixed, dn_got, dy, attended, wo, place_a, gain_two
    )
    tick()
    dq, dkv, grad_bias = run(
        lambda *a: attend_back(*a, heads, 0, []),
        queries, query_aug, kv, bias, attended, dattended, lse,
    )
    tick()
    out_got = swap_core(out_other)
    by_core = [(dkv[0], swap(dkv[2], core)), (dkv[1], swap(dkv[3], core))]
    own, other = run(add_pairs, by_core)
    other = swap(other, across)
    entries = lambda g: tuple(v.reshape(-1, each, width) for v in g)
    home_a, home_b = (core,) + ba, (core,) + ab
    gwq = run(
        lambda n, d, p: projection_grads(n, [d], [(0, inner)], [p], rows), normed, dq, place_b
    )
    query_sum = Sums([entries(gwo), entries(gwq)], [home_a, home_b])
    grad_table = run(lambda g, b: bucket_sums(g, b, count), grad_bias, buckets_t)
    query_sum.go()
    out_got = close(out_got)
    query_sum.go()
    out = run(lambda *a: layer_out_of(*a, rows), ffn_w, acts, mixed, out_got)
    query_sum.go()
    (dkv,) = run(add_pairs, [(own, other)])
    gkv = run(
        lambda n, d, pa, pb: projection_grads(n, [d], [(0, inner), (inner, 2 * inner)], [pa, pb], rows),
        normed, dkv, place_a, place_b,
    )
    value_sum = Sums([entries(gkv[:2]), entries(gkv[2:])], [home_a, home_b])
    tick()
    value_sum.go()
    gx, gain_one_part = run(
        lambda *a: last(a[0], a[1], [a[2]], [a[3]], a[4:7], a[7:10], a[10]),
        x, dmixed, dq, dkv, wq, wk, wv, place_b, place_a, place_b, gain_one,
    )
    value_sum.go()
    query_sum.go()
    tick()
    small = jnp.concatenate(
        [jnp.sum(gain_one_part, 1), jnp.sum(gain_two_part, 1), grad_table.reshape(-1)]
    )
    length = small.shape[0]
    small = jnp.pad(small, (0, -length % 1024)).reshape(-1, 128)
    bits = [core, across] + [("dp", 1 << b) for b in range(dp.bit_length() - 1)]
    for k, one in enumerate(bits):
        got = swap(small, one)
        if k in (1, 2, 3):
            value_sum.go()
        small = run(lambda a, b: a + b, small, got)
    for _ in range(len(far_bits) + 4):
        for s in [query_sum, value_sum] + sums:
            s.go()
    small = small.reshape(-1)
    real = w_query.shape[0]
    if by_hops:
        ffn_grads[-2:] = sums[0].out
    grad_gate, grad_up, grad_ffn_out = (
        jnp.concatenate([g[j].astype(F32) for g in ffn_grads])[: w_gate.shape[0]] for j in range(3)
    )
    return (
        jnp.transpose(out, (0, 2, 1)),
        jnp.transpose(gx, (0, 2, 1)),
        dkv[:, 2 * inner].astype(F32),
        small[:width],
        small[width : 2 * width],
        small[2 * width : length].reshape(count, heads),
        query_sum.out[1][:real],
        value_sum.out[0][:real],
        value_sum.out[1][:real],
        query_sum.out[0][:real],
        grad_gate,
        grad_up,
        grad_ffn_out,
    )


def solution(mesh):
    dp, ctx = mesh.shape["dp"], mesh.shape["ctx"]
    by_core = Mesh(mesh.devices.reshape(dp, ctx // 2, 2), ("dp", "x", "core"))
    ctx_axes = ("x", "core")
    split = P(("dp", "x", "core"), None)
    act = P("dp", ctx_axes, None)
    in_specs = (
        (act, P("dp", ctx_axes), P("dp", None), P(ctx_axes, None), P(), P(), P()) + (split,) * 7 + (act,)
    )
    out_specs = (act, act, P("dp", ctx_axes), P(), P(), P()) + (split,) * 7
    return jax.shard_map(
        functools.partial(per_device, dp, ctx),
        mesh=by_core,
        in_specs=in_specs,
        out_specs=out_specs,
        check_vma=False,
    )
```

```python
import functools

import jax
import jax.numpy as jnp
import numpy as np
from jax import lax
from jax.experimental import pallas as pl
from jax.experimental.pallas import tpu as pltpu
from jax.sharding import Mesh, PartitionSpec as P

NORM_EPSILON = 1e-06
MASK_VALUE = -1e30
F32, BF16 = jnp.float32, jnp.bfloat16
HEAD = 64
ROW_TILE = 16
AUG = 16
DOCS = 5
ONES = 1 + DOCS
VMEM_LIMIT = 58 * 1024 * 1024
PARAMS = pltpu.CompilerParams(vmem_limit_bytes=VMEM_LIMIT)


def dot(a, b, ca, cb):
    return lax.dot_general(a, b, (((ca,), (cb,)), ((), ())), preferred_element_type=F32)


def whole(shape):
    return pl.BlockSpec(shape, lambda t: (0,) * len(shape), pipeline_mode=pl.Buffered(1))


def cost(flops, nbytes):
    return pl.CostEstimate(flops=1, bytes_accessed=1, transcendentals=0)


ANY = pl.BlockSpec(memory_space=pl.ANY)


def join(pairs):
    return [jnp.concatenate(list(pair), axis=0) for pair in pairs]


def cut_join(parts, cuts):
    out = []
    for cut in cuts:
        at = np.s_[:, :, cut[0] : cut[0] + cut[1]] if isinstance(cut, tuple) else np.s_[:, cut]
        out.append(jnp.concatenate([p[at] for p in parts], axis=0))
    return out


def fill(pair, parts):
    start = 0
    for part in parts:
        pair = pair.at[1, start : start + part.shape[0]].set(part)
        start += part.shape[0]
    return pair


def add_halves(keep, got):
    out = []
    for k, r in zip(keep, got):
        part = k.shape[0] // 2
        out.append((k[:part] + r[:part], k[part:] + r[part:]))
    return out


def add_merge(keep, got, edges):
    part = keep[0].shape[0] // 2
    ends = [slice(None, part), slice(part, None)]
    return [jnp.concatenate([k[e] + r[e] for k, r in zip(keep, got)], axis=-2) for e in ends]


def add_piles(keep, got, edges):
    return [
        jnp.concatenate([k[i : i + 1] + r[i : i + 1] for k, r in zip(keep, got)], axis=-2)
        for i in range(keep[0].shape[0])
    ]


def add_last(keep, got, edges):
    total = keep[0].astype(F32)
    for r in got:
        total = total + r[0].astype(F32)
    return [total[..., a:b, :] for a, b in zip(edges, edges[1:])]


def add_pairs(pairs):
    return [a + b for a, b in pairs]


PIECES = 4


def pieces_of(shape, tile, pieces=PIECES):
    rows, columns = shape
    piece = (rows // pieces, columns)
    specs = [pl.BlockSpec((piece[0], tile), lambda t: (0, t)) for _ in range(pieces)]
    return specs, [jax.ShapeDtypeStruct(piece, BF16)] * pieces


def put_pieces(refs, value):
    step = refs[0].shape[0]
    for k, ref in enumerate(refs):
        ref[...] = value[k * step : (k + 1) * step]


def norm_body(x_ref, dy_ref, gain_ref, n_ref, pair_ref, *piece_refs):
    x = x_ref[0].astype(F32)
    scale = lax.rsqrt(jnp.mean(x * x, axis=0, keepdims=True) + NORM_EPSILON)
    n_ref[...] = (x * scale * gain_ref[...]).astype(BF16)
    pair_ref[0] = dy_ref[0]
    put_pieces(piece_refs, dy_ref[0])


def first_norm(x, dy, gain):
    rows, width, size = x.shape
    block = pl.BlockSpec((1, width, size), lambda r: (r, 0, 0))
    col = pl.BlockSpec((width, size), lambda r: (0, r))
    here = rows * size
    piece_specs, piece_shapes = pieces_of((width, here), size)
    return pl.pallas_call(
        norm_body,
        grid=(rows,),
        in_specs=[block, block, whole(gain.shape)],
        out_specs=[col, pl.BlockSpec((1, width, size), lambda r: (0, 0, r))] + piece_specs,
        out_shape=[
            jax.ShapeDtypeStruct((width, here), BF16),
            jax.ShapeDtypeStruct((2, width, here), BF16),
        ]
        + piece_shapes,
        compiler_params=PARAMS,
        name="first_norm",
        cost_estimate=cost(4 * x.size, 10 * x.size),
    )(x, dy, gain)


def key_value_body(inner, n_ref, wk_ref, wv_ref, pk_ref, pv_ref, aug_ref, out_ref):
    n = n_ref[...]
    for start, w_ref, p_ref in ((0, wk_ref, pk_ref), (inner, wv_ref, pv_ref)):
        mixed_up = dot(w_ref[...], n, 1, 0).astype(BF16)
        out_ref[0, start : start + inner] = dot(p_ref[...], mixed_up, 1, 0).astype(BF16)
    out_ref[0, 2 * inner :] = aug_ref[0]


def key_value(n, wk, wv, place_k, place_v, aug, first, rows):
    size = aug.shape[2]
    inner = place_k.shape[0]
    width = n.shape[0]
    return pl.pallas_call(
        functools.partial(key_value_body, inner),
        grid=(rows,),
        in_specs=[
            pl.BlockSpec((width, size), lambda r: (0, first + r)),
            whole(wk.shape),
            whole(wv.shape),
            whole(place_k.shape),
            whole(place_v.shape),
            pl.BlockSpec((1, AUG, size), lambda r: (first + r, 0, 0)),
        ],
        out_specs=pl.BlockSpec((1, 2 * inner + AUG, size), lambda r: (r, 0, 0)),
        out_shape=jax.ShapeDtypeStruct((rows, 2 * inner + AUG, size), BF16),
        compiler_params=PARAMS,
        name="key_value",
        cost_estimate=cost(4 * wk.size * rows * size, 4 * wk.size + 2 * n.size),
    )(n, wk, wv, place_k, place_v, aug)


def project_body(n_ref, w_ref, p_ref, out_ref):
    mixed_up = dot(w_ref[...], n_ref[...], 1, 0).astype(BF16)
    out_ref[...] = dot(p_ref[...], mixed_up, 1, 0).astype(BF16)


def project(n, w, place, tile):
    width, here = n.shape
    inner = place.shape[0]
    return pl.pallas_call(
        project_body,
        grid=(here // tile,),
        in_specs=[pl.BlockSpec((width, tile), lambda t: (0, t)), whole(w.shape), whole(place.shape)],
        out_specs=pl.BlockSpec((inner, tile), lambda t: (0, t)),
        out_shape=jax.ShapeDtypeStruct((inner, here), BF16),
        compiler_params=PARAMS,
        name="project",
        cost_estimate=cost(1, 1),
    )(n, w, place)


def attend_body(heads, inner, q_ref, u_ref, *refs):
    *blocks, bias_ref, o_ref, lse_ref, s_ref = refs
    for h in range(heads):
        part = slice(h * HEAD, (h + 1) * HEAD)
        q = jnp.concatenate([q_ref[part], u_ref[0]], axis=0)
        top = None
        for s, k_ref in enumerate(blocks):
            k = jnp.concatenate([k_ref[0, part], k_ref[0, 2 * inner :]], axis=0)
            logits = dot(k, q, 0, 0) + bias_ref[h, s]
            s_ref[s] = logits
            peak = jnp.max(logits, axis=0, keepdims=True)
            top = peak if top is None else jnp.maximum(top, peak)
        total, out = None, None
        for s, k_ref in enumerate(blocks):
            e = jnp.exp(s_ref[s] - top)
            part_sum = jnp.sum(e, axis=0, keepdims=True)
            total = part_sum if total is None else total + part_sum
            value = k_ref[0, slice(inner + h * HEAD, inner + (h + 1) * HEAD)]
            term = dot(value, e.astype(BF16), 1, 0)
            out = term if out is None else out + term
        o_ref[part] = (out / total).astype(BF16)
        lse_ref[0, h : h + 1] = top + jnp.log(total)
    pad = lse_ref.shape[1] - heads
    if pad:
        lse_ref[0, heads:] = jnp.zeros((pad, lse_ref.shape[2]), F32)


def attend(qt, u, kv, bias, heads, first):
    rows, depth, size = kv[0].shape
    inner = heads * HEAD
    pad = -(-heads // 8) * 8
    return pl.pallas_call(
        functools.partial(attend_body, heads, inner),
        grid=(rows,),
        in_specs=[
            pl.BlockSpec((inner, size), lambda r: (0, first + r)),
            pl.BlockSpec((1, AUG, size), lambda r: (first + r, 0, 0)),
        ]
        + [pl.BlockSpec((1, depth, size), lambda r: (r, 0, 0))] * len(kv)
        + [whole(bias.shape)],
        out_specs=[
            pl.BlockSpec((inner, size), lambda r: (0, r)),
            pl.BlockSpec((1, pad, size), lambda r: (r, 0, 0)),
        ],
        out_shape=[
            jax.ShapeDtypeStruct((inner, rows * size), BF16),
            jax.ShapeDtypeStruct((rows, pad, size), F32),
        ],
        scratch_shapes=[pltpu.VMEM((len(kv), size, size), F32)],
        compiler_params=PARAMS,
        name="attend",
        cost_estimate=cost(16 * rows * heads * len(kv) * size * size * HEAD, 40_000_000),
    )(qt, u, *kv, bias)


def three(x):
    a = x.astype(BF16).astype(F32)
    rest = x - a
    b = rest.astype(BF16).astype(F32)
    return a, b, rest - b


def attend_back_body(heads, inner, count, more, q_ref, u_ref, *refs):
    blocks = refs[:count]
    bias_ref, o_ref, do_ref, lse_ref = refs[count : count + 4]
    refs = refs[count + 4 :]
    before_ref, refs = (refs[0], refs[1:]) if more else (None, refs)
    dq_ref = refs[0]
    grads = refs[1 : count + 1]
    gb_ref = refs[count + 1]
    size = bias_ref.shape[3]
    row = pl.program_id(0)
    mask_grad = [None] * count
    extra = u_ref[0].astype(F32)
    place = lax.broadcasted_iota(jnp.int32, (AUG, size), 0)

    def pick(parts, base):
        for i, value in enumerate(parts):
            base = jnp.where(place == ONES + i, value, base)
        return base.astype(BF16)

    for h in range(heads):
        part = slice(h * HEAD, (h + 1) * HEAD)
        vpart = slice(inner + h * HEAD, inner + (h + 1) * HEAD)
        q = q_ref[part]
        do = do_ref[part]
        delta = jnp.sum(do.astype(F32) * o_ref[part].astype(F32), axis=0, keepdims=True)
        q_aug = jnp.concatenate([q, pick(three(-lse_ref[0, h : h + 1]), extra)], axis=0)
        do_aug = jnp.concatenate([do, pick(three(-delta), jnp.zeros_like(extra))], axis=0)
        dq = None
        for s, k_ref in enumerate(blocks):
            k = k_ref[0, part]
            aug = k_ref[0, 2 * inner :]
            logits = dot(jnp.concatenate([k, aug], axis=0), q_aug, 0, 0) + bias_ref[h, s]
            p = jnp.exp(logits)
            dp = dot(jnp.concatenate([k_ref[0, vpart], aug], axis=0), do_aug, 0, 0)
            ds = p * dp

            @pl.when(row == 0)
            def _():
                gb_ref[h, s] = before_ref[h, s] + ds if more else ds

            @pl.when(row > 0)
            def _():
                gb_ref[h, s] += ds

            low = ds.astype(BF16)
            grads[s][0, vpart] = dot(do, p.astype(BF16), 1, 1).astype(BF16)
            both = dot(q_aug, low, 1, 1)
            grads[s][0, part] = both[:HEAD].astype(BF16)
            g = both[HEAD : HEAD + 1]
            mask_grad[s] = g if mask_grad[s] is None else mask_grad[s] + g
            term = dot(k, low, 1, 0)
            dq = term if dq is None else dq + term
        dq_ref[part] = dq.astype(BF16)
    for s in range(count):
        grads[s][0, 2 * inner :] = jnp.broadcast_to(mask_grad[s], (AUG, size)).astype(BF16)


def attend_back(qt, u, kv, bias, ot, dot_t, lse, heads, first, before):
    rows, depth, size = kv[0].shape
    inner = heads * HEAD
    count = len(kv)
    own = pl.BlockSpec((inner, size), lambda r: (0, r))
    col = pl.BlockSpec((inner, size), lambda r: (0, first + r))
    block = pl.BlockSpec((1, depth, size), lambda r: (r, 0, 0))
    out = pl.pallas_call(
        functools.partial(attend_back_body, heads, inner, count, len(before)),
        grid=(rows,),
        in_specs=[col, pl.BlockSpec((1, AUG, size), lambda r: (first + r, 0, 0))]
        + [block] * count
        + [whole(bias.shape), own, col]
        + [pl.BlockSpec((1,) + lse.shape[1:], lambda r: (r, 0, 0))]
        + [whole(b.shape) for b in before],
        out_specs=[own] + [block] * count + [whole(bias.shape)],
        out_shape=[jax.ShapeDtypeStruct((inner, rows * size), BF16)]
        + [jax.ShapeDtypeStruct((rows, depth, size), BF16)] * count
        + [jax.ShapeDtypeStruct(bias.shape, F32)],
        compiler_params=PARAMS,
        name="attend_back",
        cost_estimate=cost(40 * rows * heads * count * size * size * HEAD, 60_000_000),
    )(qt, u, *kv, bias, ot, dot_t, lse, *before)
    return out[0], out[1:-1], out[-1]


def bias_body(heads, slots_ref, buckets_ref, table_ref, bias_ref, buckets_t_ref):
    tables = [jnp.broadcast_to(table_ref[h : h + 1], (8, 128)) for h in range(heads)]
    buckets_t_ref[0] = buckets_ref[...].T
    for i in range(buckets_ref.shape[1] // 8):
        for j in range(buckets_ref.shape[0] // 128):
            at = (slice(i * 8, (i + 1) * 8), slice(j * 128, (j + 1) * 128))
            index = buckets_t_ref[(0,) + at]
            for h in range(heads):
                bias_ref[(h, 0) + at] = jnp.take_along_axis(tables[h], index, axis=1)


def bias_of(slots, buckets, table):
    heads = table.shape[0]
    size, blocks = buckets.shape[0], slots.shape[0]
    spec = pltpu.PrefetchScalarGridSpec(
        num_scalar_prefetch=1,
        grid=(blocks,),
        in_specs=[
            pl.BlockSpec((size, size), lambda s, slots: (0, slots[s])),
            pl.BlockSpec(table.shape, lambda s, slots: (0, 0)),
        ],
        out_specs=[
            pl.BlockSpec((heads, 1, size, size), lambda s, slots: (0, s, 0, 0)),
            pl.BlockSpec((1, size, size), lambda s, slots: (s, 0, 0)),
        ],
    )
    return pl.pallas_call(
        functools.partial(bias_body, heads),
        grid_spec=spec,
        out_shape=[
            jax.ShapeDtypeStruct((heads, blocks, size, size), F32),
            jax.ShapeDtypeStruct((blocks, size, size), jnp.int32),
        ],
        compiler_params=PARAMS,
        name="bias_of",
        cost_estimate=cost(1, 1),
    )(slots, buckets, table)


def sums_body(heads, count, buckets_ref, g_ref, out_ref):
    @pl.when(pl.program_id(0) == 0)
    def _():
        out_ref[...] = jnp.zeros_like(out_ref)

    total = out_ref[...]
    for i in range(buckets_ref.shape[1] // 8):
        at = slice(i * 8, (i + 1) * 8)
        index = buckets_ref[0, at]
        hot = [jnp.where(index == b, 1.0, 0.0) for b in range(count)]
        hot = jnp.concatenate(hot, axis=0).astype(BF16)
        g = jnp.concatenate([g_ref[h, 0, at] for h in range(heads)], axis=0)
        high = g.astype(BF16)
        low = (g - high.astype(F32)).astype(BF16)
        total += dot(jnp.concatenate([high, low], axis=0), hot, 1, 1)
    out_ref[...] = total


def bucket_sums(grad_bias, buckets, count):
    heads, blocks, size, _ = grad_bias.shape
    shape = (2 * heads * 8, count * 8)
    raw = pl.pallas_call(
        functools.partial(sums_body, heads, count),
        grid=(blocks,),
        in_specs=[
            pl.BlockSpec((1, size, size), lambda s: (s, 0, 0)),
            pl.BlockSpec((heads, 1, size, size), lambda s: (0, s, 0, 0)),
        ],
        out_specs=pl.BlockSpec(shape, lambda s: (0, 0)),
        out_shape=jax.ShapeDtypeStruct(shape, F32),
        compiler_params=PARAMS,
        name="bucket_sums",
        cost_estimate=cost(64 * grad_bias.size, 4 * grad_bias.size),
    )(buckets, grad_bias)
    raw = raw.reshape(2, heads, 8, count, 8)
    return jnp.sum(jnp.where(jnp.eye(8, dtype=bool)[None, None, :, None, :], raw, 0.0), (0, 2, 4)).T


def mix_body(x_ref, o_ref, w_ref, place_ref, gain_ref, mixed_ref, pair_ref, *piece_refs):
    spread = dot(place_ref[...], o_ref[...], 0, 0).astype(BF16)
    mixed = x_ref[0].astype(F32) + dot(w_ref[...], spread, 0, 0)
    mixed_ref[...] = mixed
    scale = lax.rsqrt(jnp.mean(mixed * mixed, axis=0, keepdims=True) + NORM_EPSILON)
    n = (mixed * scale * gain_ref[...]).astype(BF16)
    pair_ref[0] = n
    put_pieces(piece_refs, n)


def group_specs(shape, count, per, rank):
    def place(g):
        def index(r):
            inside = jnp.clip(r - g * per, 0, per - 1)
            return (0, inside) if rank == 2 else (inside, 0, 0)

        return index

    return [pl.BlockSpec(shape, place(g)) for g in range(count)]


def mix(x, ot, w, place, gain):
    rows, width, size = x.shape
    inner = ot.shape[0]
    here = rows * size
    piece_specs, piece_shapes = pieces_of((width, here), size)
    return pl.pallas_call(
        mix_body,
        grid=(rows,),
        in_specs=[
            pl.BlockSpec((1, width, size), lambda r: (r, 0, 0)),
            pl.BlockSpec((inner, size), lambda r: (0, r)),
            whole(w.shape),
            whole(place.shape),
            whole(gain.shape),
        ],
        out_specs=[
            pl.BlockSpec((width, size), lambda r: (0, r)),
            pl.BlockSpec((1, width, size), lambda r: (0, 0, r)),
        ]
        + piece_specs,
        out_shape=[
            jax.ShapeDtypeStruct((width, here), F32),
            jax.ShapeDtypeStruct((2, width, here), BF16),
        ]
        + piece_shapes,
        compiler_params=PARAMS,
        name="mix",
        cost_estimate=cost(1, 1),
    )(x, ot, w, place, gain)


def units_of(ws):
    return sum(w.shape[0] * w.shape[2] for w in ws)


def entries_of(ws):
    return sum(w.shape[0] for w in ws)


def loads_of(refs, buf, sems, kinds):
    copies, start = [], 0
    for a, ref in enumerate(refs):
        for k, kind in enumerate(kinds):
            inside = buf.at[k, pl.ds(start, ref.shape[0])]
            copies.append(pltpu.make_async_copy(ref.at[:, kind], inside, sems.at[a, k]))
        start += ref.shape[0]
    return copies


def ffn_body(count, masks, me_ref, *refs):
    ws, (n_ref, dy_ref, act_ref), refs = refs[:count], refs[count : count + 3], refs[count + 3 :]
    gs, (buf, acc, in_sems, out_sems) = refs[:-4], refs[-4:]
    t = pl.program_id(0)
    entries, rows, width = buf.shape[1:]
    size = entries * rows
    loads = loads_of(ws, buf, in_sems, range(3))

    @pl.when(t == 0)
    def _():
        for copy in loads:
            copy.start()
        acc[...] = jnp.zeros_like(acc)
        for copy in loads:
            copy.wait()

    norm = n_ref[0]
    dy = dy_ref[0]
    gate = dot(buf[0].reshape(size, width), norm, 1, 0)
    up = dot(buf[1].reshape(size, width), norm, 1, 0)
    dhid = dot(buf[2].reshape(size, width), dy, 1, 0)
    inside = gate * (0.7978845608028654 + 0.035677408136300125 * (gate * gate))
    half = 0.5 + 0.5 * jnp.tanh(inside)
    gelu = gate * half
    slope = half * (1.0 + (1.0 - half) * (6.0 * inside - 3.1915382432114616 * gate))
    dgate = (dhid * up * slope).astype(BF16)
    dup = (dhid * gelu).astype(BF16)
    hidden = (gelu * up).astype(BF16)
    act_ref[0] = dgate
    act_ref[1] = dup
    act_ref[2] = hidden
    acc[0] += dot(dgate, norm, 1, 1)
    acc[1] += dot(dup, norm, 1, 1)
    acc[2] += dot(hidden, dy, 1, 1)

    @pl.when(t == pl.num_programs(0) - 1)
    def _():
        for k in range(3):
            buf[k] = acc[k].astype(BF16).reshape(entries, rows, width)
        stores = []
        if masks is None:
            start = 0
            for g, out in enumerate(gs):
                for k in range(3):
                    inside = buf.at[k, pl.ds(start, out.shape[0])]
                    stores.append(pltpu.make_async_copy(inside, out.at[:, k], out_sems.at[g, k]))
                start += out.shape[0]
        else:
            part = len(masks) // 2
            for s, mask in enumerate(masks):
                for k in range(3):
                    inside, out = buf.at[k, me_ref[0] ^ mask], gs[s // part].at[s % part, k]
                    stores.append(pltpu.make_async_copy(inside, out, out_sems.at[s, k]))
        for copy in stores:
            copy.start()
        for copy in stores:
            copy.wait()


def ffn_group(me, ws, n, dy, tile, masks=None):
    halves, width, tokens = n.shape
    per = tokens // tile
    all_tokens = halves * tokens
    size = units_of(ws)
    inner = (entries_of(ws),) + ws[0].shape[2:]
    column = pl.BlockSpec((1, width, tile), lambda t, me: (t // per, 0, t % per))
    stores = len(ws) if masks is None else len(masks)
    shapes = [w.shape for w in ws]
    if masks is not None:
        shapes = [(inner[0] // 2, 3) + inner[1:]] * 2
    spec = pltpu.PrefetchScalarGridSpec(
        num_scalar_prefetch=1,
        grid=(halves * per,),
        in_specs=[ANY] * len(ws) + [column, column],
        out_specs=[pl.BlockSpec((3, size, tile), lambda t, me: (0, 0, t))] + [ANY] * len(shapes),
        scratch_shapes=[
            pltpu.VMEM((3,) + inner, BF16),
            pltpu.VMEM((3, size, width), F32),
            pltpu.SemaphoreType.DMA((len(ws), 3)),
            pltpu.SemaphoreType.DMA((stores, 3)),
        ],
    )
    out = pl.pallas_call(
        functools.partial(ffn_body, len(ws), masks),
        grid_spec=spec,
        out_shape=[jax.ShapeDtypeStruct((3, size, all_tokens), BF16)]
        + [jax.ShapeDtypeStruct(shape, BF16) for shape in shapes],
        compiler_params=PARAMS,
        name="ffn_group",
        cost_estimate=cost(1, 1),
    )(me, *ws, n, dy)
    return out[0], out[1:]


def ffn_terms(layout, kinds, refs):
    count, total = len(layout), sum(layout)
    ws, acts, refs = refs[:total], refs[total : total + count], refs[total + count :]
    bufs, sems = refs[:count], refs[count]

    @pl.when(pl.program_id(0) == 0)
    def _():
        copies, start = [], 0
        for p, arrays in enumerate(layout):
            copies += loads_of(ws[start : start + arrays], bufs[p], sems.at[p], kinds)
            start += arrays
        for copy in copies:
            copy.start()
        for copy in copies:
            copy.wait()

    out = None
    for act, buf in zip(acts, bufs):
        _, entries, rows, width = buf.shape
        for k in range(len(kinds)):
            term = dot(buf[k].reshape(entries * rows, width), act[k], 0, 0)
            out = term if out is None else out + term
    return out


def layout_of(groups):
    return tuple(len(ws) for ws in groups)


def flat_of(groups):
    return [w for ws in groups for w in ws]


def ffn_specs(groups, acts, kinds, tile, first):
    at = kinds[0] // len(kinds)
    return [ANY] * len(flat_of(groups)) + [
        pl.BlockSpec((len(kinds), a.shape[1], tile), lambda t: (at, 0, first + t)) for a in acts
    ]


def ffn_scratch(groups, kinds):
    return [
        pltpu.VMEM((len(kinds), entries_of(ws)) + ws[0].shape[2:], BF16) for ws in groups
    ] + [pltpu.SemaphoreType.DMA((len(groups), max(layout_of(groups)), len(kinds)))]


def ffn_back_body(layout, kinds, pieces, *refs):
    ins = sum(layout) + len(layout)
    total = ffn_terms(layout, kinds, refs[:ins] + refs[ins + pieces :])
    put_pieces(refs[ins : ins + pieces], total.astype(BF16))


def ffn_back(groups, acts, kinds, start, count, tile, pieces):
    width = groups[0][0].shape[3]
    piece_specs, piece_shapes = pieces_of((width, count), tile, pieces)
    return pl.pallas_call(
        functools.partial(ffn_back_body, layout_of(groups), kinds, pieces),
        grid=(count // tile,),
        in_specs=ffn_specs(groups, acts, kinds, tile, start // tile),
        out_specs=piece_specs,
        out_shape=piece_shapes,
        scratch_shapes=ffn_scratch(groups, kinds),
        compiler_params=PARAMS,
        name="ffn_back",
        cost_estimate=cost(1, 1),
    )(*flat_of(groups), *acts)


def layer_out_body(layout, *refs):
    ins = sum(layout) + len(layout)
    mixed_ref, got_ref, out_ref = refs[ins : ins + 3]
    total = ffn_terms(layout, [2], refs[:ins] + refs[ins + 3 :])
    out_ref[0] = (mixed_ref[...] + total + got_ref[...].astype(F32)).astype(BF16)


def layer_out_of(groups, acts, mixed, got, rows):
    width, here = mixed.shape
    size = here // rows
    col = pl.BlockSpec((width, size), lambda t: (0, t))
    return pl.pallas_call(
        functools.partial(layer_out_body, layout_of(groups)),
        grid=(rows,),
        in_specs=ffn_specs(groups, acts, [2], size, 0) + [col, col],
        out_specs=pl.BlockSpec((1, width, size), lambda t: (t, 0, 0)),
        out_shape=jax.ShapeDtypeStruct((rows, width, size), BF16),
        scratch_shapes=ffn_scratch(groups, [2]),
        compiler_params=PARAMS,
        name="layer_out_of",
        cost_estimate=cost(1, 1),
    )(*flat_of(groups), *acts, mixed, got)


def mix_back_body(layout, *refs):
    ins = sum(layout) + len(layout)
    weights, refs = refs[:ins], refs[ins:]
    pieces, refs = refs[:PIECES], refs[PIECES:]
    mixed_ref, dy_ref, o_ref, w_ref, place_ref, home_ref, gain_ref = refs[:7]
    refs = refs[7:]
    inside_grad = len(refs) == 5 + len(layout) + 1
    dmixed_ref, do_ref, gg_ref = refs[:3]
    gw_ref, acc = refs[3:5] if inside_grad else (None, None)
    row = pl.program_id(0)
    got = jnp.concatenate([r[...] for r in pieces], axis=0)
    dn = ffn_terms(layout, [0, 1], weights + refs[-len(layout) - 1 :]) + got.astype(F32)
    mixed = mixed_ref[...]
    scale = lax.rsqrt(jnp.mean(mixed * mixed, axis=0, keepdims=True) + NORM_EPSILON)
    unit = mixed * scale
    scaled = dn * gain_ref[...]
    inside = jnp.mean(scaled * unit, axis=0, keepdims=True)
    dmixed = dy_ref[0].astype(F32) + scale * (scaled - unit * inside)
    dmixed_ref[...] = dmixed
    low = dmixed.astype(BF16)
    spread = dot(home_ref[...], o_ref[...], 0, 0).astype(BF16)
    mixed_up = dot(w_ref[...], low, 1, 0).astype(BF16)
    do_ref[...] = dot(place_ref[...], mixed_up, 1, 0).astype(BF16)
    both = dn * unit
    gain_part = both[:, :128]
    for j in range(1, both.shape[1] // 128):
        gain_part = gain_part + both[:, j * 128 : (j + 1) * 128]

    @pl.when(row == 0)
    def _():
        gg_ref[...] = gain_part

    @pl.when(row > 0)
    def _():
        gg_ref[...] += gain_part

    if inside_grad:
        product = dot(spread, low, 1, 1)

        @pl.when(row == 0)
        def _():
            acc[...] = product

        @pl.when(row > 0)
        def _():
            acc[...] += product

        @pl.when(row == pl.num_programs(0) - 1)
        def _():
            gw_ref[...] = acc[...].astype(BF16)


def mix_back(groups, acts, mixed, d1, dy, ot, w, place, home, gain):
    rows, width, size = dy.shape
    inner = ot.shape[0]
    here = rows * size
    col = pl.BlockSpec((width, size), lambda r: (0, r))
    head_col = pl.BlockSpec((inner, size), lambda r: (0, r))
    fits = w.shape[0] <= 1024
    out = pl.pallas_call(
        functools.partial(mix_back_body, layout_of(groups)),
        grid=(rows,),
        in_specs=ffn_specs(groups, acts, [0, 1], size, 0)
        + pieces_of(mixed.shape, size)[0]
        + [col, pl.BlockSpec((1, width, size), lambda r: (r, 0, 0)), head_col]
        + [whole(w.shape), whole(place.shape), whole(home.shape), whole(gain.shape)],
        out_specs=[col, head_col, whole((width, 128))] + [whole(w.shape)] * fits,
        out_shape=[
            jax.ShapeDtypeStruct((width, here), F32),
            jax.ShapeDtypeStruct((inner, here), BF16),
            jax.ShapeDtypeStruct((width, 128), F32),
        ]
        + [jax.ShapeDtypeStruct(w.shape, BF16)] * fits,
        scratch_shapes=[pltpu.VMEM(w.shape, F32)] * fits + ffn_scratch(groups, [0, 1]),
        compiler_params=PARAMS,
        name="mix_back",
        cost_estimate=cost(1, 1),
    )(*flat_of(groups), *acts, *d1, mixed, dy, ot, w, place, home, gain)
    if not fits:
        spread = dot(home, ot, 0, 0).astype(BF16)
        out = [*out, dot(spread, out[0].astype(BF16), 1, 1).astype(BF16)]
    return out


def grads_body(per, groups, parts, n_ref, *refs):
    d_refs, refs = refs[:groups], refs[groups:]
    places, refs = refs[: len(parts)], refs[len(parts) :]
    outs, (acc, d_scr) = refs[: 2 * len(parts)], refs[2 * len(parts) :]
    row = pl.program_id(0)
    n = n_ref[...]
    for g, d_ref in enumerate(d_refs):

        @pl.when(row // per == g)
        def _():
            d_scr[...] = d_ref[...].reshape(d_scr.shape)

    products = []
    for (start, stop), p_ref in zip(parts, places):
        spread = dot(p_ref[...], d_scr[start:stop], 0, 0).astype(BF16)
        products.append(dot(spread, n, 1, 1))

    @pl.when(row == 0)
    def _():
        for j, product in enumerate(products):
            acc[j] = product

    @pl.when(row > 0)
    def _():
        for j, product in enumerate(products):
            acc[j] += product

    @pl.when(row == pl.num_programs(0) - 1)
    def _():
        half = acc.shape[1] // 2
        for j in range(len(parts)):
            outs[2 * j][...] = acc[j, :half].astype(BF16)
            outs[2 * j + 1][...] = acc[j, half:].astype(BF16)


def projection_grads(n, groups, parts, places, rows):
    if len(parts) > 1 and places[0].shape[1] > 1024:
        return [
            half
            for part, p in zip(parts, places)
            for half in projection_grads(n, groups, [part], [p], rows)
        ]
    width, here = n.shape
    size = here // rows
    per = rows // len(groups)
    rank = groups[0].ndim
    depth = groups[0].shape[-2]
    shape = (depth, size) if rank == 2 else (1, depth, size)
    wide = (places[0].shape[1], width)
    return pl.pallas_call(
        functools.partial(grads_body, per, len(groups), parts),
        grid=(rows,),
        in_specs=[pl.BlockSpec((width, size), lambda r: (0, r))]
        + group_specs(shape, len(groups), per, rank)
        + [whole(p.shape) for p in places],
        out_specs=[whole((wide[0] // 2, width))] * (2 * len(parts)),
        out_shape=[jax.ShapeDtypeStruct((wide[0] // 2, width), BF16)] * (2 * len(parts)),
        scratch_shapes=[pltpu.VMEM((len(parts),) + wide, F32), pltpu.VMEM((depth, size), BF16)],
        compiler_params=PARAMS,
        name="projection_grads",
        cost_estimate=cost(
            2 * len(parts) * wide[0] * width * here, 2 * n.size + 2 * len(parts) * wide[0] * width
        ),
    )(n, *groups, *places)


def last_body(per, groups, x_ref, dm_ref, *refs):
    dq_refs, dkv_refs, refs = refs[:groups], refs[groups : 2 * groups], refs[2 * groups :]
    ws, places, refs = refs[:3], refs[3:6], refs[6:]
    gain_ref, gx_ref, gg_ref, d_scr = refs
    row = pl.program_id(0)
    inner = dq_refs[0].shape[0]
    for g in range(groups):

        @pl.when(row // per == g)
        def _():
            d_scr[:inner] = dq_refs[g][...]
            d_scr[inner:] = dkv_refs[g][0, : 2 * inner]

    dn = None
    for j in range(3):
        spread = dot(places[j][...], d_scr[j * inner : (j + 1) * inner], 0, 0).astype(BF16)
        term = dot(ws[j][...], spread, 0, 0)
        dn = term if dn is None else dn + term
    x = x_ref[0].astype(F32)
    scale = lax.rsqrt(jnp.mean(x * x, axis=0, keepdims=True) + NORM_EPSILON)
    unit = x * scale
    scaled = dn * gain_ref[...]
    inside = jnp.mean(scaled * unit, axis=0, keepdims=True)
    gx_ref[0] = dm_ref[...] + scale * (scaled - unit * inside)
    both = dn * unit
    gain_part = both[:, :128]
    for j in range(1, both.shape[1] // 128):
        gain_part = gain_part + both[:, j * 128 : (j + 1) * 128]

    @pl.when(row == 0)
    def _():
        gg_ref[...] = gain_part

    @pl.when(row > 0)
    def _():
        gg_ref[...] += gain_part


def last(x, dmixed, dqs, dkvs, ws, places, gain):
    rows, width, size = x.shape
    inner = dqs[0].shape[0]
    per = rows // len(dqs)
    col = pl.BlockSpec((width, size), lambda r: (0, r))
    block = pl.BlockSpec((1, width, size), lambda r: (r, 0, 0))
    return pl.pallas_call(
        functools.partial(last_body, per, len(dqs)),
        grid=(rows,),
        in_specs=[block, col]
        + group_specs((inner, size), len(dqs), per, 2)
        + group_specs((1,) + dkvs[0].shape[1:], len(dkvs), per, 3)
        + [whole(w.shape) for w in ws]
        + [whole(p.shape) for p in places]
        + [whole(gain.shape)],
        out_specs=[block, whole((width, 128))],
        out_shape=[jax.ShapeDtypeStruct(x.shape, F32), jax.ShapeDtypeStruct((width, 128), F32)],
        scratch_shapes=[pltpu.VMEM((3 * inner, size), BF16)],
        compiler_params=PARAMS,
        name="last",
        cost_estimate=cost(6 * ws[0].size * rows * size, 14 * x.size + 6 * ws[0].size),
    )(x, dmixed, *dqs, *dkvs, *ws, *places, gain)


def after(value, *markers):
    return lax.optimization_barrier((value, markers))[0]


def pad_rows(w, rows):
    return jnp.pad(w, ((0, rows - w.shape[0]), (0, 0))) if rows > w.shape[0] else w


class Links:
    def __init__(self, dp, pairs):
        self.sizes = {"dp": dp, "x": pairs, "core": 2}
        self.strides = {"dp": 2 * pairs, "x": 2, "core": 1}
        self.core = ("core", 1)
        self.across = ("x", 1)
        self.near = ("dp", 1)
        self.far_count = dp // 2

    def swap(self, x, step):
        axis, mask = step
        return lax.ppermute(x, axis, [(i, i ^ mask) for i in range(self.sizes[axis])])

    def far_steps(self):
        return [("dp", k << 1) for k in range(1, self.far_count)]

    def far_bits(self):
        return [("dp", 2 << b) for b in range(self.far_count.bit_length() - 1)]

    def masks(self, steps):
        found = [(k << 1) * self.strides["dp"] for k in range(self.far_count)]
        for axis, mask in steps:
            found = found + [f ^ (mask * self.strides[axis]) for f in found]
        return found


def per_device(
    dp, ctx,
    tokens, soft_mask, segment_ids, buckets, gain_attn, gain_ffn, bias_table,
    w_query, w_key, w_value, w_attn_out, w_gate, w_up, w_ffn_out, cotangent,
):
    links = Links(dp, ctx // 2)
    swap, core, across, near = links.swap, links.core, links.across, links.near
    far = links.far_steps()
    rows, size, width = tokens.shape
    here = rows * size
    count, heads = bias_table.shape
    inner = heads * HEAD
    my_dp, my_ctx = lax.axis_index("dp"), lax.axis_index("x") * 2 + lax.axis_index("core")
    me = my_dp * ctx + my_ctx
    tile = min(512, here)
    order_a, order_b = [near, across], [across, near]

    def spread_of(steps):
        real = w_query.shape[0]
        owners = me ^ jnp.asarray(links.masks(steps), dtype=jnp.int32)
        inside = jnp.arange(each)
        feature = owners[:, None] * real + inside[None, :]
        feature = jnp.where(inside[None, :] < real, feature, -1).reshape(-1)
        return (jnp.arange(inner)[:, None] == feature[None, :]).astype(BF16)

    token = []

    def run(work, *args):
        if token:
            args = lax.optimization_barrier((args, tuple(token)))[0]
        out = work(*args)
        token[:] = jax.tree.leaves(out)
        return out

    each = -(-w_query.shape[0] // ROW_TILE) * ROW_TILE
    slot = lambda w: pad_rows(w, each)[None]
    flat = lambda w: w.reshape(-1, width)
    far_bits = links.far_bits()
    ab, ba = (near, across), (across, near)

    def exchange(arrays, steps):
        return [(a, swap(a, step)) for a, step in zip(arrays, steps)]

    def swap_core(value):
        return [swap(v, core) for v in value]

    def close(value):
        return run(lambda v: v, value)

    class Gather:
        def __init__(self, array, cuts, direct=False, mark=None, paths=(ab, ba)):
            if mark is not None:
                array = after(array, mark)
            self.cuts, self.stage, self.paths = cuts, 0, paths
            self.hops = 1 if direct else len(far_bits)
            steps = far if direct else far_bits[:1]
            self.held = [array] + [swap(array, step) for step in steps]

        def go(self):
            self.stage += 1
            if self.stage < self.hops:
                (array,) = run(lambda *p: join([p]), *self.held)
                self.held = [array, swap(array, far_bits[self.stage])]
            elif self.stage == self.hops:
                parts = run(lambda *p: cut_join(list(p), self.cuts), *self.held)
                self.held = exchange(parts, self.paths[0])
            elif self.stage == self.hops + 1:
                self.held = exchange(run(join, self.held), self.paths[1])

        def start_of(self):
            first = self.held[0]
            return first[0] if isinstance(first, tuple) else first

        def core_go(self):
            self.held = exchange(run(join, self.held), (core, core))

        def core_end(self):
            return run(join, self.held)

    units = -(-w_gate.shape[0] // ROW_TILE)
    padded = [pad_rows(w, units * ROW_TILE) for w in (w_gate, w_up, w_ffn_out)]
    marks = [0, 3, 5, 7] if units == 7 else list(range(units + 1))
    shards = [
        jnp.stack([w[low * ROW_TILE : high * ROW_TILE] for w in padded])
        for low, high in zip(marks, marks[1:])
    ]
    attn_w = Gather(
        jnp.concatenate([slot(w) for w in (w_key, w_attn_out, w_value, w_query)], axis=1)[:, None],
        [(0, 2 * each), (2 * each, 2 * each)],
        direct=True,
    )
    same_core = ("dp", "x")
    by_hops = units == 7
    last_group = len(shards) - 1

    x = jnp.transpose(tokens, (0, 2, 1))
    dy = jnp.transpose(cotangent, (0, 2, 1))
    gain_one, gain_two = gain_attn[:, None], gain_ffn[:, None]
    place_a, place_b = spread_of(order_a + [core]), spread_of(order_b + [core])
    real = w_query.shape[0]
    home_row = jnp.arange(inner) // real * each + jnp.arange(inner) % real
    home = (home_row[:, None] == jnp.arange(inner // real * each)[None, :]).astype(BF16)
    segs = lax.dynamic_slice_in_dim(segment_ids, my_ctx * size, size, 1)
    same = segs[:, None, :] == jnp.arange(DOCS, dtype=segs.dtype)[None, :, None]
    ones = jnp.ones((rows, 1, size), BF16)
    rest = AUG - 1 - DOCS
    aug = jnp.concatenate(
        [soft_mask[:, None, :], same.astype(BF16)] + [ones] * 3
        + [jnp.zeros((rows, rest - 3, size), BF16)],
        axis=1,
    )
    query_aug = jnp.concatenate(
        [ones, jnp.where(same, 0.0, MASK_VALUE).astype(BF16), jnp.zeros((rows, rest, size), BF16)],
        axis=1,
    )
    normed, dy_pair, *dy_own = run(first_norm, x, dy, gain_one)

    attn_w.go()
    ffn_w = [
        [lax.all_gather(after(shard, attn_w.start_of()), same_core)]
        for shard in (shards[:-1] if by_hops else shards)
    ]
    slots = jnp.array([0, 2, 1, 3], jnp.int32) ^ my_ctx
    bias, buckets_t = run(
        bias_of, slots, buckets, jnp.pad(bias_table.T, ((0, 0), (0, 128 - count)))
    )
    dy_parts = swap_core(dy_own)
    attn_w.go()
    dy_pair = run(fill, dy_pair, dy_parts)
    if by_hops:
        last_w = Gather(
            shards[-1][None], [(0, shards[-1].shape[1])], mark=dy_pair, paths=((across,), (near,))
        )
    attn_w.core_go()
    wko, wvq = attn_w.core_end()
    pick = lambda w, k: w[:, 0, k * each : (k + 1) * each].reshape(-1, width)
    if by_hops:
        last_w.go()
    wk, wo, wv, wq = run(lambda a, b: [pick(a, 0), pick(a, 1), pick(b, 0), pick(b, 1)], wko, wvq)
    kv_own = run(lambda *a: key_value(*a, 0, rows), normed, wk, wv, place_a, place_b, aug)
    kv_across = swap(kv_own, across)
    kv_core = swap(kv_own, core)
    queries = run(lambda n, w, p: project(n, w, p, tile), normed, wq, place_b)
    kv_core = close(kv_core)

    kv = run(lambda *k: list(k), kv_own, kv_across, kv_core)
    kv.append(close(jnp.concatenate([swap(k, core) for k in jnp.split(kv[1], rows)])))
    if by_hops:
        last_w.go()
    attended, lse = run(lambda *a: attend(*a, heads, 0), queries, query_aug, kv, bias)
    mixed, n_pair, *normed_two = run(mix, x, attended, wo, place_a, gain_two)
    n_parts = close(swap_core(normed_two))
    if by_hops:
        last_w.go()
    n_pair = run(fill, n_pair, n_parts)

    class Sums:
        def __init__(self, grads, paths, direct=False):
            self.paths, self.direct = paths[: len(grads)], direct
            self.stage = 0
            self.send(grads)

        def send(self, halves):
            self.keep = [h[0] for h in halves]
            self.got = [swap(h[1], p[self.stage]) for h, p in zip(halves, self.paths)]

        def go(self):
            near_hops = len(self.paths[0])
            hops = near_hops + (1 if self.direct else len(far_bits))
            self.stage += 1
            if self.stage > hops:
                return
            if self.stage < near_hops:
                self.send(run(add_halves, self.keep, self.got))
                return
            if self.stage == near_hops:
                rows_of = [k.shape[-2] for k in self.keep]
                self.edges = [sum(rows_of[:k]) for k in range(len(rows_of) + 1)]
                if self.direct:
                    piles = run(lambda k, r: add_piles(k, r, self.edges), self.keep, self.got)
                    self.keep = [piles[0]]
                    self.got = [swap(pile, step) for pile, step in zip(piles[1:], far)]
                    return
                halves = run(lambda k, r: add_merge(k, r, self.edges), self.keep, self.got)
            elif self.stage < hops:
                halves = run(add_halves, self.keep, self.got)[0]
            else:
                self.out = run(lambda k, r: add_last(k[0], r, self.edges), self.keep, self.got)
                return
            self.keep = [halves[0]]
            self.got = [swap(halves[1], far_bits[hops - 1 - self.stage])]

    acts, sums = [], []
    me_same = (my_dp * (ctx // 2) + lax.axis_index("x")).reshape(1)
    masks = [[m >> 1 for m in links.masks(steps)] for steps in (ab, ba)]
    ffn_grads = []
    if by_hops:
        ffn_w.append(None)
    for i, ws in enumerate(ffn_w):
        if i == last_group and by_hops:
            ws = ffn_w[i] = close(list(last_w.held[0]))
        some = tile if units_of(ws) <= 768 else tile // 2
        mask = masks[0] if by_hops and i == last_group - 1 else None
        act, grads = run(
            lambda m, w, n, d: ffn_group(m, w, n, d, some, mask), me_same, ws, n_pair, dy_pair
        )
        acts.append(act)
        if by_hops and i >= last_group - 1:
            ffn_grads.append(grads)
        else:
            ffn_grads.append(lax.psum_scatter(grads[0], same_core))
    if by_hops:
        sums = [Sums(ffn_grads[-2:], [ba, ab])]

    def tick():
        for s in sums:
            s.go()

    back = run(lambda p, a: ffn_back(p, a, [0, 1], here, here, tile, PIECES), ffn_w, acts)
    dn_got = swap_core(back)
    (out_other,) = run(lambda p, a: ffn_back(p, a, [2], here, here, tile, 1), ffn_w, acts)
    dn_got = close(dn_got)
    out_got = swap(out_other, core)

    dmixed, dattended, gain_two_part, gwo = run(
        mix_back, ffn_w, acts, mixed, dn_got, dy, attended, wo, place_a, home, gain_two
    )
    everywhere = ("dp", "x", "core")
    scatter = lambda g: lax.psum_scatter(g.reshape(-1, each, width), everywhere, tiled=False)
    grad_attn_out = scatter(gwo)
    tick()
    dq, dkv, grad_bias = run(
        lambda *a: attend_back(*a, heads, 0, []),
        queries, query_aug, kv, bias, attended, dattended, lse,
    )
    by_core = [(dkv[0], swap(dkv[2], core)), (dkv[1], swap(dkv[3], core))]
    tick()
    if by_hops:
        ffn_grads[0] = close(ffn_grads[0])
    gwq = run(
        lambda n, d, p: projection_grads(n, [d], [(0, inner)], [p], rows), normed, dq, home
    )
    grad_query = scatter(jnp.concatenate(gwq))
    own, other = run(add_pairs, by_core)
    other = swap(other, across)
    grad_table = run(lambda g, b: bucket_sums(g, b, count), grad_bias, buckets_t)
    out = run(lambda *a: layer_out_of(*a, rows), ffn_w, acts, mixed, out_got)
    tick()
    grad_attn_out = close(grad_attn_out)
    (dkv,) = run(add_pairs, [(own, other)])
    gkv = run(
        lambda n, d, pa, pb: projection_grads(n, [d], [(0, inner), (inner, 2 * inner)], [pa, pb], rows),
        normed, dkv, place_a, place_b,
    )
    entries = lambda g: tuple(v.reshape(-1, each, width) for v in g)
    home_a, home_b = (core,) + ba, (core,) + ab
    value_sum = Sums([entries(gkv[:2]), entries(gkv[2:])], [home_a, home_b], direct=dp <= 8)
    value_sum.go()
    gx, gain_one_part = run(
        lambda *a: last(a[0], a[1], [a[2]], [a[3]], a[4:7], a[7:10], a[10]),
        x, dmixed, dq, dkv, wq, wk, wv, place_b, place_a, place_b, gain_one,
    )
    value_sum.go()
    tick()
    small = jnp.concatenate(
        [jnp.sum(gain_one_part, 1), jnp.sum(gain_two_part, 1), grad_table.reshape(-1)]
    )
    length = small.shape[0]
    small = jnp.pad(small, (0, -length % 1024)).reshape(-1, 128)
    bits = [core, across] + [("dp", 1 << b) for b in range(dp.bit_length() - 1)]
    for k, one in enumerate(bits):
        got = swap(small, one)
        if k in (1, 3):
            value_sum.go()
        small = run(lambda a, b: a + b, small, got)
    for _ in range(len(far_bits) + 4):
        for s in [value_sum] + sums:
            s.go()
    small = small.reshape(-1)
    if by_hops:
        ffn_grads[-2:] = sums[0].out
    grad_gate, grad_up, grad_ffn_out = (
        jnp.concatenate([g[j].astype(F32) for g in ffn_grads])[: w_gate.shape[0]] for j in range(3)
    )
    return (
        jnp.transpose(out, (0, 2, 1)),
        jnp.transpose(gx, (0, 2, 1)),
        dkv[:, 2 * inner].astype(F32),
        small[:width],
        small[width : 2 * width],
        small[2 * width : length].reshape(count, heads),
        grad_query[:real].astype(F32),
        value_sum.out[0][:real],
        value_sum.out[1][:real],
        grad_attn_out[:real].astype(F32),
        grad_gate,
        grad_up,
        grad_ffn_out,
    )


def solution(mesh):
    dp, ctx = mesh.shape["dp"], mesh.shape["ctx"]
    by_core = Mesh(mesh.devices.reshape(dp, ctx // 2, 2), ("dp", "x", "core"))
    ctx_axes = ("x", "core")
    split = P(("dp", "x", "core"), None)
    act = P("dp", ctx_axes, None)
    in_specs = (
        (act, P("dp", ctx_axes), P("dp", None), P(ctx_axes, None), P(), P(), P()) + (split,) * 7 + (act,)
    )
    out_specs = (act, act, P("dp", ctx_axes), P(), P(), P()) + (split,) * 7
    return jax.shard_map(
        functools.partial(per_device, dp, ctx),
        mesh=by_core,
        in_specs=in_specs,
        out_specs=out_specs,
        check_vma=False,
    )
```

```python
import functools

import jax
import jax.numpy as jnp
import numpy as np
from jax import lax
from jax.experimental import pallas as pl
from jax.experimental.pallas import tpu as pltpu
from jax.sharding import Mesh, PartitionSpec as P

NORM_EPSILON = 1e-06
MASK_VALUE = -1e30
F32, BF16 = jnp.float32, jnp.bfloat16
HEAD = 64
ROW_TILE = 16
AUG = 16
DOCS = 5
ONES = 1 + DOCS
VMEM_LIMIT = 58 * 1024 * 1024
PARAMS = pltpu.CompilerParams(vmem_limit_bytes=VMEM_LIMIT)


def dot(a, b, ca, cb):
    return lax.dot_general(a, b, (((ca,), (cb,)), ((), ())), preferred_element_type=F32)


def whole(shape):
    return pl.BlockSpec(shape, lambda t: (0,) * len(shape), pipeline_mode=pl.Buffered(1))


def cost(flops, nbytes):
    return pl.CostEstimate(flops=1, bytes_accessed=1, transcendentals=0)


ANY = pl.BlockSpec(memory_space=pl.ANY)


def join(pairs):
    return [jnp.concatenate(list(pair), axis=0) for pair in pairs]


def cut_join(parts, cuts):
    out = []
    for cut in cuts:
        at = np.s_[:, :, cut[0] : cut[0] + cut[1]] if isinstance(cut, tuple) else np.s_[:, cut]
        out.append(jnp.concatenate([p[at] for p in parts], axis=0))
    return out


def fill(pair, parts):
    start = 0
    for part in parts:
        pair = pair.at[1, start : start + part.shape[0]].set(part)
        start += part.shape[0]
    return pair


def add_halves(keep, got):
    out = []
    for k, r in zip(keep, got):
        part = k.shape[0] // 2
        out.append((k[:part] + r[:part], k[part:] + r[part:]))
    return out


def add_merge(keep, got, edges):
    part = keep[0].shape[0] // 2
    ends = [slice(None, part), slice(part, None)]
    return [jnp.concatenate([k[e] + r[e] for k, r in zip(keep, got)], axis=-2) for e in ends]


def add_piles(keep, got, edges):
    return [
        jnp.concatenate([k[i : i + 1] + r[i : i + 1] for k, r in zip(keep, got)], axis=-2)
        for i in range(keep[0].shape[0])
    ]


def add_last(keep, got, edges):
    total = keep[0].astype(F32)
    for r in got:
        total = total + r[0].astype(F32)
    return [total[..., a:b, :] for a, b in zip(edges, edges[1:])]


def add_pairs(pairs):
    return [a + b for a, b in pairs]


PIECES = 4


def pieces_of(shape, tile, pieces=PIECES):
    rows, columns = shape
    piece = (rows // pieces, columns)
    specs = [pl.BlockSpec((piece[0], tile), lambda t: (0, t)) for _ in range(pieces)]
    return specs, [jax.ShapeDtypeStruct(piece, BF16)] * pieces


def put_pieces(refs, value):
    step = refs[0].shape[0]
    for k, ref in enumerate(refs):
        ref[...] = value[k * step : (k + 1) * step]


def norm_body(x_ref, dy_ref, gain_ref, n_ref, pair_ref, *piece_refs):
    x = x_ref[0].astype(F32)
    scale = lax.rsqrt(jnp.mean(x * x, axis=0, keepdims=True) + NORM_EPSILON)
    n_ref[...] = (x * scale * gain_ref[...]).astype(BF16)
    pair_ref[0] = dy_ref[0]
    put_pieces(piece_refs, dy_ref[0])


def first_norm(x, dy, gain):
    rows, width, size = x.shape
    block = pl.BlockSpec((1, width, size), lambda r: (r, 0, 0))
    col = pl.BlockSpec((width, size), lambda r: (0, r))
    here = rows * size
    piece_specs, piece_shapes = pieces_of((width, here), size)
    return pl.pallas_call(
        norm_body,
        grid=(rows,),
        in_specs=[block, block, whole(gain.shape)],
        out_specs=[col, pl.BlockSpec((1, width, size), lambda r: (0, 0, r))] + piece_specs,
        out_shape=[
            jax.ShapeDtypeStruct((width, here), BF16),
            jax.ShapeDtypeStruct((2, width, here), BF16),
        ]
        + piece_shapes,
        compiler_params=PARAMS,
        name="first_norm",
        cost_estimate=cost(4 * x.size, 10 * x.size),
    )(x, dy, gain)


def picked(w, index):
    entries, _, _, width = w.shape
    each = w.shape[2] // 2
    return pl.BlockSpec(
        (entries, 1, each, width), lambda t: (0, 0, index, 0), pipeline_mode=pl.Buffered(1)
    )


def flat_rows(w_ref):
    entries, _, each, width = w_ref.shape
    return w_ref[...].reshape(entries * each, width)


def key_value_body(inner, n_ref, wk_ref, wv_ref, pk_ref, pv_ref, aug_ref, out_ref):
    n = n_ref[...]
    for start, w_ref, p_ref in ((0, wk_ref, pk_ref), (inner, wv_ref, pv_ref)):
        mixed_up = dot(flat_rows(w_ref), n, 1, 0).astype(BF16)
        out_ref[0, start : start + inner] = dot(p_ref[...], mixed_up, 1, 0).astype(BF16)
    out_ref[0, 2 * inner :] = aug_ref[0]


def key_value(n, wk, wv, place_k, place_v, aug, first, rows):
    size = aug.shape[2]
    inner = place_k.shape[0]
    width = n.shape[0]
    return pl.pallas_call(
        functools.partial(key_value_body, inner),
        grid=(rows,),
        in_specs=[
            pl.BlockSpec((width, size), lambda r: (0, first + r)),
            picked(wk, 0),
            picked(wv, 0),
            whole(place_k.shape),
            whole(place_v.shape),
            pl.BlockSpec((1, AUG, size), lambda r: (first + r, 0, 0)),
        ],
        out_specs=pl.BlockSpec((1, 2 * inner + AUG, size), lambda r: (r, 0, 0)),
        out_shape=jax.ShapeDtypeStruct((rows, 2 * inner + AUG, size), BF16),
        compiler_params=PARAMS,
        name="key_value",
        cost_estimate=cost(4 * wk.size * rows * size, 4 * wk.size + 2 * n.size),
    )(n, wk, wv, place_k, place_v, aug)


def project_body(n_ref, w_ref, p_ref, out_ref):
    mixed_up = dot(flat_rows(w_ref), n_ref[...], 1, 0).astype(BF16)
    out_ref[...] = dot(p_ref[...], mixed_up, 1, 0).astype(BF16)


def project(n, w, place, tile):
    width, here = n.shape
    inner = place.shape[0]
    return pl.pallas_call(
        project_body,
        grid=(here // tile,),
        in_specs=[pl.BlockSpec((width, tile), lambda t: (0, t)), picked(w, 1), whole(place.shape)],
        out_specs=pl.BlockSpec((inner, tile), lambda t: (0, t)),
        out_shape=jax.ShapeDtypeStruct((inner, here), BF16),
        compiler_params=PARAMS,
        name="project",
        cost_estimate=cost(1, 1),
    )(n, w, place)


def attend_body(heads, inner, q_ref, u_ref, *refs):
    *blocks, bias_ref, o_ref, lse_ref, s_ref = refs
    for h in range(heads):
        part = slice(h * HEAD, (h + 1) * HEAD)
        q = jnp.concatenate([q_ref[part], u_ref[0]], axis=0)
        top = None
        for s, k_ref in enumerate(blocks):
            k = jnp.concatenate([k_ref[0, part], k_ref[0, 2 * inner :]], axis=0)
            logits = dot(k, q, 0, 0) + bias_ref[h, s]
            s_ref[s] = logits
            peak = jnp.max(logits, axis=0, keepdims=True)
            top = peak if top is None else jnp.maximum(top, peak)
        total, out = None, None
        for s, k_ref in enumerate(blocks):
            e = jnp.exp(s_ref[s] - top)
            part_sum = jnp.sum(e, axis=0, keepdims=True)
            total = part_sum if total is None else total + part_sum
            value = k_ref[0, slice(inner + h * HEAD, inner + (h + 1) * HEAD)]
            term = dot(value, e.astype(BF16), 1, 0)
            out = term if out is None else out + term
        o_ref[part] = (out / total).astype(BF16)
        lse_ref[0, h : h + 1] = top + jnp.log(total)
    pad = lse_ref.shape[1] - heads
    if pad:
        lse_ref[0, heads:] = jnp.zeros((pad, lse_ref.shape[2]), F32)


def attend(qt, u, kv, bias, heads, first):
    rows, depth, size = kv[0].shape
    inner = heads * HEAD
    pad = -(-heads // 8) * 8
    return pl.pallas_call(
        functools.partial(attend_body, heads, inner),
        grid=(rows,),
        in_specs=[
            pl.BlockSpec((inner, size), lambda r: (0, first + r)),
            pl.BlockSpec((1, AUG, size), lambda r: (first + r, 0, 0)),
        ]
        + [pl.BlockSpec((1, depth, size), lambda r: (r, 0, 0))] * len(kv)
        + [whole(bias.shape)],
        out_specs=[
            pl.BlockSpec((inner, size), lambda r: (0, r)),
            pl.BlockSpec((1, pad, size), lambda r: (r, 0, 0)),
        ],
        out_shape=[
            jax.ShapeDtypeStruct((inner, rows * size), BF16),
            jax.ShapeDtypeStruct((rows, pad, size), F32),
        ],
        scratch_shapes=[pltpu.VMEM((len(kv), size, size), F32)],
        compiler_params=PARAMS,
        name="attend",
        cost_estimate=cost(16 * rows * heads * len(kv) * size * size * HEAD, 40_000_000),
    )(qt, u, *kv, bias)


def three(x):
    a = x.astype(BF16).astype(F32)
    rest = x - a
    b = rest.astype(BF16).astype(F32)
    return a, b, rest - b


def attend_back_body(heads, inner, count, more, q_ref, u_ref, *refs):
    blocks = refs[:count]
    bias_ref, o_ref, do_ref, lse_ref = refs[count : count + 4]
    refs = refs[count + 4 :]
    before_ref, refs = (refs[0], refs[1:]) if more else (None, refs)
    dq_ref = refs[0]
    grads = refs[1 : count + 1]
    gb_ref = refs[count + 1]
    size = bias_ref.shape[3]
    row = pl.program_id(0)
    mask_grad = [None] * count
    extra = u_ref[0].astype(F32)
    place = lax.broadcasted_iota(jnp.int32, (AUG, size), 0)

    def pick(parts, base):
        for i, value in enumerate(parts):
            base = jnp.where(place == ONES + i, value, base)
        return base.astype(BF16)

    for h in range(heads):
        part = slice(h * HEAD, (h + 1) * HEAD)
        vpart = slice(inner + h * HEAD, inner + (h + 1) * HEAD)
        q = q_ref[part]
        do = do_ref[part]
        delta = jnp.sum(do.astype(F32) * o_ref[part].astype(F32), axis=0, keepdims=True)
        q_aug = jnp.concatenate([q, pick(three(-lse_ref[0, h : h + 1]), extra)], axis=0)
        do_aug = jnp.concatenate([do, pick(three(-delta), jnp.zeros_like(extra))], axis=0)
        dq = None
        for s, k_ref in enumerate(blocks):
            k = k_ref[0, part]
            aug = k_ref[0, 2 * inner :]
            logits = dot(jnp.concatenate([k, aug], axis=0), q_aug, 0, 0) + bias_ref[h, s]
            p = jnp.exp(logits)
            dp = dot(jnp.concatenate([k_ref[0, vpart], aug], axis=0), do_aug, 0, 0)
            ds = p * dp

            @pl.when(row == 0)
            def _():
                gb_ref[h, s] = before_ref[h, s] + ds if more else ds

            @pl.when(row > 0)
            def _():
                gb_ref[h, s] += ds

            low = ds.astype(BF16)
            grads[s][0, vpart] = dot(do, p.astype(BF16), 1, 1).astype(BF16)
            both = dot(q_aug, low, 1, 1)
            grads[s][0, part] = both[:HEAD].astype(BF16)
            g = both[HEAD : HEAD + 1]
            mask_grad[s] = g if mask_grad[s] is None else mask_grad[s] + g
            term = dot(k, low, 1, 0)
            dq = term if dq is None else dq + term
        dq_ref[part] = dq.astype(BF16)
    for s in range(count):
        grads[s][0, 2 * inner :] = jnp.broadcast_to(mask_grad[s], (AUG, size)).astype(BF16)


def attend_back(qt, u, kv, bias, ot, dot_t, lse, heads, first, before):
    rows, depth, size = kv[0].shape
    inner = heads * HEAD
    count = len(kv)
    own = pl.BlockSpec((inner, size), lambda r: (0, r))
    col = pl.BlockSpec((inner, size), lambda r: (0, first + r))
    block = pl.BlockSpec((1, depth, size), lambda r: (r, 0, 0))
    out = pl.pallas_call(
        functools.partial(attend_back_body, heads, inner, count, len(before)),
        grid=(rows,),
        in_specs=[col, pl.BlockSpec((1, AUG, size), lambda r: (first + r, 0, 0))]
        + [block] * count
        + [whole(bias.shape), own, col]
        + [pl.BlockSpec((1,) + lse.shape[1:], lambda r: (r, 0, 0))]
        + [whole(b.shape) for b in before],
        out_specs=[own] + [block] * count + [whole(bias.shape)],
        out_shape=[jax.ShapeDtypeStruct((inner, rows * size), BF16)]
        + [jax.ShapeDtypeStruct((rows, depth, size), BF16)] * count
        + [jax.ShapeDtypeStruct(bias.shape, F32)],
        compiler_params=PARAMS,
        name="attend_back",
        cost_estimate=cost(40 * rows * heads * count * size * size * HEAD, 60_000_000),
    )(qt, u, *kv, bias, ot, dot_t, lse, *before)
    return out[0], out[1:-1], out[-1]


def bias_body(heads, slots_ref, buckets_ref, table_ref, bias_ref, buckets_t_ref):
    tables = [jnp.broadcast_to(table_ref[h : h + 1], (8, 128)) for h in range(heads)]
    buckets_t_ref[0] = buckets_ref[...].T
    for i in range(buckets_ref.shape[1] // 8):
        for j in range(buckets_ref.shape[0] // 128):
            at = (slice(i * 8, (i + 1) * 8), slice(j * 128, (j + 1) * 128))
            index = buckets_t_ref[(0,) + at]
            for h in range(heads):
                bias_ref[(h, 0) + at] = jnp.take_along_axis(tables[h], index, axis=1)


def bias_of(slots, buckets, table):
    heads = table.shape[0]
    size, blocks = buckets.shape[0], slots.shape[0]
    spec = pltpu.PrefetchScalarGridSpec(
        num_scalar_prefetch=1,
        grid=(blocks,),
        in_specs=[
            pl.BlockSpec((size, size), lambda s, slots: (0, slots[s])),
            pl.BlockSpec(table.shape, lambda s, slots: (0, 0)),
        ],
        out_specs=[
            pl.BlockSpec((heads, 1, size, size), lambda s, slots: (0, s, 0, 0)),
            pl.BlockSpec((1, size, size), lambda s, slots: (s, 0, 0)),
        ],
    )
    return pl.pallas_call(
        functools.partial(bias_body, heads),
        grid_spec=spec,
        out_shape=[
            jax.ShapeDtypeStruct((heads, blocks, size, size), F32),
            jax.ShapeDtypeStruct((blocks, size, size), jnp.int32),
        ],
        compiler_params=PARAMS,
        name="bias_of",
        cost_estimate=cost(1, 1),
    )(slots, buckets, table)


def sums_body(heads, count, buckets_ref, g_ref, out_ref):
    @pl.when(pl.program_id(0) == 0)
    def _():
        out_ref[...] = jnp.zeros_like(out_ref)

    total = out_ref[...]
    for i in range(buckets_ref.shape[1] // 8):
        at = slice(i * 8, (i + 1) * 8)
        index = buckets_ref[0, at]
        hot = [jnp.where(index == b, 1.0, 0.0) for b in range(count)]
        hot = jnp.concatenate(hot, axis=0).astype(BF16)
        g = jnp.concatenate([g_ref[h, 0, at] for h in range(heads)], axis=0)
        high = g.astype(BF16)
        low = (g - high.astype(F32)).astype(BF16)
        total += dot(jnp.concatenate([high, low], axis=0), hot, 1, 1)
    out_ref[...] = total


def bucket_sums(grad_bias, buckets, count):
    heads, blocks, size, _ = grad_bias.shape
    shape = (2 * heads * 8, count * 8)
    raw = pl.pallas_call(
        functools.partial(sums_body, heads, count),
        grid=(blocks,),
        in_specs=[
            pl.BlockSpec((1, size, size), lambda s: (s, 0, 0)),
            pl.BlockSpec((heads, 1, size, size), lambda s: (0, s, 0, 0)),
        ],
        out_specs=pl.BlockSpec(shape, lambda s: (0, 0)),
        out_shape=jax.ShapeDtypeStruct(shape, F32),
        compiler_params=PARAMS,
        name="bucket_sums",
        cost_estimate=cost(64 * grad_bias.size, 4 * grad_bias.size),
    )(buckets, grad_bias)
    raw = raw.reshape(2, heads, 8, count, 8)
    return jnp.sum(jnp.where(jnp.eye(8, dtype=bool)[None, None, :, None, :], raw, 0.0), (0, 2, 4)).T


def mix_body(x_ref, o_ref, w_ref, place_ref, gain_ref, mixed_ref, pair_ref, *piece_refs):
    spread = dot(place_ref[...], o_ref[...], 0, 0).astype(BF16)
    mixed = x_ref[0].astype(F32) + dot(flat_rows(w_ref), spread, 0, 0)
    mixed_ref[...] = mixed
    scale = lax.rsqrt(jnp.mean(mixed * mixed, axis=0, keepdims=True) + NORM_EPSILON)
    n = (mixed * scale * gain_ref[...]).astype(BF16)
    pair_ref[0] = n
    put_pieces(piece_refs, n)


def group_specs(shape, count, per, rank):
    def place(g):
        def index(r):
            inside = jnp.clip(r - g * per, 0, per - 1)
            return (0, inside) if rank == 2 else (inside, 0, 0)

        return index

    return [pl.BlockSpec(shape, place(g)) for g in range(count)]


def mix(x, ot, w, place, gain):
    rows, width, size = x.shape
    inner = ot.shape[0]
    here = rows * size
    piece_specs, piece_shapes = pieces_of((width, here), size)
    return pl.pallas_call(
        mix_body,
        grid=(rows,),
        in_specs=[
            pl.BlockSpec((1, width, size), lambda r: (r, 0, 0)),
            pl.BlockSpec((inner, size), lambda r: (0, r)),
            picked(w, 1),
            whole(place.shape),
            whole(gain.shape),
        ],
        out_specs=[
            pl.BlockSpec((width, size), lambda r: (0, r)),
            pl.BlockSpec((1, width, size), lambda r: (0, 0, r)),
        ]
        + piece_specs,
        out_shape=[
            jax.ShapeDtypeStruct((width, here), F32),
            jax.ShapeDtypeStruct((2, width, here), BF16),
        ]
        + piece_shapes,
        compiler_params=PARAMS,
        name="mix",
        cost_estimate=cost(1, 1),
    )(x, ot, w, place, gain)


def units_of(ws):
    return sum(w.shape[0] * w.shape[2] for w in ws)


def entries_of(ws):
    return sum(w.shape[0] for w in ws)


def loads_of(refs, buf, sems, kinds):
    copies, start = [], 0
    for a, ref in enumerate(refs):
        for k, kind in enumerate(kinds):
            inside = buf.at[k, pl.ds(start, ref.shape[0])]
            copies.append(pltpu.make_async_copy(ref.at[:, kind], inside, sems.at[a, k]))
        start += ref.shape[0]
    return copies


def ffn_body(count, masks, me_ref, *refs):
    ws, (n_ref, dy_ref, act_ref), refs = refs[:count], refs[count : count + 3], refs[count + 3 :]
    gs, (buf, acc, in_sems, out_sems) = refs[:-4], refs[-4:]
    t = pl.program_id(0)
    entries, rows, width = buf.shape[1:]
    size = entries * rows
    loads = loads_of(ws, buf, in_sems, range(3))

    @pl.when(t == 0)
    def _():
        for copy in loads:
            copy.start()
        acc[...] = jnp.zeros_like(acc)
        for copy in loads:
            copy.wait()

    norm = n_ref[0]
    dy = dy_ref[0]
    gate = dot(buf[0].reshape(size, width), norm, 1, 0)
    up = dot(buf[1].reshape(size, width), norm, 1, 0)
    dhid = dot(buf[2].reshape(size, width), dy, 1, 0)
    inside = gate * (0.7978845608028654 + 0.035677408136300125 * (gate * gate))
    half = 0.5 + 0.5 * jnp.tanh(inside)
    gelu = gate * half
    slope = half * (1.0 + (1.0 - half) * (6.0 * inside - 3.1915382432114616 * gate))
    dgate = (dhid * up * slope).astype(BF16)
    dup = (dhid * gelu).astype(BF16)
    hidden = (gelu * up).astype(BF16)
    act_ref[0] = dgate
    act_ref[1] = dup
    act_ref[2] = hidden
    acc[0] += dot(dgate, norm, 1, 1)
    acc[1] += dot(dup, norm, 1, 1)
    acc[2] += dot(hidden, dy, 1, 1)

    @pl.when(t == pl.num_programs(0) - 1)
    def _():
        for k in range(3):
            buf[k] = acc[k].astype(BF16).reshape(entries, rows, width)
        stores = []
        if masks is None:
            start = 0
            for g, out in enumerate(gs):
                for k in range(3):
                    inside = buf.at[k, pl.ds(start, out.shape[0])]
                    stores.append(pltpu.make_async_copy(inside, out.at[:, k], out_sems.at[g, k]))
                start += out.shape[0]
        else:
            part = len(masks) // 2
            for s, mask in enumerate(masks):
                for k in range(3):
                    inside, out = buf.at[k, me_ref[0] ^ mask], gs[s // part].at[s % part, k]
                    stores.append(pltpu.make_async_copy(inside, out, out_sems.at[s, k]))
        for copy in stores:
            copy.start()
        for copy in stores:
            copy.wait()


def ffn_group(me, ws, n, dy, tile, masks=None):
    halves, width, tokens = n.shape
    per = tokens // tile
    all_tokens = halves * tokens
    size = units_of(ws)
    inner = (entries_of(ws),) + ws[0].shape[2:]
    column = pl.BlockSpec((1, width, tile), lambda t, me: (t // per, 0, t % per))
    stores = len(ws) if masks is None else len(masks)
    shapes = [w.shape for w in ws]
    if masks is not None:
        shapes = [(inner[0] // 2, 3) + inner[1:]] * 2
    spec = pltpu.PrefetchScalarGridSpec(
        num_scalar_prefetch=1,
        grid=(halves * per,),
        in_specs=[ANY] * len(ws) + [column, column],
        out_specs=[pl.BlockSpec((3, size, tile), lambda t, me: (0, 0, t))] + [ANY] * len(shapes),
        scratch_shapes=[
            pltpu.VMEM((3,) + inner, BF16),
            pltpu.VMEM((3, size, width), F32),
            pltpu.SemaphoreType.DMA((len(ws), 3)),
            pltpu.SemaphoreType.DMA((stores, 3)),
        ],
    )
    out = pl.pallas_call(
        functools.partial(ffn_body, len(ws), masks),
        grid_spec=spec,
        out_shape=[jax.ShapeDtypeStruct((3, size, all_tokens), BF16)]
        + [jax.ShapeDtypeStruct(shape, BF16) for shape in shapes],
        compiler_params=PARAMS,
        name="ffn_group",
        cost_estimate=cost(1, 1),
    )(me, *ws, n, dy)
    return out[0], out[1:]


def ffn_terms(layout, kinds, refs):
    count, total = len(layout), sum(layout)
    ws, acts, refs = refs[:total], refs[total : total + count], refs[total + count :]
    bufs, sems = refs[:count], refs[count]

    @pl.when(pl.program_id(0) == 0)
    def _():
        copies, start = [], 0
        for p, arrays in enumerate(layout):
            copies += loads_of(ws[start : start + arrays], bufs[p], sems.at[p], kinds)
            start += arrays
        for copy in copies:
            copy.start()
        for copy in copies:
            copy.wait()

    out = None
    for act, buf in zip(acts, bufs):
        _, entries, rows, width = buf.shape
        for k in range(len(kinds)):
            term = dot(buf[k].reshape(entries * rows, width), act[k], 0, 0)
            out = term if out is None else out + term
    return out


def layout_of(groups):
    return tuple(len(ws) for ws in groups)


def flat_of(groups):
    return [w for ws in groups for w in ws]


def ffn_specs(groups, acts, kinds, tile, first):
    at = kinds[0] // len(kinds)
    return [ANY] * len(flat_of(groups)) + [
        pl.BlockSpec((len(kinds), a.shape[1], tile), lambda t: (at, 0, first + t)) for a in acts
    ]


def ffn_scratch(groups, kinds):
    return [
        pltpu.VMEM((len(kinds), entries_of(ws)) + ws[0].shape[2:], BF16) for ws in groups
    ] + [pltpu.SemaphoreType.DMA((len(groups), max(layout_of(groups)), len(kinds)))]


def ffn_back_body(layout, kinds, pieces, *refs):
    ins = sum(layout) + len(layout)
    total = ffn_terms(layout, kinds, refs[:ins] + refs[ins + pieces :])
    put_pieces(refs[ins : ins + pieces], total.astype(BF16))


def ffn_back(groups, acts, kinds, start, count, tile, pieces):
    width = groups[0][0].shape[3]
    piece_specs, piece_shapes = pieces_of((width, count), tile, pieces)
    return pl.pallas_call(
        functools.partial(ffn_back_body, layout_of(groups), kinds, pieces),
        grid=(count // tile,),
        in_specs=ffn_specs(groups, acts, kinds, tile, start // tile),
        out_specs=piece_specs,
        out_shape=piece_shapes,
        scratch_shapes=ffn_scratch(groups, kinds),
        compiler_params=PARAMS,
        name="ffn_back",
        cost_estimate=cost(1, 1),
    )(*flat_of(groups), *acts)


def layer_out_body(layout, *refs):
    ins = sum(layout) + len(layout)
    mixed_ref, got_ref, out_ref = refs[ins : ins + 3]
    total = ffn_terms(layout, [2], refs[:ins] + refs[ins + 3 :])
    out_ref[0] = (mixed_ref[...] + total + got_ref[...].astype(F32)).astype(BF16)


def layer_out_of(groups, acts, mixed, got, rows):
    width, here = mixed.shape
    size = here // rows
    col = pl.BlockSpec((width, size), lambda t: (0, t))
    return pl.pallas_call(
        functools.partial(layer_out_body, layout_of(groups)),
        grid=(rows,),
        in_specs=ffn_specs(groups, acts, [2], size, 0) + [col, col],
        out_specs=pl.BlockSpec((1, width, size), lambda t: (t, 0, 0)),
        out_shape=jax.ShapeDtypeStruct((rows, width, size), BF16),
        scratch_shapes=ffn_scratch(groups, [2]),
        compiler_params=PARAMS,
        name="layer_out_of",
        cost_estimate=cost(1, 1),
    )(*flat_of(groups), *acts, mixed, got)


def mix_back_body(layout, *refs):
    ins = sum(layout) + len(layout)
    weights, refs = refs[:ins], refs[ins:]
    pieces, refs = refs[:PIECES], refs[PIECES:]
    mixed_ref, dy_ref, o_ref, w_ref, place_ref, home_ref, gain_ref = refs[:7]
    refs = refs[7:]
    inside_grad = len(refs) == 5 + len(layout) + 1
    dmixed_ref, do_ref, gg_ref = refs[:3]
    gw_ref, acc = refs[3:5] if inside_grad else (None, None)
    row = pl.program_id(0)
    got = jnp.concatenate([r[...] for r in pieces], axis=0)
    dn = ffn_terms(layout, [0, 1], weights + refs[-len(layout) - 1 :]) + got.astype(F32)
    mixed = mixed_ref[...]
    scale = lax.rsqrt(jnp.mean(mixed * mixed, axis=0, keepdims=True) + NORM_EPSILON)
    unit = mixed * scale
    scaled = dn * gain_ref[...]
    inside = jnp.mean(scaled * unit, axis=0, keepdims=True)
    dmixed = dy_ref[0].astype(F32) + scale * (scaled - unit * inside)
    dmixed_ref[...] = dmixed
    low = dmixed.astype(BF16)
    spread = dot(home_ref[...], o_ref[...], 0, 0).astype(BF16)
    mixed_up = dot(flat_rows(w_ref), low, 1, 0).astype(BF16)
    do_ref[...] = dot(place_ref[...], mixed_up, 1, 0).astype(BF16)
    both = dn * unit
    gain_part = both[:, :128]
    for j in range(1, both.shape[1] // 128):
        gain_part = gain_part + both[:, j * 128 : (j + 1) * 128]

    @pl.when(row == 0)
    def _():
        gg_ref[...] = gain_part

    @pl.when(row > 0)
    def _():
        gg_ref[...] += gain_part

    if inside_grad:
        product = dot(spread, low, 1, 1)

        @pl.when(row == 0)
        def _():
            acc[...] = product

        @pl.when(row > 0)
        def _():
            acc[...] += product

        @pl.when(row == pl.num_programs(0) - 1)
        def _():
            gw_ref[...] = acc[...].astype(BF16)


def mix_back(groups, acts, mixed, d1, dy, ot, w, place, home, gain):
    rows, width, size = dy.shape
    inner = ot.shape[0]
    here = rows * size
    col = pl.BlockSpec((width, size), lambda r: (0, r))
    head_col = pl.BlockSpec((inner, size), lambda r: (0, r))
    grad = (home.shape[1], width)
    fits = grad[0] <= 1024
    out = pl.pallas_call(
        functools.partial(mix_back_body, layout_of(groups)),
        grid=(rows,),
        in_specs=ffn_specs(groups, acts, [0, 1], size, 0)
        + pieces_of(mixed.shape, size)[0]
        + [col, pl.BlockSpec((1, width, size), lambda r: (r, 0, 0)), head_col]
        + [picked(w, 1), whole(place.shape), whole(home.shape), whole(gain.shape)],
        out_specs=[col, head_col, whole((width, 128))] + [whole(grad)] * fits,
        out_shape=[
            jax.ShapeDtypeStruct((width, here), F32),
            jax.ShapeDtypeStruct((inner, here), BF16),
            jax.ShapeDtypeStruct((width, 128), F32),
        ]
        + [jax.ShapeDtypeStruct(grad, BF16)] * fits,
        scratch_shapes=[pltpu.VMEM(grad, F32)] * fits + ffn_scratch(groups, [0, 1]),
        compiler_params=PARAMS,
        name="mix_back",
        cost_estimate=cost(1, 1),
    )(*flat_of(groups), *acts, *d1, mixed, dy, ot, w, place, home, gain)
    if not fits:
        spread = dot(home, ot, 0, 0).astype(BF16)
        out = [*out, dot(spread, out[0].astype(BF16), 1, 1).astype(BF16)]
    return out


def grads_body(per, groups, parts, n_ref, *refs):
    d_refs, refs = refs[:groups], refs[groups:]
    places, refs = refs[: len(parts)], refs[len(parts) :]
    outs, (acc, d_scr) = refs[: 2 * len(parts)], refs[2 * len(parts) :]
    row = pl.program_id(0)
    n = n_ref[...]
    for g, d_ref in enumerate(d_refs):

        @pl.when(row // per == g)
        def _():
            d_scr[...] = d_ref[...].reshape(d_scr.shape)

    products = []
    for (start, stop), p_ref in zip(parts, places):
        spread = dot(p_ref[...], d_scr[start:stop], 0, 0).astype(BF16)
        products.append(dot(spread, n, 1, 1))

    @pl.when(row == 0)
    def _():
        for j, product in enumerate(products):
            acc[j] = product

    @pl.when(row > 0)
    def _():
        for j, product in enumerate(products):
            acc[j] += product

    @pl.when(row == pl.num_programs(0) - 1)
    def _():
        half = acc.shape[1] // 2
        for j in range(len(parts)):
            outs[2 * j][...] = acc[j, :half].astype(BF16)
            outs[2 * j + 1][...] = acc[j, half:].astype(BF16)


def projection_grads(n, groups, parts, places, rows):
    if len(parts) > 1 and places[0].shape[1] > 1024:
        return [
            half
            for part, p in zip(parts, places)
            for half in projection_grads(n, groups, [part], [p], rows)
        ]
    width, here = n.shape
    size = here // rows
    per = rows // len(groups)
    rank = groups[0].ndim
    depth = groups[0].shape[-2]
    shape = (depth, size) if rank == 2 else (1, depth, size)
    wide = (places[0].shape[1], width)
    return pl.pallas_call(
        functools.partial(grads_body, per, len(groups), parts),
        grid=(rows,),
        in_specs=[pl.BlockSpec((width, size), lambda r: (0, r))]
        + group_specs(shape, len(groups), per, rank)
        + [whole(p.shape) for p in places],
        out_specs=[whole((wide[0] // 2, width))] * (2 * len(parts)),
        out_shape=[jax.ShapeDtypeStruct((wide[0] // 2, width), BF16)] * (2 * len(parts)),
        scratch_shapes=[pltpu.VMEM((len(parts),) + wide, F32), pltpu.VMEM((depth, size), BF16)],
        compiler_params=PARAMS,
        name="projection_grads",
        cost_estimate=cost(
            2 * len(parts) * wide[0] * width * here, 2 * n.size + 2 * len(parts) * wide[0] * width
        ),
    )(n, *groups, *places)


def last_body(per, groups, x_ref, dm_ref, *refs):
    dq_refs, dkv_refs, refs = refs[:groups], refs[groups : 2 * groups], refs[2 * groups :]
    ws, places, refs = refs[:3], refs[3:6], refs[6:]
    gain_ref, gx_ref, gg_ref, d_scr = refs
    row = pl.program_id(0)
    inner = dq_refs[0].shape[0]
    for g in range(groups):

        @pl.when(row // per == g)
        def _():
            d_scr[:inner] = dq_refs[g][...]
            d_scr[inner:] = dkv_refs[g][0, : 2 * inner]

    dn = None
    for j in range(3):
        spread = dot(places[j][...], d_scr[j * inner : (j + 1) * inner], 0, 0).astype(BF16)
        term = dot(flat_rows(ws[j]), spread, 0, 0)
        dn = term if dn is None else dn + term
    x = x_ref[0].astype(F32)
    scale = lax.rsqrt(jnp.mean(x * x, axis=0, keepdims=True) + NORM_EPSILON)
    unit = x * scale
    scaled = dn * gain_ref[...]
    inside = jnp.mean(scaled * unit, axis=0, keepdims=True)
    gx_ref[0] = dm_ref[...] + scale * (scaled - unit * inside)
    both = dn * unit
    gain_part = both[:, :128]
    for j in range(1, both.shape[1] // 128):
        gain_part = gain_part + both[:, j * 128 : (j + 1) * 128]

    @pl.when(row == 0)
    def _():
        gg_ref[...] = gain_part

    @pl.when(row > 0)
    def _():
        gg_ref[...] += gain_part


def last(x, dmixed, dqs, dkvs, ws, places, gain):
    rows, width, size = x.shape
    inner = dqs[0].shape[0]
    per = rows // len(dqs)
    col = pl.BlockSpec((width, size), lambda r: (0, r))
    block = pl.BlockSpec((1, width, size), lambda r: (r, 0, 0))
    return pl.pallas_call(
        functools.partial(last_body, per, len(dqs)),
        grid=(rows,),
        in_specs=[block, col]
        + group_specs((inner, size), len(dqs), per, 2)
        + group_specs((1,) + dkvs[0].shape[1:], len(dkvs), per, 3)
        + [picked(w, index) for w, index in zip(ws, (1, 0, 0))]
        + [whole(p.shape) for p in places]
        + [whole(gain.shape)],
        out_specs=[block, whole((width, 128))],
        out_shape=[jax.ShapeDtypeStruct(x.shape, F32), jax.ShapeDtypeStruct((width, 128), F32)],
        scratch_shapes=[pltpu.VMEM((3 * inner, size), BF16)],
        compiler_params=PARAMS,
        name="last",
        cost_estimate=cost(6 * ws[0].size * rows * size, 14 * x.size + 6 * ws[0].size),
    )(x, dmixed, *dqs, *dkvs, *ws, *places, gain)


def after(value, *markers):
    return lax.optimization_barrier((value, markers))[0]


def pad_rows(w, rows):
    return jnp.pad(w, ((0, rows - w.shape[0]), (0, 0))) if rows > w.shape[0] else w


class Links:
    def __init__(self, dp, pairs):
        self.sizes = {"dp": dp, "x": pairs, "core": 2}
        self.strides = {"dp": 2 * pairs, "x": 2, "core": 1}
        self.core = ("core", 1)
        self.across = ("x", 1)
        self.near = ("dp", 1)
        self.far_count = dp // 2

    def swap(self, x, step):
        axis, mask = step
        return lax.ppermute(x, axis, [(i, i ^ mask) for i in range(self.sizes[axis])])

    def far_steps(self):
        return [("dp", k << 1) for k in range(1, self.far_count)]

    def far_bits(self):
        return [("dp", 2 << b) for b in range(self.far_count.bit_length() - 1)]

    def masks(self, steps):
        found = [(k << 1) * self.strides["dp"] for k in range(self.far_count)]
        for axis, mask in steps:
            found = found + [f ^ (mask * self.strides[axis]) for f in found]
        return found


def per_device(
    dp, ctx,
    tokens, soft_mask, segment_ids, buckets, gain_attn, gain_ffn, bias_table,
    w_query, w_key, w_value, w_attn_out, w_gate, w_up, w_ffn_out, cotangent,
):
    links = Links(dp, ctx // 2)
    swap, core, across, near = links.swap, links.core, links.across, links.near
    far = links.far_steps()
    rows, size, width = tokens.shape
    here = rows * size
    count, heads = bias_table.shape
    inner = heads * HEAD
    my_dp, my_ctx = lax.axis_index("dp"), lax.axis_index("x") * 2 + lax.axis_index("core")
    me = my_dp * ctx + my_ctx
    tile = min(512, here)
    order_a, order_b = [near, across], [across, near]

    def spread_of(steps):
        real = w_query.shape[0]
        owners = me ^ jnp.asarray(links.masks(steps), dtype=jnp.int32)
        inside = jnp.arange(each)
        feature = owners[:, None] * real + inside[None, :]
        feature = jnp.where(inside[None, :] < real, feature, -1).reshape(-1)
        return (jnp.arange(inner)[:, None] == feature[None, :]).astype(BF16)

    token = []

    def run(work, *args):
        if token:
            args = lax.optimization_barrier((args, tuple(token)))[0]
        out = work(*args)
        token[:] = jax.tree.leaves(out)
        return out

    each = -(-w_query.shape[0] // ROW_TILE) * ROW_TILE
    slot = lambda w: pad_rows(w, each)[None]
    flat = lambda w: w.reshape(-1, width)
    far_bits = links.far_bits()
    ab, ba = (near, across), (across, near)

    def exchange(arrays, steps):
        return [(a, swap(a, step)) for a, step in zip(arrays, steps)]

    def swap_core(value):
        return [swap(v, core) for v in value]

    def close(value):
        return run(lambda v: v, value)

    class Gather:
        def __init__(self, array, cuts, direct=False, mark=None, paths=(ab, ba)):
            if mark is not None:
                array = after(array, mark)
            self.cuts, self.stage, self.paths = cuts, 0, paths
            self.hops = 1 if direct else len(far_bits)
            steps = far if direct else far_bits[:1]
            self.held = [array] + [swap(array, step) for step in steps]

        def go(self):
            self.stage += 1
            if self.stage < self.hops:
                (array,) = run(lambda *p: join([p]), *self.held)
                self.held = [array, swap(array, far_bits[self.stage])]
            elif self.stage == self.hops:
                parts = run(lambda *p: cut_join(list(p), self.cuts), *self.held)
                self.held = exchange(parts, self.paths[0])
            elif self.stage == self.hops + 1:
                self.held = exchange(run(join, self.held), self.paths[1])

        def start_of(self):
            first = self.held[0]
            return first[0] if isinstance(first, tuple) else first

        def core_go(self):
            self.held = exchange(run(join, self.held), (core, core))

        def core_end(self):
            return run(join, self.held)

    attn_w = Gather(
        jnp.concatenate([slot(w) for w in (w_key, w_attn_out, w_value, w_query)], axis=1)[:, None],
        [(0, 2 * each), (2 * each, 2 * each)],
        direct=True,
    )
    units = -(-w_gate.shape[0] // ROW_TILE)
    ffn_own = after((w_gate, w_up, w_ffn_out), attn_w.held[0])
    padded = [pad_rows(w, units * ROW_TILE) for w in ffn_own]
    marks = [0, 3, 5, 7] if units == 7 else list(range(units + 1))
    shards = [
        jnp.stack([w[low * ROW_TILE : high * ROW_TILE] for w in padded])
        for low, high in zip(marks, marks[1:])
    ]
    same_core = ("dp", "x")
    by_hops = units == 7
    last_group = len(shards) - 1

    x = jnp.transpose(tokens, (0, 2, 1))
    dy = jnp.transpose(cotangent, (0, 2, 1))
    gain_one, gain_two = gain_attn[:, None], gain_ffn[:, None]
    place_a, place_b = spread_of(order_a + [core]), spread_of(order_b + [core])
    real = w_query.shape[0]
    segs = lax.dynamic_slice_in_dim(segment_ids, my_ctx * size, size, 1)
    same = segs[:, None, :] == jnp.arange(DOCS, dtype=segs.dtype)[None, :, None]
    ones = jnp.ones((rows, 1, size), BF16)
    rest = AUG - 1 - DOCS
    aug = jnp.concatenate(
        [soft_mask[:, None, :], same.astype(BF16)] + [ones] * 3
        + [jnp.zeros((rows, rest - 3, size), BF16)],
        axis=1,
    )
    query_aug = jnp.concatenate(
        [ones, jnp.where(same, 0.0, MASK_VALUE).astype(BF16), jnp.zeros((rows, rest, size), BF16)],
        axis=1,
    )
    normed, dy_pair, *dy_own = run(first_norm, x, dy, gain_one)
    place_a, place_b, aug, query_aug, shards = close((place_a, place_b, aug, query_aug, shards))

    attn_w.go()
    ffn_w = [
        [lax.all_gather(after(shard, attn_w.start_of()), same_core)]
        for shard in (shards[:-1] if by_hops else shards)
    ]
    slots = jnp.array([0, 2, 1, 3], jnp.int32) ^ my_ctx
    bias, buckets_t = run(
        bias_of, slots, buckets, jnp.pad(bias_table.T, ((0, 0), (0, 128 - count)))
    )
    dy_parts = swap_core(dy_own)
    attn_w.go()
    if by_hops:
        last_w = Gather(
            shards[-1][None],
            [(0, shards[-1].shape[1])],
            mark=attn_w.start_of(),
            paths=((across,), (near,)),
        )
    dy_pair = run(fill, dy_pair, dy_parts)
    if by_hops:
        last_w.go()
    attn_w.core_go()
    wko, wvq = attn_w.core_end()
    kv_own = run(lambda *a: key_value(*a, 0, rows), normed, wko, wvq, place_a, place_b, aug)
    kv_across = swap(kv_own, across)
    kv_core = swap(kv_own, core)
    queries = run(lambda n, w, p: project(n, w, p, tile), normed, wvq, place_b)
    kv_core = close(kv_core)

    kv = run(lambda *k: list(k), kv_own, kv_across, kv_core)
    kv.append(close(jnp.concatenate([swap(k, core) for k in jnp.split(kv[1], rows)])))
    if by_hops:
        last_w.go()
    attended, lse = run(lambda *a: attend(*a, heads, 0), queries, query_aug, kv, bias)
    mixed, n_pair, *normed_two = run(mix, x, attended, wko, place_a, gain_two)
    n_parts = close(swap_core(normed_two))
    if by_hops:
        last_w.go()
    n_pair = run(fill, n_pair, n_parts)

    class Sums:
        def __init__(self, grads, paths, direct=False):
            self.paths, self.direct = paths[: len(grads)], direct
            self.stage = 0
            self.send(grads)

        def send(self, halves):
            self.keep = [h[0] for h in halves]
            self.got = [swap(h[1], p[self.stage]) for h, p in zip(halves, self.paths)]

        def go(self):
            near_hops = len(self.paths[0])
            hops = near_hops + (1 if self.direct else len(far_bits))
            self.stage += 1
            if self.stage > hops:
                return
            if self.stage < near_hops:
                self.send(run(add_halves, self.keep, self.got))
                return
            if self.stage == near_hops:
                rows_of = [k.shape[-2] for k in self.keep]
                self.edges = [sum(rows_of[:k]) for k in range(len(rows_of) + 1)]
                if self.direct:
                    piles = run(lambda k, r: add_piles(k, r, self.edges), self.keep, self.got)
                    self.keep = [piles[0]]
                    self.got = [swap(pile, step) for pile, step in zip(piles[1:], far)]
                    return
                halves = run(lambda k, r: add_merge(k, r, self.edges), self.keep, self.got)
            elif self.stage < hops:
                halves = run(add_halves, self.keep, self.got)[0]
            else:
                got = after(self.got, *token)
                self.out = add_last(self.keep[0], got, self.edges)
                return
            self.keep = [halves[0]]
            self.got = [swap(halves[1], far_bits[hops - 1 - self.stage])]

    acts, sums = [], []
    me_same = (my_dp * (ctx // 2) + lax.axis_index("x")).reshape(1)
    masks = [[m >> 1 for m in links.masks(steps)] for steps in (ab, ba)]
    ffn_grads = []
    if by_hops:
        ffn_w.append(None)
    for i, ws in enumerate(ffn_w):
        if i == last_group and by_hops:
            ws = ffn_w[i] = last_ws
        some = tile if units_of(ws) <= 768 else tile // 2
        mask = masks[0] if by_hops and i == last_group - 1 else None
        act, grads = run(
            lambda m, w, n, d: ffn_group(m, w, n, d, some, mask), me_same, ws, n_pair, dy_pair
        )
        acts.append(act)
        if by_hops and i == 0:
            last_ws = close(list(last_w.held[0]))
            grads = [after(g, last_ws) for g in grads]
        if by_hops and i >= last_group - 1:
            ffn_grads.append(grads)
        else:
            ffn_grads.append(lax.psum_scatter(grads[0], same_core))
    if by_hops:
        sums = [Sums(ffn_grads[-2:], [ba, ab])]

    def tick():
        for s in sums:
            s.go()

    back = run(lambda p, a: ffn_back(p, a, [0, 1], here, here, tile, PIECES), ffn_w, acts)
    dn_got = swap_core(back)
    (out_other,) = run(lambda p, a: ffn_back(p, a, [2], here, here, tile, 1), ffn_w, acts)
    dn_got = close(dn_got)
    out_got = swap(out_other, core)

    dmixed, dattended, gain_two_part, gwo = run(
        mix_back, ffn_w, acts, mixed, dn_got, dy, attended, wko, place_a, place_a, gain_two
    )
    tick()
    out_got = close(out_got)
    dq, dkv, grad_bias = run(
        lambda *a: attend_back(*a, heads, 0, []),
        queries, query_aug, kv, bias, attended, dattended, lse,
    )
    by_core = [(dkv[0], swap(dkv[2], core)), (dkv[1], swap(dkv[3], core))]
    tick()
    if by_hops:
        ffn_grads[0] = close(ffn_grads[0])
    entries = lambda g: tuple(v.reshape(-1, each, width) for v in g)
    home_a, home_b = (core,) + ba, (core,) + ab
    gwq = run(
        lambda n, d, p: projection_grads(n, [d], [(0, inner)], [p], rows), normed, dq, place_b
    )
    own, other = run(add_pairs, by_core)
    other = swap(other, across)
    part = gwo.shape[0] // 2
    query_sum = Sums([entries((gwo[:part], gwo[part:])), entries(gwq)], [home_a, home_b])
    grad_table = run(lambda g, b: bucket_sums(g, b, count), grad_bias, buckets_t)
    query_sum.go()
    out = run(lambda *a: layer_out_of(*a, rows), ffn_w, acts, mixed, out_got)
    query_sum.go()
    (dkv,) = run(add_pairs, [(own, other)])
    gkv = run(
        lambda n, d, pa, pb: projection_grads(n, [d], [(0, inner), (inner, 2 * inner)], [pa, pb], rows),
        normed, dkv, place_a, place_b,
    )
    value_sum = Sums([entries(gkv[:2]), entries(gkv[2:])], [home_a, home_b], direct=dp <= 8)
    tick()
    query_sum.go()
    value_sum.go()
    gx, gain_one_part = run(
        lambda *a: last(a[0], a[1], [a[2]], [a[3]], a[4:7], a[7:10], a[10]),
        x, dmixed, dq, dkv, wvq, wko, wvq, place_b, place_a, place_b, gain_one,
    )
    value_sum.go()
    tick()
    query_sum.go()
    small = jnp.concatenate(
        [jnp.sum(gain_one_part, 1), jnp.sum(gain_two_part, 1), grad_table.reshape(-1)]
    )
    length = small.shape[0]
    small = jnp.pad(small, (0, -length % 1024)).reshape(-1, 128)
    bits = [core, across] + [("dp", 1 << b) for b in range(dp.bit_length() - 1)]
    for k, one in enumerate(bits):
        got = swap(small, one)
        if k in (1, 3):
            value_sum.go()
        small = run(lambda a, b: a + b, small, got)
    for _ in range(len(far_bits) + 4):
        for s in [query_sum, value_sum] + sums:
            s.go()
    small = small.reshape(-1)
    if by_hops:
        ffn_grads[-2:] = sums[0].out
    grad_gate, grad_up, grad_ffn_out = (
        jnp.concatenate([g[j].astype(F32) for g in ffn_grads])[: w_gate.shape[0]] for j in range(3)
    )
    return (
        jnp.transpose(out, (0, 2, 1)),
        jnp.transpose(gx, (0, 2, 1)),
        dkv[:, 2 * inner].astype(F32),
        small[:width],
        small[width : 2 * width],
        small[2 * width : length].reshape(count, heads),
        query_sum.out[1][:real],
        value_sum.out[0][:real],
        value_sum.out[1][:real],
        query_sum.out[0][:real],
        grad_gate,
        grad_up,
        grad_ffn_out,
    )


def solution(mesh):
    dp, ctx = mesh.shape["dp"], mesh.shape["ctx"]
    by_core = Mesh(mesh.devices.reshape(dp, ctx // 2, 2), ("dp", "x", "core"))
    ctx_axes = ("x", "core")
    split = P(("dp", "x", "core"), None)
    act = P("dp", ctx_axes, None)
    in_specs = (
        (act, P("dp", ctx_axes), P("dp", None), P(ctx_axes, None), P(), P(), P()) + (split,) * 7 + (act,)
    )
    out_specs = (act, act, P("dp", ctx_axes), P(), P(), P()) + (split,) * 7
    return jax.shard_map(
        functools.partial(per_device, dp, ctx),
        mesh=by_core,
        in_specs=in_specs,
        out_specs=out_specs,
        check_vma=False,
    )
```

```python
import functools

import jax
import jax.numpy as jnp
import numpy as np
from jax import lax
from jax.experimental import pallas as pl
from jax.experimental.pallas import tpu as pltpu
from jax.sharding import Mesh, PartitionSpec as P

NORM_EPSILON = 1e-06
MASK_VALUE = -1e30
F32, BF16 = jnp.float32, jnp.bfloat16
HEAD = 64
ROW_TILE = 16
AUG = 16
DOCS = 5
ONES = 1 + DOCS
VMEM_LIMIT = 58 * 1024 * 1024
PARAMS = pltpu.CompilerParams(vmem_limit_bytes=VMEM_LIMIT)


def dot(a, b, ca, cb):
    return lax.dot_general(a, b, (((ca,), (cb,)), ((), ())), preferred_element_type=F32)


def whole(shape):
    return pl.BlockSpec(shape, lambda t: (0,) * len(shape), pipeline_mode=pl.Buffered(1))


def cost(flops, nbytes):
    return pl.CostEstimate(flops=1, bytes_accessed=1, transcendentals=0)


ANY = pl.BlockSpec(memory_space=pl.ANY)


def join(pairs):
    return [jnp.concatenate(list(pair), axis=0) for pair in pairs]


def cut_join(parts, cuts):
    out = []
    for cut in cuts:
        at = np.s_[:, :, cut[0] : cut[0] + cut[1]] if isinstance(cut, tuple) else np.s_[:, cut]
        out.append(jnp.concatenate([p[at] for p in parts], axis=0))
    return out


def fill(pair, parts):
    start = 0
    for part in parts:
        pair = pair.at[1, start : start + part.shape[0]].set(part)
        start += part.shape[0]
    return pair


def add_halves(keep, got):
    out = []
    for k, r in zip(keep, got):
        part = k.shape[0] // 2
        out.append((k[:part] + r[:part], k[part:] + r[part:]))
    return out


def add_merge(keep, got, edges):
    part = keep[0].shape[0] // 2
    ends = [slice(None, part), slice(part, None)]
    return [jnp.concatenate([k[e] + r[e] for k, r in zip(keep, got)], axis=-2) for e in ends]


def add_piles(keep, got, edges):
    return [
        jnp.concatenate([k[i : i + 1] + r[i : i + 1] for k, r in zip(keep, got)], axis=-2)
        for i in range(keep[0].shape[0])
    ]


def add_last(keep, got, edges):
    total = keep[0].astype(F32)
    for r in got:
        total = total + r[0].astype(F32)
    return [total[..., a:b, :] for a, b in zip(edges, edges[1:])]


def add_pairs(pairs):
    return [a + b for a, b in pairs]


PIECES = 4


def pieces_of(shape, tile, pieces=PIECES):
    rows, columns = shape
    piece = (rows // pieces, columns)
    specs = [pl.BlockSpec((piece[0], tile), lambda t: (0, t)) for _ in range(pieces)]
    return specs, [jax.ShapeDtypeStruct(piece, BF16)] * pieces


def put_pieces(refs, value):
    step = refs[0].shape[0]
    for k, ref in enumerate(refs):
        ref[...] = value[k * step : (k + 1) * step]


def norm_body(x_ref, dy_ref, gain_ref, n_ref, pair_ref, *piece_refs):
    x = x_ref[0].astype(F32)
    scale = lax.rsqrt(jnp.mean(x * x, axis=0, keepdims=True) + NORM_EPSILON)
    n_ref[...] = (x * scale * gain_ref[...]).astype(BF16)
    pair_ref[0] = dy_ref[0]
    put_pieces(piece_refs, dy_ref[0])


def first_norm(x, dy, gain):
    rows, width, size = x.shape
    block = pl.BlockSpec((1, width, size), lambda r: (r, 0, 0))
    col = pl.BlockSpec((width, size), lambda r: (0, r))
    here = rows * size
    piece_specs, piece_shapes = pieces_of((width, here), size)
    return pl.pallas_call(
        norm_body,
        grid=(rows,),
        in_specs=[block, block, whole(gain.shape)],
        out_specs=[col, pl.BlockSpec((1, width, size), lambda r: (0, 0, r))] + piece_specs,
        out_shape=[
            jax.ShapeDtypeStruct((width, here), BF16),
            jax.ShapeDtypeStruct((2, width, here), BF16),
        ]
        + piece_shapes,
        compiler_params=PARAMS,
        name="first_norm",
        cost_estimate=cost(4 * x.size, 10 * x.size),
    )(x, dy, gain)


def picked(w, index):
    entries, _, _, width = w.shape
    each = w.shape[2] // 2
    return pl.BlockSpec(
        (entries, 1, each, width), lambda t: (0, 0, index, 0), pipeline_mode=pl.Buffered(1)
    )


def flat_rows(w_ref):
    entries, _, each, width = w_ref.shape
    return w_ref[...].reshape(entries * each, width)


def key_value_body(inner, n_ref, wk_ref, wv_ref, pk_ref, pv_ref, aug_ref, out_ref):
    n = n_ref[...]
    for start, w_ref, p_ref in ((0, wk_ref, pk_ref), (inner, wv_ref, pv_ref)):
        mixed_up = dot(flat_rows(w_ref), n, 1, 0).astype(BF16)
        out_ref[0, start : start + inner] = dot(p_ref[...], mixed_up, 1, 0).astype(BF16)
    out_ref[0, 2 * inner :] = aug_ref[0]


def key_value(n, wk, wv, place_k, place_v, aug, first, rows):
    size = aug.shape[2]
    inner = place_k.shape[0]
    width = n.shape[0]
    return pl.pallas_call(
        functools.partial(key_value_body, inner),
        grid=(rows,),
        in_specs=[
            pl.BlockSpec((width, size), lambda r: (0, first + r)),
            picked(wk, 0),
            picked(wv, 0),
            whole(place_k.shape),
            whole(place_v.shape),
            pl.BlockSpec((1, AUG, size), lambda r: (first + r, 0, 0)),
        ],
        out_specs=pl.BlockSpec((1, 2 * inner + AUG, size), lambda r: (r, 0, 0)),
        out_shape=jax.ShapeDtypeStruct((rows, 2 * inner + AUG, size), BF16),
        compiler_params=PARAMS,
        name="key_value",
        cost_estimate=cost(4 * wk.size * rows * size, 4 * wk.size + 2 * n.size),
    )(n, wk, wv, place_k, place_v, aug)


def project_body(n_ref, w_ref, p_ref, out_ref):
    mixed_up = dot(flat_rows(w_ref), n_ref[...], 1, 0).astype(BF16)
    out_ref[...] = dot(p_ref[...], mixed_up, 1, 0).astype(BF16)


def project(n, w, place, tile):
    width, here = n.shape
    inner = place.shape[0]
    return pl.pallas_call(
        project_body,
        grid=(here // tile,),
        in_specs=[pl.BlockSpec((width, tile), lambda t: (0, t)), picked(w, 1), whole(place.shape)],
        out_specs=pl.BlockSpec((inner, tile), lambda t: (0, t)),
        out_shape=jax.ShapeDtypeStruct((inner, here), BF16),
        compiler_params=PARAMS,
        name="project",
        cost_estimate=cost(1, 1),
    )(n, w, place)


def attend_body(heads, inner, q_ref, u_ref, *refs):
    *blocks, bias_ref, o_ref, lse_ref, s_ref = refs
    for h in range(heads):
        part = slice(h * HEAD, (h + 1) * HEAD)
        q = jnp.concatenate([q_ref[part], u_ref[0]], axis=0)
        top = None
        for s, k_ref in enumerate(blocks):
            k = jnp.concatenate([k_ref[0, part], k_ref[0, 2 * inner :]], axis=0)
            logits = dot(k, q, 0, 0) + bias_ref[h, s]
            s_ref[s] = logits
            peak = jnp.max(logits, axis=0, keepdims=True)
            top = peak if top is None else jnp.maximum(top, peak)
        total, out = None, None
        for s, k_ref in enumerate(blocks):
            e = jnp.exp(s_ref[s] - top)
            part_sum = jnp.sum(e, axis=0, keepdims=True)
            total = part_sum if total is None else total + part_sum
            value = k_ref[0, slice(inner + h * HEAD, inner + (h + 1) * HEAD)]
            term = dot(value, e.astype(BF16), 1, 0)
            out = term if out is None else out + term
        o_ref[part] = (out / total).astype(BF16)
        lse_ref[0, h : h + 1] = top + jnp.log(total)
    pad = lse_ref.shape[1] - heads
    if pad:
        lse_ref[0, heads:] = jnp.zeros((pad, lse_ref.shape[2]), F32)


def attend(qt, u, kv, bias, heads, first):
    rows, depth, size = kv[0].shape
    inner = heads * HEAD
    pad = -(-heads // 8) * 8
    return pl.pallas_call(
        functools.partial(attend_body, heads, inner),
        grid=(rows,),
        in_specs=[
            pl.BlockSpec((inner, size), lambda r: (0, first + r)),
            pl.BlockSpec((1, AUG, size), lambda r: (first + r, 0, 0)),
        ]
        + [pl.BlockSpec((1, depth, size), lambda r: (r, 0, 0))] * len(kv)
        + [whole(bias.shape)],
        out_specs=[
            pl.BlockSpec((inner, size), lambda r: (0, r)),
            pl.BlockSpec((1, pad, size), lambda r: (r, 0, 0)),
        ],
        out_shape=[
            jax.ShapeDtypeStruct((inner, rows * size), BF16),
            jax.ShapeDtypeStruct((rows, pad, size), F32),
        ],
        scratch_shapes=[pltpu.VMEM((len(kv), size, size), F32)],
        compiler_params=PARAMS,
        name="attend",
        cost_estimate=cost(16 * rows * heads * len(kv) * size * size * HEAD, 40_000_000),
    )(qt, u, *kv, bias)


def three(x):
    a = x.astype(BF16).astype(F32)
    rest = x - a
    b = rest.astype(BF16).astype(F32)
    return a, b, rest - b


def attend_back_body(heads, inner, count, more, q_ref, u_ref, *refs):
    blocks = refs[:count]
    bias_ref, o_ref, do_ref, lse_ref = refs[count : count + 4]
    refs = refs[count + 4 :]
    before_ref, refs = (refs[0], refs[1:]) if more else (None, refs)
    dq_ref = refs[0]
    grads = refs[1 : count + 1]
    gb_ref = refs[count + 1]
    size = bias_ref.shape[3]
    row = pl.program_id(0)
    mask_grad = [None] * count
    extra = u_ref[0].astype(F32)
    place = lax.broadcasted_iota(jnp.int32, (AUG, size), 0)

    def pick(parts, base):
        for i, value in enumerate(parts):
            base = jnp.where(place == ONES + i, value, base)
        return base.astype(BF16)

    for h in range(heads):
        part = slice(h * HEAD, (h + 1) * HEAD)
        vpart = slice(inner + h * HEAD, inner + (h + 1) * HEAD)
        q = q_ref[part]
        do = do_ref[part]
        delta = jnp.sum(do.astype(F32) * o_ref[part].astype(F32), axis=0, keepdims=True)
        q_aug = jnp.concatenate([q, pick(three(-lse_ref[0, h : h + 1]), extra)], axis=0)
        do_aug = jnp.concatenate([do, pick(three(-delta), jnp.zeros_like(extra))], axis=0)
        dq = None
        for s, k_ref in enumerate(blocks):
            k = k_ref[0, part]
            aug = k_ref[0, 2 * inner :]
            logits = dot(jnp.concatenate([k, aug], axis=0), q_aug, 0, 0) + bias_ref[h, s]
            p = jnp.exp(logits)
            dp = dot(jnp.concatenate([k_ref[0, vpart], aug], axis=0), do_aug, 0, 0)
            ds = p * dp

            @pl.when(row == 0)
            def _():
                gb_ref[h, s] = before_ref[h, s] + ds if more else ds

            @pl.when(row > 0)
            def _():
                gb_ref[h, s] += ds

            low = ds.astype(BF16)
            grads[s][0, vpart] = dot(do, p.astype(BF16), 1, 1).astype(BF16)
            both = dot(q_aug, low, 1, 1)
            grads[s][0, part] = both[:HEAD].astype(BF16)
            g = both[HEAD : HEAD + 1]
            mask_grad[s] = g if mask_grad[s] is None else mask_grad[s] + g
            term = dot(k, low, 1, 0)
            dq = term if dq is None else dq + term
        dq_ref[part] = dq.astype(BF16)
    for s in range(count):
        grads[s][0, 2 * inner :] = jnp.broadcast_to(mask_grad[s], (AUG, size)).astype(BF16)


def attend_back(qt, u, kv, bias, ot, dot_t, lse, heads, first, before):
    rows, depth, size = kv[0].shape
    inner = heads * HEAD
    count = len(kv)
    own = pl.BlockSpec((inner, size), lambda r: (0, r))
    col = pl.BlockSpec((inner, size), lambda r: (0, first + r))
    block = pl.BlockSpec((1, depth, size), lambda r: (r, 0, 0))
    out = pl.pallas_call(
        functools.partial(attend_back_body, heads, inner, count, len(before)),
        grid=(rows,),
        in_specs=[col, pl.BlockSpec((1, AUG, size), lambda r: (first + r, 0, 0))]
        + [block] * count
        + [whole(bias.shape), own, col]
        + [pl.BlockSpec((1,) + lse.shape[1:], lambda r: (r, 0, 0))]
        + [whole(b.shape) for b in before],
        out_specs=[own] + [block] * count + [whole(bias.shape)],
        out_shape=[jax.ShapeDtypeStruct((inner, rows * size), BF16)]
        + [jax.ShapeDtypeStruct((rows, depth, size), BF16)] * count
        + [jax.ShapeDtypeStruct(bias.shape, F32)],
        compiler_params=PARAMS,
        name="attend_back",
        cost_estimate=cost(40 * rows * heads * count * size * size * HEAD, 60_000_000),
    )(qt, u, *kv, bias, ot, dot_t, lse, *before)
    return out[0], out[1:-1], out[-1]


def bias_body(heads, slots_ref, buckets_ref, table_ref, bias_ref, buckets_t_ref):
    tables = [jnp.broadcast_to(table_ref[h : h + 1], (8, 128)) for h in range(heads)]
    buckets_t_ref[0] = buckets_ref[...].T
    for i in range(buckets_ref.shape[1] // 8):
        for j in range(buckets_ref.shape[0] // 128):
            at = (slice(i * 8, (i + 1) * 8), slice(j * 128, (j + 1) * 128))
            index = buckets_t_ref[(0,) + at]
            for h in range(heads):
                bias_ref[(h, 0) + at] = jnp.take_along_axis(tables[h], index, axis=1)


def bias_of(slots, buckets, table):
    heads = table.shape[0]
    size, blocks = buckets.shape[0], slots.shape[0]
    spec = pltpu.PrefetchScalarGridSpec(
        num_scalar_prefetch=1,
        grid=(blocks,),
        in_specs=[
            pl.BlockSpec((size, size), lambda s, slots: (0, slots[s])),
            pl.BlockSpec(table.shape, lambda s, slots: (0, 0)),
        ],
        out_specs=[
            pl.BlockSpec((heads, 1, size, size), lambda s, slots: (0, s, 0, 0)),
            pl.BlockSpec((1, size, size), lambda s, slots: (s, 0, 0)),
        ],
    )
    return pl.pallas_call(
        functools.partial(bias_body, heads),
        grid_spec=spec,
        out_shape=[
            jax.ShapeDtypeStruct((heads, blocks, size, size), F32),
            jax.ShapeDtypeStruct((blocks, size, size), jnp.int32),
        ],
        compiler_params=PARAMS,
        name="bias_of",
        cost_estimate=cost(1, 1),
    )(slots, buckets, table)


def sums_body(heads, count, buckets_ref, g_ref, out_ref):
    @pl.when(pl.program_id(0) == 0)
    def _():
        out_ref[...] = jnp.zeros_like(out_ref)

    total = out_ref[...]
    for i in range(buckets_ref.shape[1] // 8):
        at = slice(i * 8, (i + 1) * 8)
        index = buckets_ref[0, at]
        hot = [jnp.where(index == b, 1.0, 0.0) for b in range(count)]
        hot = jnp.concatenate(hot, axis=0).astype(BF16)
        g = jnp.concatenate([g_ref[h, 0, at] for h in range(heads)], axis=0)
        high = g.astype(BF16)
        low = (g - high.astype(F32)).astype(BF16)
        total += dot(jnp.concatenate([high, low], axis=0), hot, 1, 1)
    out_ref[...] = total


def bucket_sums(grad_bias, buckets, count):
    heads, blocks, size, _ = grad_bias.shape
    shape = (2 * heads * 8, count * 8)
    raw = pl.pallas_call(
        functools.partial(sums_body, heads, count),
        grid=(blocks,),
        in_specs=[
            pl.BlockSpec((1, size, size), lambda s: (s, 0, 0)),
            pl.BlockSpec((heads, 1, size, size), lambda s: (0, s, 0, 0)),
        ],
        out_specs=pl.BlockSpec(shape, lambda s: (0, 0)),
        out_shape=jax.ShapeDtypeStruct(shape, F32),
        compiler_params=PARAMS,
        name="bucket_sums",
        cost_estimate=cost(64 * grad_bias.size, 4 * grad_bias.size),
    )(buckets, grad_bias)
    raw = raw.reshape(2, heads, 8, count, 8)
    return jnp.sum(jnp.where(jnp.eye(8, dtype=bool)[None, None, :, None, :], raw, 0.0), (0, 2, 4)).T


def mix_body(x_ref, o_ref, w_ref, place_ref, gain_ref, mixed_ref, pair_ref, *piece_refs):
    spread = dot(place_ref[...], o_ref[...], 0, 0).astype(BF16)
    mixed = x_ref[0].astype(F32) + dot(flat_rows(w_ref), spread, 0, 0)
    mixed_ref[...] = mixed
    scale = lax.rsqrt(jnp.mean(mixed * mixed, axis=0, keepdims=True) + NORM_EPSILON)
    n = (mixed * scale * gain_ref[...]).astype(BF16)
    pair_ref[0] = n
    put_pieces(piece_refs, n)


def group_specs(shape, count, per, rank):
    def place(g):
        def index(r):
            inside = jnp.clip(r - g * per, 0, per - 1)
            return (0, inside) if rank == 2 else (inside, 0, 0)

        return index

    return [pl.BlockSpec(shape, place(g)) for g in range(count)]


def mix(x, ot, w, place, gain):
    rows, width, size = x.shape
    inner = ot.shape[0]
    here = rows * size
    piece_specs, piece_shapes = pieces_of((width, here), size)
    return pl.pallas_call(
        mix_body,
        grid=(rows,),
        in_specs=[
            pl.BlockSpec((1, width, size), lambda r: (r, 0, 0)),
            pl.BlockSpec((inner, size), lambda r: (0, r)),
            picked(w, 1),
            whole(place.shape),
            whole(gain.shape),
        ],
        out_specs=[
            pl.BlockSpec((width, size), lambda r: (0, r)),
            pl.BlockSpec((1, width, size), lambda r: (0, 0, r)),
        ]
        + piece_specs,
        out_shape=[
            jax.ShapeDtypeStruct((width, here), F32),
            jax.ShapeDtypeStruct((2, width, here), BF16),
        ]
        + piece_shapes,
        compiler_params=PARAMS,
        name="mix",
        cost_estimate=cost(1, 1),
    )(x, ot, w, place, gain)


def units_of(ws):
    return sum(w.shape[0] * w.shape[2] for w in ws)


def entries_of(ws):
    return sum(w.shape[0] for w in ws)


def loads_of(refs, buf, sems, kinds):
    copies, start = [], 0
    for a, ref in enumerate(refs):
        for k, kind in enumerate(kinds):
            inside = buf.at[k, pl.ds(start, ref.shape[0])]
            copies.append(pltpu.make_async_copy(ref.at[:, kind], inside, sems.at[a, k]))
        start += ref.shape[0]
    return copies


def ffn_body(count, masks, me_ref, *refs):
    ws, (n_ref, dy_ref, act_ref), refs = refs[:count], refs[count : count + 3], refs[count + 3 :]
    gs, (buf, acc, in_sems, out_sems) = refs[:-4], refs[-4:]
    t = pl.program_id(0)
    entries, rows, width = buf.shape[1:]
    size = entries * rows
    loads = loads_of(ws, buf, in_sems, range(3))

    @pl.when(t == 0)
    def _():
        for copy in loads:
            copy.start()
        acc[...] = jnp.zeros_like(acc)
        for copy in loads:
            copy.wait()

    norm = n_ref[0]
    dy = dy_ref[0]
    gate = dot(buf[0].reshape(size, width), norm, 1, 0)
    up = dot(buf[1].reshape(size, width), norm, 1, 0)
    dhid = dot(buf[2].reshape(size, width), dy, 1, 0)
    inside = gate * (0.7978845608028654 + 0.035677408136300125 * (gate * gate))
    half = 0.5 + 0.5 * jnp.tanh(inside)
    gelu = gate * half
    slope = half * (1.0 + (1.0 - half) * (6.0 * inside - 3.1915382432114616 * gate))
    dgate = (dhid * up * slope).astype(BF16)
    dup = (dhid * gelu).astype(BF16)
    hidden = (gelu * up).astype(BF16)
    act_ref[0] = dgate
    act_ref[1] = dup
    act_ref[2] = hidden
    acc[0] += dot(dgate, norm, 1, 1)
    acc[1] += dot(dup, norm, 1, 1)
    acc[2] += dot(hidden, dy, 1, 1)

    @pl.when(t == pl.num_programs(0) - 1)
    def _():
        for k in range(3):
            buf[k] = acc[k].astype(BF16).reshape(entries, rows, width)
        stores = []
        if masks is None:
            start = 0
            for g, out in enumerate(gs):
                for k in range(3):
                    inside = buf.at[k, pl.ds(start, out.shape[0])]
                    stores.append(pltpu.make_async_copy(inside, out.at[:, k], out_sems.at[g, k]))
                start += out.shape[0]
        else:
            part = len(masks) // 2
            for s, mask in enumerate(masks):
                for k in range(3):
                    inside, out = buf.at[k, me_ref[0] ^ mask], gs[s // part].at[s % part, k]
                    stores.append(pltpu.make_async_copy(inside, out, out_sems.at[s, k]))
        for copy in stores:
            copy.start()
        for copy in stores:
            copy.wait()


def ffn_group(me, ws, n, dy, tile, masks=None):
    halves, width, tokens = n.shape
    per = tokens // tile
    all_tokens = halves * tokens
    size = units_of(ws)
    inner = (entries_of(ws),) + ws[0].shape[2:]
    column = pl.BlockSpec((1, width, tile), lambda t, me: (t // per, 0, t % per))
    stores = len(ws) if masks is None else len(masks)
    shapes = [w.shape for w in ws]
    if masks is not None:
        shapes = [(inner[0] // 2, 3) + inner[1:]] * 2
    spec = pltpu.PrefetchScalarGridSpec(
        num_scalar_prefetch=1,
        grid=(halves * per,),
        in_specs=[ANY] * len(ws) + [column, column],
        out_specs=[pl.BlockSpec((3, size, tile), lambda t, me: (0, 0, t))] + [ANY] * len(shapes),
        scratch_shapes=[
            pltpu.VMEM((3,) + inner, BF16),
            pltpu.VMEM((3, size, width), F32),
            pltpu.SemaphoreType.DMA((len(ws), 3)),
            pltpu.SemaphoreType.DMA((stores, 3)),
        ],
    )
    out = pl.pallas_call(
        functools.partial(ffn_body, len(ws), masks),
        grid_spec=spec,
        out_shape=[jax.ShapeDtypeStruct((3, size, all_tokens), BF16)]
        + [jax.ShapeDtypeStruct(shape, BF16) for shape in shapes],
        compiler_params=PARAMS,
        name="ffn_group",
        cost_estimate=cost(1, 1),
    )(me, *ws, n, dy)
    return out[0], out[1:]


def ffn_terms(layout, kinds, refs):
    count, total = len(layout), sum(layout)
    ws, acts, refs = refs[:total], refs[total : total + count], refs[total + count :]
    bufs, sems = refs[:count], refs[count]

    @pl.when(pl.program_id(0) == 0)
    def _():
        copies, start = [], 0
        for p, arrays in enumerate(layout):
            copies += loads_of(ws[start : start + arrays], bufs[p], sems.at[p], kinds)
            start += arrays
        for copy in copies:
            copy.start()
        for copy in copies:
            copy.wait()

    out = None
    for act, buf in zip(acts, bufs):
        _, entries, rows, width = buf.shape
        for k in range(len(kinds)):
            term = dot(buf[k].reshape(entries * rows, width), act[k], 0, 0)
            out = term if out is None else out + term
    return out


def layout_of(groups):
    return tuple(len(ws) for ws in groups)


def flat_of(groups):
    return [w for ws in groups for w in ws]


def ffn_specs(groups, acts, kinds, tile, first):
    at = kinds[0] // len(kinds)
    return [ANY] * len(flat_of(groups)) + [
        pl.BlockSpec((len(kinds), a.shape[1], tile), lambda t: (at, 0, first + t)) for a in acts
    ]


def ffn_scratch(groups, kinds):
    return [
        pltpu.VMEM((len(kinds), entries_of(ws)) + ws[0].shape[2:], BF16) for ws in groups
    ] + [pltpu.SemaphoreType.DMA((len(groups), max(layout_of(groups)), len(kinds)))]


def ffn_back_body(layout, kinds, pieces, *refs):
    ins = sum(layout) + len(layout)
    total = ffn_terms(layout, kinds, refs[:ins] + refs[ins + pieces :])
    put_pieces(refs[ins : ins + pieces], total.astype(BF16))


def ffn_back(groups, acts, kinds, start, count, tile, pieces):
    width = groups[0][0].shape[3]
    piece_specs, piece_shapes = pieces_of((width, count), tile, pieces)
    return pl.pallas_call(
        functools.partial(ffn_back_body, layout_of(groups), kinds, pieces),
        grid=(count // tile,),
        in_specs=ffn_specs(groups, acts, kinds, tile, start // tile),
        out_specs=piece_specs,
        out_shape=piece_shapes,
        scratch_shapes=ffn_scratch(groups, kinds),
        compiler_params=PARAMS,
        name="ffn_back",
        cost_estimate=cost(1, 1),
    )(*flat_of(groups), *acts)


def layer_out_body(layout, *refs):
    ins = sum(layout) + len(layout)
    mixed_ref, got_ref, out_ref = refs[ins : ins + 3]
    total = ffn_terms(layout, [2], refs[:ins] + refs[ins + 3 :])
    out_ref[0] = (mixed_ref[...] + total + got_ref[...].astype(F32)).astype(BF16)


def layer_out_of(groups, acts, mixed, got, rows):
    width, here = mixed.shape
    size = here // rows
    col = pl.BlockSpec((width, size), lambda t: (0, t))
    return pl.pallas_call(
        functools.partial(layer_out_body, layout_of(groups)),
        grid=(rows,),
        in_specs=ffn_specs(groups, acts, [2], size, 0) + [col, col],
        out_specs=pl.BlockSpec((1, width, size), lambda t: (t, 0, 0)),
        out_shape=jax.ShapeDtypeStruct((rows, width, size), BF16),
        scratch_shapes=ffn_scratch(groups, [2]),
        compiler_params=PARAMS,
        name="layer_out_of",
        cost_estimate=cost(1, 1),
    )(*flat_of(groups), *acts, mixed, got)


def mix_back_body(layout, *refs):
    ins = sum(layout) + len(layout)
    weights, refs = refs[:ins], refs[ins:]
    pieces, refs = refs[:PIECES], refs[PIECES:]
    mixed_ref, dy_ref, o_ref, w_ref, place_ref, home_ref, gain_ref = refs[:7]
    refs = refs[7:]
    inside_grad = len(refs) == 5 + len(layout) + 1
    dmixed_ref, do_ref, gg_ref = refs[:3]
    gw_ref, acc = refs[3:5] if inside_grad else (None, None)
    row = pl.program_id(0)
    got = jnp.concatenate([r[...] for r in pieces], axis=0)
    dn = ffn_terms(layout, [0, 1], weights + refs[-len(layout) - 1 :]) + got.astype(F32)
    mixed = mixed_ref[...]
    scale = lax.rsqrt(jnp.mean(mixed * mixed, axis=0, keepdims=True) + NORM_EPSILON)
    unit = mixed * scale
    scaled = dn * gain_ref[...]
    inside = jnp.mean(scaled * unit, axis=0, keepdims=True)
    dmixed = dy_ref[0].astype(F32) + scale * (scaled - unit * inside)
    dmixed_ref[...] = dmixed
    low = dmixed.astype(BF16)
    spread = dot(home_ref[...], o_ref[...], 0, 0).astype(BF16)
    mixed_up = dot(flat_rows(w_ref), low, 1, 0).astype(BF16)
    do_ref[...] = dot(place_ref[...], mixed_up, 1, 0).astype(BF16)
    both = dn * unit
    gain_part = both[:, :128]
    for j in range(1, both.shape[1] // 128):
        gain_part = gain_part + both[:, j * 128 : (j + 1) * 128]

    @pl.when(row == 0)
    def _():
        gg_ref[...] = gain_part

    @pl.when(row > 0)
    def _():
        gg_ref[...] += gain_part

    if inside_grad:
        product = dot(spread, low, 1, 1)

        @pl.when(row == 0)
        def _():
            acc[...] = product

        @pl.when(row > 0)
        def _():
            acc[...] += product

        @pl.when(row == pl.num_programs(0) - 1)
        def _():
            gw_ref[...] = acc[...].astype(BF16)


def mix_back(groups, acts, mixed, d1, dy, ot, w, place, home, gain):
    rows, width, size = dy.shape
    inner = ot.shape[0]
    here = rows * size
    col = pl.BlockSpec((width, size), lambda r: (0, r))
    head_col = pl.BlockSpec((inner, size), lambda r: (0, r))
    grad = (home.shape[1], width)
    fits = grad[0] <= 1024
    out = pl.pallas_call(
        functools.partial(mix_back_body, layout_of(groups)),
        grid=(rows,),
        in_specs=ffn_specs(groups, acts, [0, 1], size, 0)
        + pieces_of(mixed.shape, size)[0]
        + [col, pl.BlockSpec((1, width, size), lambda r: (r, 0, 0)), head_col]
        + [picked(w, 1), whole(place.shape), whole(home.shape), whole(gain.shape)],
        out_specs=[col, head_col, whole((width, 128))] + [whole(grad)] * fits,
        out_shape=[
            jax.ShapeDtypeStruct((width, here), F32),
            jax.ShapeDtypeStruct((inner, here), BF16),
            jax.ShapeDtypeStruct((width, 128), F32),
        ]
        + [jax.ShapeDtypeStruct(grad, BF16)] * fits,
        scratch_shapes=[pltpu.VMEM(grad, F32)] * fits + ffn_scratch(groups, [0, 1]),
        compiler_params=PARAMS,
        name="mix_back",
        cost_estimate=cost(1, 1),
    )(*flat_of(groups), *acts, *d1, mixed, dy, ot, w, place, home, gain)
    if not fits:
        spread = dot(home, ot, 0, 0).astype(BF16)
        out = [*out, dot(spread, out[0].astype(BF16), 1, 1).astype(BF16)]
    return out


def grads_body(per, groups, parts, n_ref, *refs):
    d_refs, refs = refs[:groups], refs[groups:]
    places, refs = refs[: len(parts)], refs[len(parts) :]
    outs, (acc, d_scr) = refs[: 2 * len(parts)], refs[2 * len(parts) :]
    row = pl.program_id(0)
    n = n_ref[...]
    for g, d_ref in enumerate(d_refs):

        @pl.when(row // per == g)
        def _():
            d_scr[...] = d_ref[...].reshape(d_scr.shape)

    products = []
    for (start, stop), p_ref in zip(parts, places):
        spread = dot(p_ref[...], d_scr[start:stop], 0, 0).astype(BF16)
        products.append(dot(spread, n, 1, 1))

    @pl.when(row == 0)
    def _():
        for j, product in enumerate(products):
            acc[j] = product

    @pl.when(row > 0)
    def _():
        for j, product in enumerate(products):
            acc[j] += product

    @pl.when(row == pl.num_programs(0) - 1)
    def _():
        half = acc.shape[1] // 2
        for j in range(len(parts)):
            outs[2 * j][...] = acc[j, :half].astype(BF16)
            outs[2 * j + 1][...] = acc[j, half:].astype(BF16)


def projection_grads(n, groups, parts, places, rows):
    if len(parts) > 1 and places[0].shape[1] > 1024:
        return [
            half
            for part, p in zip(parts, places)
            for half in projection_grads(n, groups, [part], [p], rows)
        ]
    width, here = n.shape
    size = here // rows
    per = rows // len(groups)
    rank = groups[0].ndim
    depth = groups[0].shape[-2]
    shape = (depth, size) if rank == 2 else (1, depth, size)
    wide = (places[0].shape[1], width)
    return pl.pallas_call(
        functools.partial(grads_body, per, len(groups), parts),
        grid=(rows,),
        in_specs=[pl.BlockSpec((width, size), lambda r: (0, r))]
        + group_specs(shape, len(groups), per, rank)
        + [whole(p.shape) for p in places],
        out_specs=[whole((wide[0] // 2, width))] * (2 * len(parts)),
        out_shape=[jax.ShapeDtypeStruct((wide[0] // 2, width), BF16)] * (2 * len(parts)),
        scratch_shapes=[pltpu.VMEM((len(parts),) + wide, F32), pltpu.VMEM((depth, size), BF16)],
        compiler_params=PARAMS,
        name="projection_grads",
        cost_estimate=cost(
            2 * len(parts) * wide[0] * width * here, 2 * n.size + 2 * len(parts) * wide[0] * width
        ),
    )(n, *groups, *places)


def last_body(per, groups, x_ref, dm_ref, *refs):
    dq_refs, dkv_refs, refs = refs[:groups], refs[groups : 2 * groups], refs[2 * groups :]
    ws, places, refs = refs[:3], refs[3:6], refs[6:]
    gain_ref, gx_ref, gg_ref, d_scr = refs
    row = pl.program_id(0)
    inner = dq_refs[0].shape[0]
    for g in range(groups):

        @pl.when(row // per == g)
        def _():
            d_scr[:inner] = dq_refs[g][...]
            d_scr[inner:] = dkv_refs[g][0, : 2 * inner]

    dn = None
    for j in range(3):
        spread = dot(places[j][...], d_scr[j * inner : (j + 1) * inner], 0, 0).astype(BF16)
        term = dot(flat_rows(ws[j]), spread, 0, 0)
        dn = term if dn is None else dn + term
    x = x_ref[0].astype(F32)
    scale = lax.rsqrt(jnp.mean(x * x, axis=0, keepdims=True) + NORM_EPSILON)
    unit = x * scale
    scaled = dn * gain_ref[...]
    inside = jnp.mean(scaled * unit, axis=0, keepdims=True)
    gx_ref[0] = dm_ref[...] + scale * (scaled - unit * inside)
    both = dn * unit
    gain_part = both[:, :128]
    for j in range(1, both.shape[1] // 128):
        gain_part = gain_part + both[:, j * 128 : (j + 1) * 128]

    @pl.when(row == 0)
    def _():
        gg_ref[...] = gain_part

    @pl.when(row > 0)
    def _():
        gg_ref[...] += gain_part


def last(x, dmixed, dqs, dkvs, ws, places, gain):
    rows, width, size = x.shape
    inner = dqs[0].shape[0]
    per = rows // len(dqs)
    col = pl.BlockSpec((width, size), lambda r: (0, r))
    block = pl.BlockSpec((1, width, size), lambda r: (r, 0, 0))
    return pl.pallas_call(
        functools.partial(last_body, per, len(dqs)),
        grid=(rows,),
        in_specs=[block, col]
        + group_specs((inner, size), len(dqs), per, 2)
        + group_specs((1,) + dkvs[0].shape[1:], len(dkvs), per, 3)
        + [picked(w, index) for w, index in zip(ws, (1, 0, 0))]
        + [whole(p.shape) for p in places]
        + [whole(gain.shape)],
        out_specs=[block, whole((width, 128))],
        out_shape=[jax.ShapeDtypeStruct(x.shape, F32), jax.ShapeDtypeStruct((width, 128), F32)],
        scratch_shapes=[pltpu.VMEM((3 * inner, size), BF16)],
        compiler_params=PARAMS,
        name="last",
        cost_estimate=cost(6 * ws[0].size * rows * size, 14 * x.size + 6 * ws[0].size),
    )(x, dmixed, *dqs, *dkvs, *ws, *places, gain)


def after(value, *markers):
    return lax.optimization_barrier((value, markers))[0]


def pad_rows(w, rows):
    return jnp.pad(w, ((0, rows - w.shape[0]), (0, 0))) if rows > w.shape[0] else w


class Links:
    def __init__(self, dp, pairs):
        self.sizes = {"dp": dp, "x": pairs, "core": 2}
        self.strides = {"dp": 2 * pairs, "x": 2, "core": 1}
        self.core = ("core", 1)
        self.across = ("x", 1)
        self.near = ("dp", 1)
        self.far_count = dp // 2

    def swap(self, x, step):
        axis, mask = step
        return lax.ppermute(x, axis, [(i, i ^ mask) for i in range(self.sizes[axis])])

    def far_steps(self):
        return [("dp", k << 1) for k in range(1, self.far_count)]

    def far_bits(self):
        return [("dp", 2 << b) for b in range(self.far_count.bit_length() - 1)]

    def masks(self, steps):
        found = [(k << 1) * self.strides["dp"] for k in range(self.far_count)]
        for axis, mask in steps:
            found = found + [f ^ (mask * self.strides[axis]) for f in found]
        return found


def per_device(
    dp, ctx,
    tokens, soft_mask, segment_ids, buckets, gain_attn, gain_ffn, bias_table,
    w_query, w_key, w_value, w_attn_out, w_gate, w_up, w_ffn_out, cotangent,
):
    links = Links(dp, ctx // 2)
    swap, core, across, near = links.swap, links.core, links.across, links.near
    far = links.far_steps()
    rows, size, width = tokens.shape
    here = rows * size
    count, heads = bias_table.shape
    inner = heads * HEAD
    my_dp, my_ctx = lax.axis_index("dp"), lax.axis_index("x") * 2 + lax.axis_index("core")
    me = my_dp * ctx + my_ctx
    tile = min(512, here)
    order_a, order_b = [near, across], [across, near]

    def spread_of(steps):
        real = w_query.shape[0]
        owners = me ^ jnp.asarray(links.masks(steps), dtype=jnp.int32)
        inside = jnp.arange(each)
        feature = owners[:, None] * real + inside[None, :]
        feature = jnp.where(inside[None, :] < real, feature, -1).reshape(-1)
        return (jnp.arange(inner)[:, None] == feature[None, :]).astype(BF16)

    token = []

    def run(work, *args):
        if token:
            args = lax.optimization_barrier((args, tuple(token)))[0]
        out = work(*args)
        token[:] = jax.tree.leaves(out)
        return out

    each = -(-w_query.shape[0] // ROW_TILE) * ROW_TILE
    slot = lambda w: pad_rows(w, each)[None]
    flat = lambda w: w.reshape(-1, width)
    far_bits = links.far_bits()
    ab, ba = (near, across), (across, near)

    def exchange(arrays, steps):
        return [(a, swap(a, step)) for a, step in zip(arrays, steps)]

    def swap_core(value):
        return [swap(v, core) for v in value]

    def close(value):
        return run(lambda v: v, value)

    class Gather:
        def __init__(self, array, cuts, direct=False, mark=None, paths=(ab, ba)):
            if mark is not None:
                array = after(array, mark)
            self.cuts, self.stage, self.paths = cuts, 0, paths
            self.hops = 1 if direct else len(far_bits)
            steps = far if direct else far_bits[:1]
            self.held = [array] + [swap(array, step) for step in steps]

        def go(self):
            self.stage += 1
            if self.stage < self.hops:
                (array,) = run(lambda *p: join([p]), *self.held)
                self.held = [array, swap(array, far_bits[self.stage])]
            elif self.stage == self.hops:
                parts = run(lambda *p: cut_join(list(p), self.cuts), *self.held)
                self.held = exchange(parts, self.paths[0])
            elif self.stage == self.hops + 1:
                self.held = exchange(run(join, self.held), self.paths[1])

        def start_of(self):
            first = self.held[0]
            return first[0] if isinstance(first, tuple) else first

        def core_go(self):
            self.held = exchange(run(join, self.held), (core, core))

        def core_end(self):
            return run(join, self.held)

    attn_w = Gather(
        jnp.concatenate([slot(w) for w in (w_key, w_attn_out, w_value, w_query)], axis=1)[:, None],
        [(0, 2 * each), (2 * each, 2 * each)],
        direct=True,
    )
    units = -(-w_gate.shape[0] // ROW_TILE)
    ffn_own = after((w_gate, w_up, w_ffn_out), attn_w.held[0])
    padded = [pad_rows(w, units * ROW_TILE) for w in ffn_own]
    marks = [0, 3, 5, 7] if units == 7 else list(range(units + 1))
    shards = [
        jnp.stack([w[low * ROW_TILE : high * ROW_TILE] for w in padded])
        for low, high in zip(marks, marks[1:])
    ]
    same_core = ("dp", "x")
    by_hops = units == 7
    last_group = len(shards) - 1

    x = jnp.transpose(tokens, (0, 2, 1))
    dy = jnp.transpose(cotangent, (0, 2, 1))
    gain_one, gain_two = gain_attn[:, None], gain_ffn[:, None]
    place_a, place_b = spread_of(order_a + [core]), spread_of(order_b + [core])
    real = w_query.shape[0]
    segs = lax.dynamic_slice_in_dim(segment_ids, my_ctx * size, size, 1)
    same = segs[:, None, :] == jnp.arange(DOCS, dtype=segs.dtype)[None, :, None]
    ones = jnp.ones((rows, 1, size), BF16)
    rest = AUG - 1 - DOCS
    aug = jnp.concatenate(
        [soft_mask[:, None, :], same.astype(BF16)] + [ones] * 3
        + [jnp.zeros((rows, rest - 3, size), BF16)],
        axis=1,
    )
    query_aug = jnp.concatenate(
        [ones, jnp.where(same, 0.0, MASK_VALUE).astype(BF16), jnp.zeros((rows, rest, size), BF16)],
        axis=1,
    )
    normed, dy_pair, *dy_own = run(first_norm, x, dy, gain_one)
    place_a, place_b, aug, query_aug, shards = close((place_a, place_b, aug, query_aug, shards))

    attn_w.go()
    ffn_w = [
        [lax.all_gather(after(shard, attn_w.start_of()), same_core)]
        for shard in (shards[:-1] if by_hops else shards)
    ]
    slots = jnp.array([0, 2, 1, 3], jnp.int32) ^ my_ctx
    bias, buckets_t = run(
        bias_of, slots, buckets, jnp.pad(bias_table.T, ((0, 0), (0, 128 - count)))
    )
    dy_parts = swap_core(dy_own)
    attn_w.go()
    if by_hops:
        last_w = Gather(
            shards[-1][None],
            [(0, shards[-1].shape[1])],
            mark=attn_w.start_of(),
            paths=((near,), (across,)),
        )
    dy_pair = run(fill, dy_pair, dy_parts)
    if by_hops:
        last_w.go()
    attn_w.core_go()
    wko, wvq = attn_w.core_end()
    kv_own = run(lambda *a: key_value(*a, 0, rows), normed, wko, wvq, place_a, place_b, aug)
    kv_across = swap(kv_own, across)
    kv_core = swap(kv_own, core)
    queries = run(lambda n, w, p: project(n, w, p, tile), normed, wvq, place_b)
    kv_core = close(kv_core)
    if by_hops:
        last_w.go()

    kv = run(lambda *k: list(k), kv_own, kv_across, kv_core)
    kv.append(close(jnp.concatenate([swap(k, core) for k in jnp.split(kv[1], min(2, rows))])))
    attended, lse = run(lambda *a: attend(*a, heads, 0), queries, query_aug, kv, bias)
    if by_hops:
        last_w.go()
    mixed, n_pair, *normed_two = run(mix, x, attended, wko, place_a, gain_two)
    n_parts = close(swap_core(normed_two))
    n_pair = run(fill, n_pair, n_parts)

    class Sums:
        def __init__(self, grads, paths, direct=False):
            self.paths, self.direct = paths[: len(grads)], direct
            self.stage = 0
            self.send(grads)

        def send(self, halves):
            self.keep = [h[0] for h in halves]
            self.got = [swap(h[1], p[self.stage]) for h, p in zip(halves, self.paths)]

        def go(self):
            near_hops = len(self.paths[0])
            hops = near_hops + (1 if self.direct else len(far_bits))
            self.stage += 1
            if self.stage > hops:
                return
            if self.stage < near_hops:
                self.send(run(add_halves, self.keep, self.got))
                return
            if self.stage == near_hops:
                rows_of = [k.shape[-2] for k in self.keep]
                self.edges = [sum(rows_of[:k]) for k in range(len(rows_of) + 1)]
                if self.direct:
                    piles = run(lambda k, r: add_piles(k, r, self.edges), self.keep, self.got)
                    self.keep = [piles[0]]
                    self.got = [swap(pile, step) for pile, step in zip(piles[1:], far)]
                    return
                halves = run(lambda k, r: add_merge(k, r, self.edges), self.keep, self.got)
            elif self.stage < hops:
                halves = run(add_halves, self.keep, self.got)[0]
            else:
                got = after(self.got, *token)
                self.out = add_last(self.keep[0], got, self.edges)
                return
            self.keep = [halves[0]]
            self.got = [swap(halves[1], far_bits[hops - 1 - self.stage])]

    acts, sums = [], []
    me_same = (my_dp * (ctx // 2) + lax.axis_index("x")).reshape(1)
    masks = [[m >> 1 for m in links.masks(steps)] for steps in (ab, ba)]
    ffn_grads = []
    if by_hops:
        ffn_w.append(None)
    for i, ws in enumerate(ffn_w):
        if i == last_group and by_hops:
            ws = ffn_w[i] = last_ws
        some = tile if units_of(ws) <= 768 else tile // 2
        mask = masks[1] if by_hops and i == last_group - 1 else None
        act, grads = run(
            lambda m, w, n, d: ffn_group(m, w, n, d, some, mask), me_same, ws, n_pair, dy_pair
        )
        acts.append(act)
        if by_hops and i == 0:
            last_ws = close(list(last_w.held[0]))
            grads = [after(g, last_ws) for g in grads]
        if by_hops and i >= last_group - 1:
            ffn_grads.append(grads)
        else:
            ffn_grads.append(lax.psum_scatter(grads[0], same_core))
    if by_hops:
        sums = [Sums(ffn_grads[-2:], [ab, ba])]

    def tick():
        for s in sums:
            s.go()

    back = run(lambda p, a: ffn_back(p, a, [0, 1], here, here, tile, PIECES), ffn_w, acts)
    dn_got = swap_core(back)
    (out_other,) = run(lambda p, a: ffn_back(p, a, [2], here, here, tile, 1), ffn_w, acts)
    dn_got = close(dn_got)
    out_got = swap(out_other, core)

    dmixed, dattended, gain_two_part, gwo = run(
        mix_back, ffn_w, acts, mixed, dn_got, dy, attended, wko, place_a, place_b, gain_two
    )
    tick()
    out_got = close(out_got)
    dq, dkv, grad_bias = run(
        lambda *a: attend_back(*a, heads, 0, []),
        queries, query_aug, kv, bias, attended, dattended, lse,
    )
    by_core = [(dkv[0], swap(dkv[2], core)), (dkv[1], swap(dkv[3], core))]
    tick()
    if by_hops:
        ffn_grads[0] = close(ffn_grads[0])
    entries = lambda g: tuple(v.reshape(-1, each, width) for v in g)
    home_a, home_b = (core,) + ba, (core,) + ab
    gwq = run(
        lambda n, d, p: projection_grads(n, [d], [(0, inner)], [p], rows), normed, dq, place_b
    )
    own, other = run(add_pairs, by_core)
    other = swap(other, across)
    part = gwo.shape[0] // 2
    query_sum = Sums([entries((gwo[:part], gwo[part:])), entries(gwq)], [home_b, home_b])
    grad_table = run(lambda g, b: bucket_sums(g, b, count), grad_bias, buckets_t)
    query_sum.go()
    out = run(lambda *a: layer_out_of(*a, rows), ffn_w, acts, mixed, out_got)
    query_sum.go()
    (dkv,) = run(add_pairs, [(own, other)])
    gkv = run(
        lambda n, d, pa, pb: projection_grads(n, [d], [(0, inner), (inner, 2 * inner)], [pa, pb], rows),
        normed, dkv, place_a, place_b,
    )
    value_sum = Sums([entries(gkv[:2]), entries(gkv[2:])], [home_a, home_b], direct=dp <= 8)
    tick()
    query_sum.go()
    value_sum.go()
    gx, gain_one_part = run(
        lambda *a: last(a[0], a[1], [a[2]], [a[3]], a[4:7], a[7:10], a[10]),
        x, dmixed, dq, dkv, wvq, wko, wvq, place_b, place_a, place_b, gain_one,
    )
    value_sum.go()
    tick()
    query_sum.go()
    small = jnp.concatenate(
        [jnp.sum(gain_one_part, 1), jnp.sum(gain_two_part, 1), grad_table.reshape(-1)]
    )
    length = small.shape[0]
    small = jnp.pad(small, (0, -length % 1024)).reshape(-1, 128)
    bits = [core, across] + [("dp", 1 << b) for b in range(dp.bit_length() - 1)]
    for k, one in enumerate(bits):
        got = swap(small, one)
        if k == 1:
            value_sum.go()
        if k == 3:
            value_sum.got = close(value_sum.got)
        small = run(lambda a, b: a + b, small, got)
    for _ in range(len(far_bits) + 4):
        for s in [query_sum, value_sum] + sums:
            s.go()
    small = small.reshape(-1)
    if by_hops:
        ffn_grads[-2:] = sums[0].out
    grad_gate, grad_up, grad_ffn_out = (
        jnp.concatenate([g[j].astype(F32) for g in ffn_grads])[: w_gate.shape[0]] for j in range(3)
    )
    return (
        jnp.transpose(out, (0, 2, 1)),
        jnp.transpose(gx, (0, 2, 1)),
        dkv[:, 2 * inner].astype(F32),
        small[:width],
        small[width : 2 * width],
        small[2 * width : length].reshape(count, heads),
        query_sum.out[1][:real],
        value_sum.out[0][:real],
        value_sum.out[1][:real],
        query_sum.out[0][:real],
        grad_gate,
        grad_up,
        grad_ffn_out,
    )


def solution(mesh):
    dp, ctx = mesh.shape["dp"], mesh.shape["ctx"]
    by_core = Mesh(mesh.devices.reshape(dp, ctx // 2, 2), ("dp", "x", "core"))
    ctx_axes = ("x", "core")
    split = P(("dp", "x", "core"), None)
    act = P("dp", ctx_axes, None)
    in_specs = (
        (act, P("dp", ctx_axes), P("dp", None), P(ctx_axes, None), P(), P(), P()) + (split,) * 7 + (act,)
    )
    out_specs = (act, act, P("dp", ctx_axes), P(), P(), P()) + (split,) * 7
    return jax.shard_map(
        functools.partial(per_device, dp, ctx),
        mesh=by_core,
        in_specs=in_specs,
        out_specs=out_specs,
        check_vma=False,
    )
```

```python
import functools

import jax
import jax.numpy as jnp
import numpy as np
from jax import lax
from jax.experimental import pallas as pl
from jax.experimental.pallas import tpu as pltpu
from jax.sharding import Mesh, PartitionSpec as P

NORM_EPSILON = 1e-06
MASK_VALUE = -1e30
F32, BF16 = jnp.float32, jnp.bfloat16
HEAD = 64
ROW_TILE = 16
AUG = 16
DOCS = 5
ONES = 1 + DOCS
VMEM_LIMIT = 58 * 1024 * 1024
PARAMS = pltpu.CompilerParams(vmem_limit_bytes=VMEM_LIMIT)


def dot(a, b, ca, cb):
    return lax.dot_general(a, b, (((ca,), (cb,)), ((), ())), preferred_element_type=F32)


def whole(shape):
    return pl.BlockSpec(shape, lambda t: (0,) * len(shape), pipeline_mode=pl.Buffered(1))


def cost(flops, nbytes):
    return pl.CostEstimate(flops=1, bytes_accessed=1, transcendentals=0)


ANY = pl.BlockSpec(memory_space=pl.ANY)


def join(pairs):
    return [jnp.concatenate(list(pair), axis=0) for pair in pairs]


def cut_join(parts, cuts):
    out = []
    for cut in cuts:
        at = np.s_[:, :, cut[0] : cut[0] + cut[1]] if isinstance(cut, tuple) else np.s_[:, cut]
        out.append(jnp.concatenate([p[at] for p in parts], axis=0))
    return out


def fill(pair, parts):
    start = 0
    for part in parts:
        pair = pair.at[1, start : start + part.shape[0]].set(part)
        start += part.shape[0]
    return pair


def add_halves(keep, got):
    out = []
    for k, r in zip(keep, got):
        part = k.shape[0] // 2
        out.append((k[:part] + r[:part], k[part:] + r[part:]))
    return out


def add_merge(keep, got, edges):
    part = keep[0].shape[0] // 2
    ends = [slice(None, part), slice(part, None)]
    return [jnp.concatenate([k[e] + r[e] for k, r in zip(keep, got)], axis=-2) for e in ends]


def add_piles(keep, got, edges):
    return [
        jnp.concatenate([k[i : i + 1] + r[i : i + 1] for k, r in zip(keep, got)], axis=-2)
        for i in range(keep[0].shape[0])
    ]


def add_last(keep, got, edges):
    total = keep[0].astype(F32)
    for r in got:
        total = total + r[0].astype(F32)
    return [total[..., a:b, :] for a, b in zip(edges, edges[1:])]


def add_pairs(pairs):
    return [a + b for a, b in pairs]


PIECES = 2


def pieces_of(shape, tile, pieces=PIECES):
    rows, columns = shape
    piece = (rows // pieces, columns)
    specs = [pl.BlockSpec((piece[0], tile), lambda t: (0, t)) for _ in range(pieces)]
    return specs, [jax.ShapeDtypeStruct(piece, BF16)] * pieces


def put_pieces(refs, value):
    step = refs[0].shape[0]
    for k, ref in enumerate(refs):
        ref[...] = value[k * step : (k + 1) * step]


def norm_body(x_ref, dy_ref, gain_ref, n_ref, pair_ref, *piece_refs):
    x = x_ref[0].astype(F32)
    scale = lax.rsqrt(jnp.mean(x * x, axis=0, keepdims=True) + NORM_EPSILON)
    n_ref[...] = (x * scale * gain_ref[...]).astype(BF16)
    pair_ref[0] = dy_ref[0]
    put_pieces(piece_refs, dy_ref[0])


def first_norm(x, dy, gain):
    rows, width, size = x.shape
    block = pl.BlockSpec((1, width, size), lambda r: (r, 0, 0))
    col = pl.BlockSpec((width, size), lambda r: (0, r))
    here = rows * size
    piece_specs, piece_shapes = pieces_of((width, here), size)
    return pl.pallas_call(
        norm_body,
        grid=(rows,),
        in_specs=[block, block, whole(gain.shape)],
        out_specs=[col, pl.BlockSpec((1, width, size), lambda r: (0, 0, r))] + piece_specs,
        out_shape=[
            jax.ShapeDtypeStruct((width, here), BF16),
            jax.ShapeDtypeStruct((2, width, here), BF16),
        ]
        + piece_shapes,
        compiler_params=PARAMS,
        name="first_norm",
        cost_estimate=cost(4 * x.size, 10 * x.size),
    )(x, dy, gain)


def picked(pair, index):
    return [
        pl.BlockSpec(
            (w.shape[0], 1, w.shape[2] // 2, w.shape[3]),
            lambda t: (0, 0, index, 0),
            pipeline_mode=pl.Buffered(1),
        )
        for w in pair
    ]


def flat_rows(w_ref):
    entries, _, each, width = w_ref.shape
    return w_ref[...].reshape(entries * each, width)


def forth(refs, x):
    return jnp.concatenate([dot(flat_rows(w), x, 1, 0).astype(BF16) for w in refs], axis=0)


def back(refs, x):
    part = x.shape[0] // 2
    return dot(flat_rows(refs[0]), x[:part], 0, 0) + dot(flat_rows(refs[1]), x[part:], 0, 0)


def key_value_body(inner, n_ref, wk0, wk1, wv0, wv1, pk_ref, pv_ref, aug_ref, out_ref):
    n = n_ref[...]
    for start, refs, p_ref in ((0, (wk0, wk1), pk_ref), (inner, (wv0, wv1), pv_ref)):
        out_ref[0, start : start + inner] = dot(p_ref[...], forth(refs, n), 1, 0).astype(BF16)
    out_ref[0, 2 * inner :] = aug_ref[0]


def key_value(n, wk, wv, place_k, place_v, aug, first, rows):
    size = aug.shape[2]
    inner = place_k.shape[0]
    width = n.shape[0]
    return pl.pallas_call(
        functools.partial(key_value_body, inner),
        grid=(rows,),
        in_specs=[pl.BlockSpec((width, size), lambda r: (0, first + r))]
        + picked(wk, 0)
        + picked(wv, 0)
        + [
            whole(place_k.shape),
            whole(place_v.shape),
            pl.BlockSpec((1, AUG, size), lambda r: (first + r, 0, 0)),
        ],
        out_specs=pl.BlockSpec((1, 2 * inner + AUG, size), lambda r: (r, 0, 0)),
        out_shape=jax.ShapeDtypeStruct((rows, 2 * inner + AUG, size), BF16),
        compiler_params=PARAMS,
        name="key_value",
        cost_estimate=cost(1, 1),
    )(n, *wk, *wv, place_k, place_v, aug)


def project_body(n_ref, w0, w1, p_ref, out_ref):
    out_ref[...] = dot(p_ref[...], forth((w0, w1), n_ref[...]), 1, 0).astype(BF16)


def project(n, w, place, tile):
    width, here = n.shape
    inner = place.shape[0]
    return pl.pallas_call(
        project_body,
        grid=(here // tile,),
        in_specs=[pl.BlockSpec((width, tile), lambda t: (0, t))] + picked(w, 1) + [whole(place.shape)],
        out_specs=pl.BlockSpec((inner, tile), lambda t: (0, t)),
        out_shape=jax.ShapeDtypeStruct((inner, here), BF16),
        compiler_params=PARAMS,
        name="project",
        cost_estimate=cost(1, 1),
    )(n, *w, place)


def attend_body(heads, inner, q_ref, u_ref, *refs):
    *blocks, bias_ref, o_ref, lse_ref, s_ref = refs
    for h in range(heads):
        part = slice(h * HEAD, (h + 1) * HEAD)
        q = jnp.concatenate([q_ref[part], u_ref[0]], axis=0)
        top = None
        for s, k_ref in enumerate(blocks):
            k = jnp.concatenate([k_ref[0, part], k_ref[0, 2 * inner :]], axis=0)
            logits = dot(k, q, 0, 0) + bias_ref[h, s]
            s_ref[s] = logits
            peak = jnp.max(logits, axis=0, keepdims=True)
            top = peak if top is None else jnp.maximum(top, peak)
        total, out = None, None
        for s, k_ref in enumerate(blocks):
            e = jnp.exp(s_ref[s] - top)
            part_sum = jnp.sum(e, axis=0, keepdims=True)
            total = part_sum if total is None else total + part_sum
            value = k_ref[0, slice(inner + h * HEAD, inner + (h + 1) * HEAD)]
            term = dot(value, e.astype(BF16), 1, 0)
            out = term if out is None else out + term
        o_ref[part] = (out / total).astype(BF16)
        lse_ref[0, h : h + 1] = top + jnp.log(total)
    pad = lse_ref.shape[1] - heads
    if pad:
        lse_ref[0, heads:] = jnp.zeros((pad, lse_ref.shape[2]), F32)


def attend(qt, u, kv, bias, heads, first):
    rows, depth, size = kv[0].shape
    inner = heads * HEAD
    pad = -(-heads // 8) * 8
    return pl.pallas_call(
        functools.partial(attend_body, heads, inner),
        grid=(rows,),
        in_specs=[
            pl.BlockSpec((inner, size), lambda r: (0, first + r)),
            pl.BlockSpec((1, AUG, size), lambda r: (first + r, 0, 0)),
        ]
        + [pl.BlockSpec((1, depth, size), lambda r: (r, 0, 0))] * len(kv)
        + [whole(bias.shape)],
        out_specs=[
            pl.BlockSpec((inner, size), lambda r: (0, r)),
            pl.BlockSpec((1, pad, size), lambda r: (r, 0, 0)),
        ],
        out_shape=[
            jax.ShapeDtypeStruct((inner, rows * size), BF16),
            jax.ShapeDtypeStruct((rows, pad, size), F32),
        ],
        scratch_shapes=[pltpu.VMEM((len(kv), size, size), F32)],
        compiler_params=PARAMS,
        name="attend",
        cost_estimate=cost(16 * rows * heads * len(kv) * size * size * HEAD, 40_000_000),
    )(qt, u, *kv, bias)


def three(x):
    a = x.astype(BF16).astype(F32)
    rest = x - a
    b = rest.astype(BF16).astype(F32)
    return a, b, rest - b


def attend_back_body(heads, inner, count, more, q_ref, u_ref, *refs):
    blocks = refs[:count]
    bias_ref, o_ref, do_ref, lse_ref = refs[count : count + 4]
    refs = refs[count + 4 :]
    before_ref, refs = (refs[0], refs[1:]) if more else (None, refs)
    dq_ref = refs[0]
    grads = refs[1 : count + 1]
    gb_ref = refs[count + 1]
    size = bias_ref.shape[3]
    row = pl.program_id(0)
    mask_grad = [None] * count
    extra = u_ref[0].astype(F32)
    place = lax.broadcasted_iota(jnp.int32, (AUG, size), 0)

    def pick(parts, base):
        for i, value in enumerate(parts):
            base = jnp.where(place == ONES + i, value, base)
        return base.astype(BF16)

    for h in range(heads):
        part = slice(h * HEAD, (h + 1) * HEAD)
        vpart = slice(inner + h * HEAD, inner + (h + 1) * HEAD)
        q = q_ref[part]
        do = do_ref[part]
        delta = jnp.sum(do.astype(F32) * o_ref[part].astype(F32), axis=0, keepdims=True)
        q_aug = jnp.concatenate([q, pick(three(-lse_ref[0, h : h + 1]), extra)], axis=0)
        do_aug = jnp.concatenate([do, pick(three(-delta), jnp.zeros_like(extra))], axis=0)
        dq = None
        for s, k_ref in enumerate(blocks):
            k = k_ref[0, part]
            aug = k_ref[0, 2 * inner :]
            logits = dot(jnp.concatenate([k, aug], axis=0), q_aug, 0, 0) + bias_ref[h, s]
            p = jnp.exp(logits)
            dp = dot(jnp.concatenate([k_ref[0, vpart], aug], axis=0), do_aug, 0, 0)
            ds = p * dp

            @pl.when(row == 0)
            def _():
                gb_ref[h, s] = before_ref[h, s] + ds if more else ds

            @pl.when(row > 0)
            def _():
                gb_ref[h, s] += ds

            low = ds.astype(BF16)
            grads[s][0, vpart] = dot(do, p.astype(BF16), 1, 1).astype(BF16)
            both = dot(q_aug, low, 1, 1)
            grads[s][0, part] = both[:HEAD].astype(BF16)
            g = both[HEAD : HEAD + 1]
            mask_grad[s] = g if mask_grad[s] is None else mask_grad[s] + g
            term = dot(k, low, 1, 0)
            dq = term if dq is None else dq + term
        dq_ref[part] = dq.astype(BF16)
    for s in range(count):
        grads[s][0, 2 * inner :] = jnp.broadcast_to(mask_grad[s], (AUG, size)).astype(BF16)


def attend_back(qt, u, kv, bias, ot, dot_t, lse, heads, first, before):
    rows, depth, size = kv[0].shape
    inner = heads * HEAD
    count = len(kv)
    own = pl.BlockSpec((inner, size), lambda r: (0, r))
    col = pl.BlockSpec((inner, size), lambda r: (0, first + r))
    block = pl.BlockSpec((1, depth, size), lambda r: (r, 0, 0))
    out = pl.pallas_call(
        functools.partial(attend_back_body, heads, inner, count, len(before)),
        grid=(rows,),
        in_specs=[col, pl.BlockSpec((1, AUG, size), lambda r: (first + r, 0, 0))]
        + [block] * count
        + [whole(bias.shape), own, col]
        + [pl.BlockSpec((1,) + lse.shape[1:], lambda r: (r, 0, 0))]
        + [whole(b.shape) for b in before],
        out_specs=[own] + [block] * count + [whole(bias.shape)],
        out_shape=[jax.ShapeDtypeStruct((inner, rows * size), BF16)]
        + [jax.ShapeDtypeStruct((rows, depth, size), BF16)] * count
        + [jax.ShapeDtypeStruct(bias.shape, F32)],
        compiler_params=PARAMS,
        name="attend_back",
        cost_estimate=cost(40 * rows * heads * count * size * size * HEAD, 60_000_000),
    )(qt, u, *kv, bias, ot, dot_t, lse, *before)
    return out[0], out[1:-1], out[-1]


def bias_body(heads, slots_ref, buckets_ref, table_ref, bias_ref, buckets_t_ref):
    tables = [jnp.broadcast_to(table_ref[h : h + 1], (8, 128)) for h in range(heads)]
    buckets_t_ref[0] = buckets_ref[...].T
    for i in range(buckets_ref.shape[1] // 8):
        for j in range(buckets_ref.shape[0] // 128):
            at = (slice(i * 8, (i + 1) * 8), slice(j * 128, (j + 1) * 128))
            index = buckets_t_ref[(0,) + at]
            for h in range(heads):
                bias_ref[(h, 0) + at] = jnp.take_along_axis(tables[h], index, axis=1)


def bias_of(slots, buckets, table):
    heads = table.shape[0]
    size, blocks = buckets.shape[0], slots.shape[0]
    spec = pltpu.PrefetchScalarGridSpec(
        num_scalar_prefetch=1,
        grid=(blocks,),
        in_specs=[
            pl.BlockSpec((size, size), lambda s, slots: (0, slots[s])),
            pl.BlockSpec(table.shape, lambda s, slots: (0, 0)),
        ],
        out_specs=[
            pl.BlockSpec((heads, 1, size, size), lambda s, slots: (0, s, 0, 0)),
            pl.BlockSpec((1, size, size), lambda s, slots: (s, 0, 0)),
        ],
    )
    return pl.pallas_call(
        functools.partial(bias_body, heads),
        grid_spec=spec,
        out_shape=[
            jax.ShapeDtypeStruct((heads, blocks, size, size), F32),
            jax.ShapeDtypeStruct((blocks, size, size), jnp.int32),
        ],
        compiler_params=PARAMS,
        name="bias_of",
        cost_estimate=cost(1, 1),
    )(slots, buckets, table)


def sums_body(heads, count, buckets_ref, g_ref, out_ref):
    @pl.when(pl.program_id(0) == 0)
    def _():
        out_ref[...] = jnp.zeros_like(out_ref)

    total = out_ref[...]
    for i in range(buckets_ref.shape[1] // 8):
        at = slice(i * 8, (i + 1) * 8)
        index = buckets_ref[0, at]
        hot = [jnp.where(index == b, 1.0, 0.0) for b in range(count)]
        hot = jnp.concatenate(hot, axis=0).astype(BF16)
        g = jnp.concatenate([g_ref[h, 0, at] for h in range(heads)], axis=0)
        high = g.astype(BF16)
        low = (g - high.astype(F32)).astype(BF16)
        total += dot(jnp.concatenate([high, low], axis=0), hot, 1, 1)
    out_ref[...] = total


def bucket_sums(grad_bias, buckets, count):
    heads, blocks, size, _ = grad_bias.shape
    shape = (2 * heads * 8, count * 8)
    raw = pl.pallas_call(
        functools.partial(sums_body, heads, count),
        grid=(blocks,),
        in_specs=[
            pl.BlockSpec((1, size, size), lambda s: (s, 0, 0)),
            pl.BlockSpec((heads, 1, size, size), lambda s: (0, s, 0, 0)),
        ],
        out_specs=pl.BlockSpec(shape, lambda s: (0, 0)),
        out_shape=jax.ShapeDtypeStruct(shape, F32),
        compiler_params=PARAMS,
        name="bucket_sums",
        cost_estimate=cost(64 * grad_bias.size, 4 * grad_bias.size),
    )(buckets, grad_bias)
    raw = raw.reshape(2, heads, 8, count, 8)
    return jnp.sum(jnp.where(jnp.eye(8, dtype=bool)[None, None, :, None, :], raw, 0.0), (0, 2, 4)).T


def mix_body(x_ref, o_ref, w0, w1, place_ref, gain_ref, mixed_ref, pair_ref, *piece_refs):
    spread = dot(place_ref[...], o_ref[...], 0, 0).astype(BF16)
    mixed = x_ref[0].astype(F32) + back((w0, w1), spread)
    mixed_ref[...] = mixed
    scale = lax.rsqrt(jnp.mean(mixed * mixed, axis=0, keepdims=True) + NORM_EPSILON)
    n = (mixed * scale * gain_ref[...]).astype(BF16)
    pair_ref[0] = n
    put_pieces(piece_refs, n)


def group_specs(shape, count, per, rank):
    def place(g):
        def index(r):
            inside = jnp.clip(r - g * per, 0, per - 1)
            return (0, inside) if rank == 2 else (inside, 0, 0)

        return index

    return [pl.BlockSpec(shape, place(g)) for g in range(count)]


def mix(x, ot, w, place, gain):
    rows, width, size = x.shape
    inner = ot.shape[0]
    here = rows * size
    piece_specs, piece_shapes = pieces_of((width, here), size)
    return pl.pallas_call(
        mix_body,
        grid=(rows,),
        in_specs=[
            pl.BlockSpec((1, width, size), lambda r: (r, 0, 0)),
            pl.BlockSpec((inner, size), lambda r: (0, r)),
        ]
        + picked(w, 1)
        + [whole(place.shape), whole(gain.shape)],
        out_specs=[
            pl.BlockSpec((width, size), lambda r: (0, r)),
            pl.BlockSpec((1, width, size), lambda r: (0, 0, r)),
        ]
        + piece_specs,
        out_shape=[
            jax.ShapeDtypeStruct((width, here), F32),
            jax.ShapeDtypeStruct((2, width, here), BF16),
        ]
        + piece_shapes,
        compiler_params=PARAMS,
        name="mix",
        cost_estimate=cost(1, 1),
    )(x, ot, *w, place, gain)


def units_of(ws):
    return sum(w.shape[0] * w.shape[2] for w in ws)


def entries_of(ws):
    return sum(w.shape[0] for w in ws)


def loads_of(refs, buf, sems, kinds):
    copies, start = [], 0
    for a, ref in enumerate(refs):
        for k, kind in enumerate(kinds):
            inside = buf.at[k, pl.ds(start, ref.shape[0])]
            copies.append(pltpu.make_async_copy(ref.at[:, kind], inside, sems.at[a, k]))
        start += ref.shape[0]
    return copies


def ffn_body(count, masks, me_ref, *refs):
    ws, (n_ref, dy_ref, act_ref), refs = refs[:count], refs[count : count + 3], refs[count + 3 :]
    gs, (buf, acc, in_sems, out_sems) = refs[:-4], refs[-4:]
    t = pl.program_id(0)
    entries, rows, width = buf.shape[1:]
    size = entries * rows
    loads = loads_of(ws, buf, in_sems, range(3))

    @pl.when(t == 0)
    def _():
        for copy in loads:
            copy.start()
        acc[...] = jnp.zeros_like(acc)
        for copy in loads:
            copy.wait()

    norm = n_ref[0]
    dy = dy_ref[0]
    gate = dot(buf[0].reshape(size, width), norm, 1, 0)
    up = dot(buf[1].reshape(size, width), norm, 1, 0)
    dhid = dot(buf[2].reshape(size, width), dy, 1, 0)
    inside = gate * (0.7978845608028654 + 0.035677408136300125 * (gate * gate))
    half = 0.5 + 0.5 * jnp.tanh(inside)
    gelu = gate * half
    slope = half * (1.0 + (1.0 - half) * (6.0 * inside - 3.1915382432114616 * gate))
    dgate = (dhid * up * slope).astype(BF16)
    dup = (dhid * gelu).astype(BF16)
    hidden = (gelu * up).astype(BF16)
    act_ref[0] = dgate
    act_ref[1] = dup
    act_ref[2] = hidden
    acc[0] += dot(dgate, norm, 1, 1)
    acc[1] += dot(dup, norm, 1, 1)
    acc[2] += dot(hidden, dy, 1, 1)

    @pl.when(t == pl.num_programs(0) - 1)
    def _():
        for k in range(3):
            buf[k] = acc[k].astype(BF16).reshape(entries, rows, width)
        stores = []
        if masks is None:
            start = 0
            for g, out in enumerate(gs):
                for k in range(3):
                    inside = buf.at[k, pl.ds(start, out.shape[0])]
                    stores.append(pltpu.make_async_copy(inside, out.at[:, k], out_sems.at[g, k]))
                start += out.shape[0]
        else:
            part = len(masks) // 2
            for s, mask in enumerate(masks):
                for k in range(3):
                    inside, out = buf.at[k, me_ref[0] ^ mask], gs[s // part].at[s % part, k]
                    stores.append(pltpu.make_async_copy(inside, out, out_sems.at[s, k]))
        for copy in stores:
            copy.start()
        for copy in stores:
            copy.wait()


def ffn_group(me, ws, n, dy, tile, masks=None):
    halves, width, tokens = n.shape
    per = tokens // tile
    all_tokens = halves * tokens
    size = units_of(ws)
    inner = (entries_of(ws),) + ws[0].shape[2:]
    column = pl.BlockSpec((1, width, tile), lambda t, me: (t // per, 0, t % per))
    stores = len(ws) if masks is None else len(masks)
    shapes = [w.shape for w in ws]
    if masks is not None:
        shapes = [(inner[0] // 2, 3) + inner[1:]] * 2
    spec = pltpu.PrefetchScalarGridSpec(
        num_scalar_prefetch=1,
        grid=(halves * per,),
        in_specs=[ANY] * len(ws) + [column, column],
        out_specs=[pl.BlockSpec((3, size, tile), lambda t, me: (0, 0, t))] + [ANY] * len(shapes),
        scratch_shapes=[
            pltpu.VMEM((3,) + inner, BF16),
            pltpu.VMEM((3, size, width), F32),
            pltpu.SemaphoreType.DMA((len(ws), 3)),
            pltpu.SemaphoreType.DMA((stores, 3)),
        ],
    )
    out = pl.pallas_call(
        functools.partial(ffn_body, len(ws), masks),
        grid_spec=spec,
        out_shape=[jax.ShapeDtypeStruct((3, size, all_tokens), BF16)]
        + [jax.ShapeDtypeStruct(shape, BF16) for shape in shapes],
        compiler_params=PARAMS,
        name="ffn_group",
        cost_estimate=cost(1, 1),
    )(me, *ws, n, dy)
    return out[0], out[1:]


def ffn_terms(layout, kinds, refs):
    count, total = len(layout), sum(layout)
    ws, acts, refs = refs[:total], refs[total : total + count], refs[total + count :]
    bufs, sems = refs[:count], refs[count]

    @pl.when(pl.program_id(0) == 0)
    def _():
        copies, start = [], 0
        for p, arrays in enumerate(layout):
            copies += loads_of(ws[start : start + arrays], bufs[p], sems.at[p], kinds)
            start += arrays
        for copy in copies:
            copy.start()
        for copy in copies:
            copy.wait()

    out = None
    for act, buf in zip(acts, bufs):
        _, entries, rows, width = buf.shape
        for k in range(len(kinds)):
            term = dot(buf[k].reshape(entries * rows, width), act[k], 0, 0)
            out = term if out is None else out + term
    return out


def layout_of(groups):
    return tuple(len(ws) for ws in groups)


def flat_of(groups):
    return [w for ws in groups for w in ws]


def ffn_specs(groups, acts, kinds, tile, first):
    at = kinds[0] // len(kinds)
    return [ANY] * len(flat_of(groups)) + [
        pl.BlockSpec((len(kinds), a.shape[1], tile), lambda t: (at, 0, first + t)) for a in acts
    ]


def ffn_scratch(groups, kinds):
    return [
        pltpu.VMEM((len(kinds), entries_of(ws)) + ws[0].shape[2:], BF16) for ws in groups
    ] + [pltpu.SemaphoreType.DMA((len(groups), max(layout_of(groups)), len(kinds)))]


def ffn_back_body(layout, kinds, pieces, *refs):
    ins = sum(layout) + len(layout)
    total = ffn_terms(layout, kinds, refs[:ins] + refs[ins + pieces :])
    put_pieces(refs[ins : ins + pieces], total.astype(BF16))


def ffn_back(groups, acts, kinds, start, count, tile, pieces):
    width = groups[0][0].shape[3]
    piece_specs, piece_shapes = pieces_of((width, count), tile, pieces)
    return pl.pallas_call(
        functools.partial(ffn_back_body, layout_of(groups), kinds, pieces),
        grid=(count // tile,),
        in_specs=ffn_specs(groups, acts, kinds, tile, start // tile),
        out_specs=piece_specs,
        out_shape=piece_shapes,
        scratch_shapes=ffn_scratch(groups, kinds),
        compiler_params=PARAMS,
        name="ffn_back",
        cost_estimate=cost(1, 1),
    )(*flat_of(groups), *acts)


def layer_out_body(layout, *refs):
    ins = sum(layout) + len(layout)
    mixed_ref, got_ref, out_ref = refs[ins : ins + 3]
    total = ffn_terms(layout, [2], refs[:ins] + refs[ins + 3 :])
    out_ref[0] = (mixed_ref[...] + total + got_ref[...].astype(F32)).astype(BF16)


def layer_out_of(groups, acts, mixed, got, rows):
    width, here = mixed.shape
    size = here // rows
    col = pl.BlockSpec((width, size), lambda t: (0, t))
    return pl.pallas_call(
        functools.partial(layer_out_body, layout_of(groups)),
        grid=(rows,),
        in_specs=ffn_specs(groups, acts, [2], size, 0) + [col, col],
        out_specs=pl.BlockSpec((1, width, size), lambda t: (t, 0, 0)),
        out_shape=jax.ShapeDtypeStruct((rows, width, size), BF16),
        scratch_shapes=ffn_scratch(groups, [2]),
        compiler_params=PARAMS,
        name="layer_out_of",
        cost_estimate=cost(1, 1),
    )(*flat_of(groups), *acts, mixed, got)


def mix_back_body(layout, *refs):
    ins = sum(layout) + len(layout)
    weights, refs = refs[:ins], refs[ins:]
    pieces, refs = refs[:PIECES], refs[PIECES:]
    mixed_ref, dy_ref, o_ref, w0, w1, place_ref, home_ref, gain_ref = refs[:8]
    refs = refs[8:]
    inside_grad = len(refs) == 5 + len(layout) + 1
    dmixed_ref, do_ref, gg_ref = refs[:3]
    gw_ref, acc = refs[3:5] if inside_grad else (None, None)
    row = pl.program_id(0)
    got = jnp.concatenate([r[...] for r in pieces], axis=0)
    dn = ffn_terms(layout, [0, 1], weights + refs[-len(layout) - 1 :]) + got.astype(F32)
    mixed = mixed_ref[...]
    scale = lax.rsqrt(jnp.mean(mixed * mixed, axis=0, keepdims=True) + NORM_EPSILON)
    unit = mixed * scale
    scaled = dn * gain_ref[...]
    inside = jnp.mean(scaled * unit, axis=0, keepdims=True)
    dmixed = dy_ref[0].astype(F32) + scale * (scaled - unit * inside)
    dmixed_ref[...] = dmixed
    low = dmixed.astype(BF16)
    spread = dot(home_ref[...], o_ref[...], 0, 0).astype(BF16)
    do_ref[...] = dot(place_ref[...], forth((w0, w1), low), 1, 0).astype(BF16)
    both = dn * unit
    gain_part = both[:, :128]
    for j in range(1, both.shape[1] // 128):
        gain_part = gain_part + both[:, j * 128 : (j + 1) * 128]

    @pl.when(row == 0)
    def _():
        gg_ref[...] = gain_part

    @pl.when(row > 0)
    def _():
        gg_ref[...] += gain_part

    if inside_grad:
        product = dot(spread, low, 1, 1)

        @pl.when(row == 0)
        def _():
            acc[...] = product

        @pl.when(row > 0)
        def _():
            acc[...] += product

        @pl.when(row == pl.num_programs(0) - 1)
        def _():
            gw_ref[...] = acc[...].astype(BF16)


def mix_back(groups, acts, mixed, d1, dy, ot, w, place, home, gain):
    rows, width, size = dy.shape
    inner = ot.shape[0]
    here = rows * size
    col = pl.BlockSpec((width, size), lambda r: (0, r))
    head_col = pl.BlockSpec((inner, size), lambda r: (0, r))
    grad = (home.shape[1], width)
    fits = grad[0] <= 1024
    out = pl.pallas_call(
        functools.partial(mix_back_body, layout_of(groups)),
        grid=(rows,),
        in_specs=ffn_specs(groups, acts, [0, 1], size, 0)
        + pieces_of(mixed.shape, size)[0]
        + [col, pl.BlockSpec((1, width, size), lambda r: (r, 0, 0)), head_col]
        + picked(w, 1)
        + [whole(place.shape), whole(home.shape), whole(gain.shape)],
        out_specs=[col, head_col, whole((width, 128))] + [whole(grad)] * fits,
        out_shape=[
            jax.ShapeDtypeStruct((width, here), F32),
            jax.ShapeDtypeStruct((inner, here), BF16),
            jax.ShapeDtypeStruct((width, 128), F32),
        ]
        + [jax.ShapeDtypeStruct(grad, BF16)] * fits,
        scratch_shapes=[pltpu.VMEM(grad, F32)] * fits + ffn_scratch(groups, [0, 1]),
        compiler_params=PARAMS,
        name="mix_back",
        cost_estimate=cost(1, 1),
    )(*flat_of(groups), *acts, *d1, mixed, dy, ot, *w, place, home, gain)
    if not fits:
        spread = dot(home, ot, 0, 0).astype(BF16)
        out = [*out, dot(spread, out[0].astype(BF16), 1, 1).astype(BF16)]
    return out


def grads_body(per, groups, parts, n_ref, *refs):
    d_refs, refs = refs[:groups], refs[groups:]
    places, refs = refs[: len(parts)], refs[len(parts) :]
    outs, (acc, d_scr) = refs[: 2 * len(parts)], refs[2 * len(parts) :]
    row = pl.program_id(0)
    n = n_ref[...]
    for g, d_ref in enumerate(d_refs):

        @pl.when(row // per == g)
        def _():
            d_scr[...] = d_ref[...].reshape(d_scr.shape)

    products = []
    for (start, stop), p_ref in zip(parts, places):
        spread = dot(p_ref[...], d_scr[start:stop], 0, 0).astype(BF16)
        products.append(dot(spread, n, 1, 1))

    @pl.when(row == 0)
    def _():
        for j, product in enumerate(products):
            acc[j] = product

    @pl.when(row > 0)
    def _():
        for j, product in enumerate(products):
            acc[j] += product

    @pl.when(row == pl.num_programs(0) - 1)
    def _():
        half = acc.shape[1] // 2
        for j in range(len(parts)):
            outs[2 * j][...] = acc[j, :half].astype(BF16)
            outs[2 * j + 1][...] = acc[j, half:].astype(BF16)


def projection_grads(n, groups, parts, places, rows):
    if len(parts) > 1 and places[0].shape[1] > 1024:
        return [
            half
            for part, p in zip(parts, places)
            for half in projection_grads(n, groups, [part], [p], rows)
        ]
    width, here = n.shape
    size = here // rows
    per = rows // len(groups)
    rank = groups[0].ndim
    depth = groups[0].shape[-2]
    shape = (depth, size) if rank == 2 else (1, depth, size)
    wide = (places[0].shape[1], width)
    return pl.pallas_call(
        functools.partial(grads_body, per, len(groups), parts),
        grid=(rows,),
        in_specs=[pl.BlockSpec((width, size), lambda r: (0, r))]
        + group_specs(shape, len(groups), per, rank)
        + [whole(p.shape) for p in places],
        out_specs=[whole((wide[0] // 2, width))] * (2 * len(parts)),
        out_shape=[jax.ShapeDtypeStruct((wide[0] // 2, width), BF16)] * (2 * len(parts)),
        scratch_shapes=[pltpu.VMEM((len(parts),) + wide, F32), pltpu.VMEM((depth, size), BF16)],
        compiler_params=PARAMS,
        name="projection_grads",
        cost_estimate=cost(
            2 * len(parts) * wide[0] * width * here, 2 * n.size + 2 * len(parts) * wide[0] * width
        ),
    )(n, *groups, *places)


def last_body(per, groups, x_ref, dm_ref, *refs):
    dq_refs, dkv_refs, refs = refs[:groups], refs[groups : 2 * groups], refs[2 * groups :]
    ws, places, refs = (refs[:2], refs[2:4], refs[4:6]), refs[6:9], refs[9:]
    gain_ref, gx_ref, gg_ref, d_scr = refs
    row = pl.program_id(0)
    inner = dq_refs[0].shape[0]
    for g in range(groups):

        @pl.when(row // per == g)
        def _():
            d_scr[:inner] = dq_refs[g][...]
            d_scr[inner:] = dkv_refs[g][0, : 2 * inner]

    dn = None
    for j in range(3):
        spread = dot(places[j][...], d_scr[j * inner : (j + 1) * inner], 0, 0).astype(BF16)
        term = back(ws[j], spread)
        dn = term if dn is None else dn + term
    x = x_ref[0].astype(F32)
    scale = lax.rsqrt(jnp.mean(x * x, axis=0, keepdims=True) + NORM_EPSILON)
    unit = x * scale
    scaled = dn * gain_ref[...]
    inside = jnp.mean(scaled * unit, axis=0, keepdims=True)
    gx_ref[0] = dm_ref[...] + scale * (scaled - unit * inside)
    both = dn * unit
    gain_part = both[:, :128]
    for j in range(1, both.shape[1] // 128):
        gain_part = gain_part + both[:, j * 128 : (j + 1) * 128]

    @pl.when(row == 0)
    def _():
        gg_ref[...] = gain_part

    @pl.when(row > 0)
    def _():
        gg_ref[...] += gain_part


def last(x, dmixed, dqs, dkvs, ws, places, gain):
    rows, width, size = x.shape
    inner = dqs[0].shape[0]
    per = rows // len(dqs)
    col = pl.BlockSpec((width, size), lambda r: (0, r))
    block = pl.BlockSpec((1, width, size), lambda r: (r, 0, 0))
    return pl.pallas_call(
        functools.partial(last_body, per, len(dqs)),
        grid=(rows,),
        in_specs=[block, col]
        + group_specs((inner, size), len(dqs), per, 2)
        + group_specs((1,) + dkvs[0].shape[1:], len(dkvs), per, 3)
        + [spec for w, index in zip(ws, (1, 0, 0)) for spec in picked(w, index)]
        + [whole(p.shape) for p in places]
        + [whole(gain.shape)],
        out_specs=[block, whole((width, 128))],
        out_shape=[jax.ShapeDtypeStruct(x.shape, F32), jax.ShapeDtypeStruct((width, 128), F32)],
        scratch_shapes=[pltpu.VMEM((3 * inner, size), BF16)],
        compiler_params=PARAMS,
        name="last",
        cost_estimate=cost(1, 1),
    )(x, dmixed, *dqs, *dkvs, *[w for pair in ws for w in pair], *places, gain)


def after(value, *markers):
    return lax.optimization_barrier((value, markers))[0]


def pad_rows(w, rows):
    return jnp.pad(w, ((0, rows - w.shape[0]), (0, 0))) if rows > w.shape[0] else w


class Links:
    def __init__(self, dp, pairs):
        self.sizes = {"dp": dp, "x": pairs, "core": 2}
        self.strides = {"dp": 2 * pairs, "x": 2, "core": 1}
        self.core = ("core", 1)
        self.across = ("x", 1)
        self.near = ("dp", 1)
        self.far_count = dp // 2

    def swap(self, x, step):
        axis, mask = step
        return lax.ppermute(x, axis, [(i, i ^ mask) for i in range(self.sizes[axis])])

    def far_steps(self):
        return [("dp", k << 1) for k in range(1, self.far_count)]

    def far_bits(self):
        return [("dp", 2 << b) for b in range(self.far_count.bit_length() - 1)]

    def masks(self, steps):
        found = [(k << 1) * self.strides["dp"] for k in range(self.far_count)]
        for axis, mask in steps:
            found = found + [f ^ (mask * self.strides[axis]) for f in found]
        return found


def per_device(
    dp, ctx,
    tokens, soft_mask, segment_ids, buckets, gain_attn, gain_ffn, bias_table,
    w_query, w_key, w_value, w_attn_out, w_gate, w_up, w_ffn_out, cotangent,
):
    links = Links(dp, ctx // 2)
    swap, core, across, near = links.swap, links.core, links.across, links.near
    far = links.far_steps()
    rows, size, width = tokens.shape
    here = rows * size
    count, heads = bias_table.shape
    inner = heads * HEAD
    my_dp, my_ctx = lax.axis_index("dp"), lax.axis_index("x") * 2 + lax.axis_index("core")
    me = my_dp * ctx + my_ctx
    tile = min(512, here)
    order_a, order_b = [near, across], [across, near]

    def spread_of(steps):
        real = w_query.shape[0]
        owners = me ^ jnp.asarray(links.masks(steps), dtype=jnp.int32)
        inside = jnp.arange(each)
        feature = owners[:, None] * real + inside[None, :]
        feature = jnp.where(inside[None, :] < real, feature, -1).reshape(-1)
        return (jnp.arange(inner)[:, None] == feature[None, :]).astype(BF16)

    token = []

    def run(work, *args):
        if token:
            args = lax.optimization_barrier((args, tuple(token)))[0]
        out = work(*args)
        token[:] = jax.tree.leaves(out)
        return out

    each = -(-w_query.shape[0] // ROW_TILE) * ROW_TILE
    slot = lambda w: pad_rows(w, each)[None]
    flat = lambda w: w.reshape(-1, width)
    far_bits = links.far_bits()
    ab, ba = (near, across), (across, near)

    def exchange(arrays, steps):
        return [(a, swap(a, step)) for a, step in zip(arrays, steps)]

    def swap_core(value):
        return [swap(v, core) for v in value]

    def close(value):
        return run(lambda v: v, value)

    class Gather:
        def __init__(self, array, cuts, direct=False, mark=None, paths=(ab, ba)):
            if mark is not None:
                array = after(array, mark)
            self.cuts, self.stage, self.paths = cuts, 0, paths
            self.hops = 1 if direct else len(far_bits)
            steps = far if direct else far_bits[:1]
            self.held = [array] + [swap(array, step) for step in steps]

        def go(self):
            self.stage += 1
            if self.stage < self.hops:
                (array,) = run(lambda *p: join([p]), *self.held)
                self.held = [array, swap(array, far_bits[self.stage])]
            elif self.stage == self.hops:
                parts = run(lambda *p: cut_join(list(p), self.cuts), *self.held)
                self.held = exchange(parts, self.paths[0])
            elif self.stage == self.hops + 1:
                self.held = exchange(run(join, self.held), self.paths[1])

        def start_of(self):
            first = self.held[0]
            return first[0] if isinstance(first, tuple) else first

        def core_go(self):
            self.held = exchange(run(join, self.held), (core, core))

        def core_end(self):
            return close([list(pair) for pair in self.held])

    attn_w = Gather(
        jnp.concatenate([slot(w) for w in (w_key, w_attn_out, w_value, w_query)], axis=1)[:, None],
        [(0, 2 * each), (2 * each, 2 * each)],
        direct=True,
    )
    units = -(-w_gate.shape[0] // ROW_TILE)
    ffn_own = after((w_gate, w_up, w_ffn_out), attn_w.held[0])
    padded = [pad_rows(w, units * ROW_TILE) for w in ffn_own]
    marks = [0, 3, 5, 7] if units == 7 else list(range(units + 1))
    shards = [
        jnp.stack([w[low * ROW_TILE : high * ROW_TILE] for w in padded])
        for low, high in zip(marks, marks[1:])
    ]
    same_core = ("dp", "x")
    by_hops = units == 7
    last_group = len(shards) - 1

    x = jnp.transpose(tokens, (0, 2, 1))
    dy = jnp.transpose(cotangent, (0, 2, 1))
    gain_one, gain_two = gain_attn[:, None], gain_ffn[:, None]
    place_a, place_b = spread_of(order_a + [core]), spread_of(order_b + [core])
    real = w_query.shape[0]
    segs = lax.dynamic_slice_in_dim(segment_ids, my_ctx * size, size, 1)
    same = segs[:, None, :] == jnp.arange(DOCS, dtype=segs.dtype)[None, :, None]
    ones = jnp.ones((rows, 1, size), BF16)
    rest = AUG - 1 - DOCS
    aug = jnp.concatenate(
        [soft_mask[:, None, :], same.astype(BF16)] + [ones] * 3
        + [jnp.zeros((rows, rest - 3, size), BF16)],
        axis=1,
    )
    query_aug = jnp.concatenate(
        [ones, jnp.where(same, 0.0, MASK_VALUE).astype(BF16), jnp.zeros((rows, rest, size), BF16)],
        axis=1,
    )
    normed, dy_pair, *dy_own = run(first_norm, x, dy, gain_one)
    place_a, place_b, aug, query_aug, shards = close((place_a, place_b, aug, query_aug, shards))

    attn_w.go()
    ffn_w = [
        [lax.all_gather(after(shard, attn_w.start_of()), same_core)]
        for shard in (shards[:-1] if by_hops else shards)
    ]
    slots = jnp.array([0, 2, 1, 3], jnp.int32) ^ my_ctx
    bias, buckets_t = run(
        bias_of, slots, buckets, jnp.pad(bias_table.T, ((0, 0), (0, 128 - count)))
    )
    dy_parts = swap_core(dy_own)
    attn_w.go()
    if by_hops:
        last_w = Gather(
            shards[-1][None],
            [(0, shards[-1].shape[1])],
            mark=attn_w.start_of(),
            paths=((near,), (across,)),
        )
    dy_pair = run(fill, dy_pair, dy_parts)
    if by_hops:
        last_w.go()
    attn_w.core_go()
    wko, wvq = attn_w.core_end()
    kv_own = run(lambda *a: key_value(*a, 0, rows), normed, wko, wvq, place_a, place_b, aug)
    kv_across = swap(kv_own, across)
    kv_core = swap(kv_own, core)
    queries = run(lambda n, w, p: project(n, w, p, tile), normed, wvq, place_b)
    kv_core = close(kv_core)
    if by_hops:
        last_w.go()

    kv = run(lambda *k: list(k), kv_own, kv_across, kv_core)
    kv.append(close(jnp.concatenate([swap(k, core) for k in jnp.split(kv[1], min(2, rows))])))
    attended, lse = run(lambda *a: attend(*a, heads, 0), queries, query_aug, kv, bias)
    if by_hops:
        last_w.go()
    mixed, n_pair, *normed_two = run(mix, x, attended, wko, place_a, gain_two)
    n_parts = close(swap_core(normed_two))
    n_pair = run(fill, n_pair, n_parts)

    class Sums:
        def __init__(self, grads, paths, direct=False):
            self.paths, self.direct = paths[: len(grads)], direct
            self.stage = 0
            self.send(grads)

        def send(self, halves):
            self.keep = [h[0] for h in halves]
            self.got = [swap(h[1], p[self.stage]) for h, p in zip(halves, self.paths)]

        def go(self):
            near_hops = len(self.paths[0])
            hops = near_hops + (1 if self.direct else len(far_bits))
            self.stage += 1
            if self.stage > hops:
                return
            if self.stage < near_hops:
                self.send(run(add_halves, self.keep, self.got))
                return
            if self.stage == near_hops:
                rows_of = [k.shape[-2] for k in self.keep]
                self.edges = [sum(rows_of[:k]) for k in range(len(rows_of) + 1)]
                if self.direct:
                    piles = run(lambda k, r: add_piles(k, r, self.edges), self.keep, self.got)
                    self.keep = [piles[0]]
                    self.got = [swap(pile, step) for pile, step in zip(piles[1:], far)]
                    return
                halves = run(lambda k, r: add_merge(k, r, self.edges), self.keep, self.got)
            elif self.stage < hops:
                halves = run(add_halves, self.keep, self.got)[0]
            else:
                got = after(self.got, *token)
                self.out = add_last(self.keep[0], got, self.edges)
                return
            self.keep = [halves[0]]
            self.got = [swap(halves[1], far_bits[hops - 1 - self.stage])]

    acts, sums = [], []
    me_same = (my_dp * (ctx // 2) + lax.axis_index("x")).reshape(1)
    masks = [[m >> 1 for m in links.masks(steps)] for steps in (ab, ba)]
    ffn_grads = {}
    if by_hops:
        ffn_w.append(None)
    sequence = [0, 2, 1] if by_hops else range(len(ffn_w))
    by_group = {}
    for i in sequence:
        ws = ffn_w[i]
        if i == last_group and by_hops:
            ws = ffn_w[i] = last_ws
        some = tile if units_of(ws) <= 768 else tile // 2
        mask = masks[1] if by_hops and i == last_group - 1 else None
        act, grads = run(
            lambda m, w, n, d: ffn_group(m, w, n, d, some, mask), me_same, ws, n_pair, dy_pair
        )
        by_group[i] = act
        if by_hops and i == 0:
            last_ws = close(list(last_w.held[0]))
            grads = [after(g, last_ws) for g in grads]
        ffn_grads[i] = grads if by_hops and i else lax.psum_scatter(grads[0], same_core)
    ffn_grads = [ffn_grads[i] for i in range(len(ffn_w))]
    acts = [by_group[i] for i in range(len(ffn_w))]
    if by_hops:
        sums = [Sums(ffn_grads[-2:], [ab, ba])]

    def tick():
        for s in sums:
            s.go()

    back = run(lambda p, a: ffn_back(p, a, [0, 1], here, here, tile, PIECES), ffn_w, acts)
    dn_got = swap_core(back)
    (out_other,) = run(lambda p, a: ffn_back(p, a, [2], here, here, tile, 1), ffn_w, acts)
    dn_got = close(dn_got)
    out_got = swap(out_other, core)

    dmixed, dattended, gain_two_part, gwo = run(
        mix_back, ffn_w, acts, mixed, dn_got, dy, attended, wko, place_a, place_b, gain_two
    )
    tick()
    out_got = close(out_got)
    dq, dkv, grad_bias = run(
        lambda *a: attend_back(*a, heads, 0, []),
        queries, query_aug, kv, bias, attended, dattended, lse,
    )
    by_core = [(dkv[0], swap(dkv[2], core)), (dkv[1], swap(dkv[3], core))]
    tick()
    if by_hops:
        ffn_grads[0] = close(ffn_grads[0])
    entries = lambda g: tuple(v.reshape(-1, each, width) for v in g)
    home_a, home_b = (core,) + ba, (core,) + ab
    gwq = run(
        lambda n, d, p: projection_grads(n, [d], [(0, inner)], [p], rows), normed, dq, place_b
    )
    own, other = run(add_pairs, by_core)
    other = swap(other, across)
    part = gwo.shape[0] // 2
    query_sum = Sums([entries((gwo[:part], gwo[part:])), entries(gwq)], [home_b, home_b])
    grad_table = run(lambda g, b: bucket_sums(g, b, count), grad_bias, buckets_t)
    query_sum.go()
    out = run(lambda *a: layer_out_of(*a, rows), ffn_w, acts, mixed, out_got)
    tick()
    query_sum.go()
    (dkv,) = run(add_pairs, [(own, other)])
    gkv = run(
        lambda n, d, pa, pb: projection_grads(n, [d], [(0, inner), (inner, 2 * inner)], [pa, pb], rows),
        normed, dkv, place_a, place_b,
    )
    value_sum = Sums([entries(gkv[:2]), entries(gkv[2:])], [home_a, home_b], direct=dp <= 8)
    query_sum.go()
    value_sum.go()
    gx, gain_one_part = run(
        lambda *a: last(a[0], a[1], [a[2]], [a[3]], a[4:7], a[7:10], a[10]),
        x, dmixed, dq, dkv, wvq, wko, wvq, place_b, place_a, place_b, gain_one,
    )
    value_sum.go()
    tick()
    query_sum.go()
    small = jnp.concatenate(
        [jnp.sum(gain_one_part, 1), jnp.sum(gain_two_part, 1), grad_table.reshape(-1)]
    )
    length = small.shape[0]
    small = jnp.pad(small, (0, -length % 1024)).reshape(-1, 128)
    bits = [core, across] + [("dp", 1 << b) for b in range(dp.bit_length() - 1)]
    for k, one in enumerate(bits):
        got = swap(small, one)
        if k == 1:
            value_sum.go()
        if k == 3:
            value_sum.got = close(value_sum.got)
        small = run(lambda a, b: a + b, small, got)
    for _ in range(len(far_bits) + 4):
        for s in [query_sum, value_sum] + sums:
            s.go()
    small = small.reshape(-1)
    if by_hops:
        ffn_grads[-2:] = sums[0].out
    grad_gate, grad_up, grad_ffn_out = (
        jnp.concatenate([g[j].astype(F32) for g in ffn_grads])[: w_gate.shape[0]] for j in range(3)
    )
    return (
        jnp.transpose(out, (0, 2, 1)),
        jnp.transpose(gx, (0, 2, 1)),
        dkv[:, 2 * inner].astype(F32),
        small[:width],
        small[width : 2 * width],
        small[2 * width : length].reshape(count, heads),
        query_sum.out[1][:real],
        value_sum.out[0][:real],
        value_sum.out[1][:real],
        query_sum.out[0][:real],
        grad_gate,
        grad_up,
        grad_ffn_out,
    )


def solution(mesh):
    dp, ctx = mesh.shape["dp"], mesh.shape["ctx"]
    by_core = Mesh(mesh.devices.reshape(dp, ctx // 2, 2), ("dp", "x", "core"))
    ctx_axes = ("x", "core")
    split = P(("dp", "x", "core"), None)
    act = P("dp", ctx_axes, None)
    in_specs = (
        (act, P("dp", ctx_axes), P("dp", None), P(ctx_axes, None), P(), P(), P()) + (split,) * 7 + (act,)
    )
    out_specs = (act, act, P("dp", ctx_axes), P(), P(), P()) + (split,) * 7
    return jax.shard_map(
        functools.partial(per_device, dp, ctx),
        mesh=by_core,
        in_specs=in_specs,
        out_specs=out_specs,
        check_vma=False,
    )
```

```python
import functools

import jax
import jax.numpy as jnp
import numpy as np
from jax import lax
from jax.experimental import pallas as pl
from jax.experimental.pallas import tpu as pltpu
from jax.sharding import Mesh, PartitionSpec as P

NORM_EPSILON = 1e-06
MASK_VALUE = -1e30
F32, BF16 = jnp.float32, jnp.bfloat16
HEAD = 64
ROW_TILE = 16
AUG = 16
DOCS = 5
ONES = 1 + DOCS
VMEM_LIMIT = 58 * 1024 * 1024
PARAMS = pltpu.CompilerParams(vmem_limit_bytes=VMEM_LIMIT)


def dot(a, b, ca, cb):
    return lax.dot_general(a, b, (((ca,), (cb,)), ((), ())), preferred_element_type=F32)


def whole(shape):
    return pl.BlockSpec(shape, lambda t: (0,) * len(shape), pipeline_mode=pl.Buffered(1))


def cost(flops, nbytes):
    return pl.CostEstimate(flops=1, bytes_accessed=1, transcendentals=0)


ANY = pl.BlockSpec(memory_space=pl.ANY)


def join(pairs):
    return [jnp.concatenate(list(pair), axis=0) for pair in pairs]


def cut_join(parts, cuts):
    out = []
    for cut in cuts:
        at = np.s_[:, :, cut[0] : cut[0] + cut[1]] if isinstance(cut, tuple) else np.s_[:, cut]
        out.append(jnp.concatenate([p[at] for p in parts], axis=0))
    return out


def fill(pair, parts):
    start = 0
    for part in parts:
        pair = pair.at[1, start : start + part.shape[0]].set(part)
        start += part.shape[0]
    return pair


def add_halves(keep, got):
    out = []
    for k, r in zip(keep, got):
        part = k.shape[0] // 2
        out.append((k[:part] + r[:part], k[part:] + r[part:]))
    return out


def add_merge(keep, got, edges):
    part = keep[0].shape[0] // 2
    ends = [slice(None, part), slice(part, None)]
    return [jnp.concatenate([k[e] + r[e] for k, r in zip(keep, got)], axis=-2) for e in ends]


def add_piles(keep, got, edges):
    return [
        jnp.concatenate([k[i : i + 1] + r[i : i + 1] for k, r in zip(keep, got)], axis=-2)
        for i in range(keep[0].shape[0])
    ]


def add_last(keep, got, edges):
    total = keep[0].astype(F32)
    for r in got:
        total = total + r[0].astype(F32)
    return [total[..., a:b, :] for a, b in zip(edges, edges[1:])]


def add_pairs(pairs):
    return [a + b for a, b in pairs]


PIECES = 2


def pieces_of(shape, tile, pieces=PIECES):
    rows, columns = shape
    piece = (rows // pieces, columns)
    specs = [pl.BlockSpec((piece[0], tile), lambda t: (0, t)) for _ in range(pieces)]
    return specs, [jax.ShapeDtypeStruct(piece, BF16)] * pieces


def put_pieces(refs, value):
    step = refs[0].shape[0]
    for k, ref in enumerate(refs):
        ref[...] = value[k * step : (k + 1) * step]


def norm_body(x_ref, dy_ref, gain_ref, n_ref, pair_ref, *piece_refs):
    x = x_ref[0].astype(F32)
    scale = lax.rsqrt(jnp.mean(x * x, axis=0, keepdims=True) + NORM_EPSILON)
    n_ref[...] = (x * scale * gain_ref[...]).astype(BF16)
    pair_ref[0] = dy_ref[0]
    put_pieces(piece_refs, dy_ref[0])


def first_norm(x, dy, gain):
    rows, width, size = x.shape
    block = pl.BlockSpec((1, width, size), lambda r: (r, 0, 0))
    col = pl.BlockSpec((width, size), lambda r: (0, r))
    here = rows * size
    piece_specs, piece_shapes = pieces_of((width, here), size)
    return pl.pallas_call(
        norm_body,
        grid=(rows,),
        in_specs=[block, block, whole(gain.shape)],
        out_specs=[col, pl.BlockSpec((1, width, size), lambda r: (0, 0, r))] + piece_specs,
        out_shape=[
            jax.ShapeDtypeStruct((width, here), BF16),
            jax.ShapeDtypeStruct((2, width, here), BF16),
        ]
        + piece_shapes,
        compiler_params=PARAMS,
        name="first_norm",
        cost_estimate=cost(4 * x.size, 10 * x.size),
    )(x, dy, gain)


def picked(pair, index):
    return [
        pl.BlockSpec(
            (w.shape[0], 1, w.shape[2] // 2, w.shape[3]),
            lambda t: (0, 0, index, 0),
            pipeline_mode=pl.Buffered(1),
        )
        for w in pair
    ]


def flat_rows(w_ref):
    entries, _, each, width = w_ref.shape
    return w_ref[...].reshape(entries * each, width)


def forth(refs, x):
    return jnp.concatenate([dot(flat_rows(w), x, 1, 0).astype(BF16) for w in refs], axis=0)


def back(refs, x):
    part = x.shape[0] // 2
    return dot(flat_rows(refs[0]), x[:part], 0, 0) + dot(flat_rows(refs[1]), x[part:], 0, 0)


def key_value_body(inner, n_ref, wk0, wk1, wv0, wv1, pk_ref, pv_ref, aug_ref, out_ref):
    n = n_ref[...]
    for start, refs, p_ref in ((0, (wk0, wk1), pk_ref), (inner, (wv0, wv1), pv_ref)):
        out_ref[0, start : start + inner] = dot(p_ref[...], forth(refs, n), 1, 0).astype(BF16)
    out_ref[0, 2 * inner :] = aug_ref[0]


def key_value(n, wk, wv, place_k, place_v, aug, first, rows):
    size = aug.shape[2]
    inner = place_k.shape[0]
    width = n.shape[0]
    return pl.pallas_call(
        functools.partial(key_value_body, inner),
        grid=(rows,),
        in_specs=[pl.BlockSpec((width, size), lambda r: (0, first + r))]
        + picked(wk, 0)
        + picked(wv, 0)
        + [
            whole(place_k.shape),
            whole(place_v.shape),
            pl.BlockSpec((1, AUG, size), lambda r: (first + r, 0, 0)),
        ],
        out_specs=pl.BlockSpec((1, 2 * inner + AUG, size), lambda r: (r, 0, 0)),
        out_shape=jax.ShapeDtypeStruct((rows, 2 * inner + AUG, size), BF16),
        compiler_params=PARAMS,
        name="key_value",
        cost_estimate=cost(1, 1),
    )(n, *wk, *wv, place_k, place_v, aug)


def project_body(n_ref, w0, w1, p_ref, out_ref):
    out_ref[...] = dot(p_ref[...], forth((w0, w1), n_ref[...]), 1, 0).astype(BF16)


def project(n, w, place, tile):
    width, here = n.shape
    inner = place.shape[0]
    return pl.pallas_call(
        project_body,
        grid=(here // tile,),
        in_specs=[pl.BlockSpec((width, tile), lambda t: (0, t))] + picked(w, 1) + [whole(place.shape)],
        out_specs=pl.BlockSpec((inner, tile), lambda t: (0, t)),
        out_shape=jax.ShapeDtypeStruct((inner, here), BF16),
        compiler_params=PARAMS,
        name="project",
        cost_estimate=cost(1, 1),
    )(n, *w, place)


def attend_body(heads, inner, q_ref, u_ref, *refs):
    *blocks, bias_ref, o_ref, lse_ref, s_ref = refs
    for h in range(heads):
        part = slice(h * HEAD, (h + 1) * HEAD)
        q = jnp.concatenate([q_ref[part], u_ref[0]], axis=0)
        top = None
        for s, k_ref in enumerate(blocks):
            k = jnp.concatenate([k_ref[0, part], k_ref[0, 2 * inner :]], axis=0)
            logits = dot(k, q, 0, 0) + bias_ref[h, s]
            s_ref[s] = logits
            peak = jnp.max(logits, axis=0, keepdims=True)
            top = peak if top is None else jnp.maximum(top, peak)
        total, out = None, None
        for s, k_ref in enumerate(blocks):
            e = jnp.exp(s_ref[s] - top)
            part_sum = jnp.sum(e, axis=0, keepdims=True)
            total = part_sum if total is None else total + part_sum
            value = k_ref[0, slice(inner + h * HEAD, inner + (h + 1) * HEAD)]
            term = dot(value, e.astype(BF16), 1, 0)
            out = term if out is None else out + term
        o_ref[part] = (out / total).astype(BF16)
        lse_ref[0, h : h + 1] = top + jnp.log(total)
    pad = lse_ref.shape[1] - heads
    if pad:
        lse_ref[0, heads:] = jnp.zeros((pad, lse_ref.shape[2]), F32)


def attend(qt, u, kv, bias, heads, first):
    rows, depth, size = kv[0].shape
    inner = heads * HEAD
    pad = -(-heads // 8) * 8
    return pl.pallas_call(
        functools.partial(attend_body, heads, inner),
        grid=(rows,),
        in_specs=[
            pl.BlockSpec((inner, size), lambda r: (0, first + r)),
            pl.BlockSpec((1, AUG, size), lambda r: (first + r, 0, 0)),
        ]
        + [pl.BlockSpec((1, depth, size), lambda r: (r, 0, 0))] * len(kv)
        + [whole(bias.shape)],
        out_specs=[
            pl.BlockSpec((inner, size), lambda r: (0, r)),
            pl.BlockSpec((1, pad, size), lambda r: (r, 0, 0)),
        ],
        out_shape=[
            jax.ShapeDtypeStruct((inner, rows * size), BF16),
            jax.ShapeDtypeStruct((rows, pad, size), F32),
        ],
        scratch_shapes=[pltpu.VMEM((len(kv), size, size), F32)],
        compiler_params=PARAMS,
        name="attend",
        cost_estimate=cost(16 * rows * heads * len(kv) * size * size * HEAD, 40_000_000),
    )(qt, u, *kv, bias)


def three(x):
    a = x.astype(BF16).astype(F32)
    rest = x - a
    b = rest.astype(BF16).astype(F32)
    return a, b, rest - b


def attend_back_body(heads, inner, count, more, q_ref, u_ref, *refs):
    blocks = refs[:count]
    bias_ref, o_ref, do_ref, lse_ref = refs[count : count + 4]
    refs = refs[count + 4 :]
    before_ref, refs = (refs[0], refs[1:]) if more else (None, refs)
    dq_ref = refs[0]
    grads = refs[1 : count + 1]
    gb_ref = refs[count + 1]
    size = bias_ref.shape[3]
    row = pl.program_id(0)
    mask_grad = [None] * count
    extra = u_ref[0].astype(F32)
    place = lax.broadcasted_iota(jnp.int32, (AUG, size), 0)

    def pick(parts, base):
        for i, value in enumerate(parts):
            base = jnp.where(place == ONES + i, value, base)
        return base.astype(BF16)

    for h in range(heads):
        part = slice(h * HEAD, (h + 1) * HEAD)
        vpart = slice(inner + h * HEAD, inner + (h + 1) * HEAD)
        q = q_ref[part]
        do = do_ref[part]
        delta = jnp.sum(do.astype(F32) * o_ref[part].astype(F32), axis=0, keepdims=True)
        q_aug = jnp.concatenate([q, pick(three(-lse_ref[0, h : h + 1]), extra)], axis=0)
        do_aug = jnp.concatenate([do, pick(three(-delta), jnp.zeros_like(extra))], axis=0)
        dq = None
        for s, k_ref in enumerate(blocks):
            k = k_ref[0, part]
            aug = k_ref[0, 2 * inner :]
            logits = dot(jnp.concatenate([k, aug], axis=0), q_aug, 0, 0) + bias_ref[h, s]
            p = jnp.exp(logits)
            dp = dot(jnp.concatenate([k_ref[0, vpart], aug], axis=0), do_aug, 0, 0)
            ds = p * dp

            @pl.when(row == 0)
            def _():
                gb_ref[h, s] = before_ref[h, s] + ds if more else ds

            @pl.when(row > 0)
            def _():
                gb_ref[h, s] += ds

            low = ds.astype(BF16)
            grads[s][0, vpart] = dot(do, p.astype(BF16), 1, 1).astype(BF16)
            both = dot(q_aug, low, 1, 1)
            grads[s][0, part] = both[:HEAD].astype(BF16)
            g = both[HEAD : HEAD + 1]
            mask_grad[s] = g if mask_grad[s] is None else mask_grad[s] + g
            term = dot(k, low, 1, 0)
            dq = term if dq is None else dq + term
        dq_ref[part] = dq.astype(BF16)
    for s in range(count):
        grads[s][0, 2 * inner :] = jnp.broadcast_to(mask_grad[s], (AUG, size)).astype(BF16)


def attend_back(qt, u, kv, bias, ot, dot_t, lse, heads, first, before):
    rows, depth, size = kv[0].shape
    inner = heads * HEAD
    count = len(kv)
    own = pl.BlockSpec((inner, size), lambda r: (0, r))
    col = pl.BlockSpec((inner, size), lambda r: (0, first + r))
    block = pl.BlockSpec((1, depth, size), lambda r: (r, 0, 0))
    out = pl.pallas_call(
        functools.partial(attend_back_body, heads, inner, count, len(before)),
        grid=(rows,),
        in_specs=[col, pl.BlockSpec((1, AUG, size), lambda r: (first + r, 0, 0))]
        + [block] * count
        + [whole(bias.shape), own, col]
        + [pl.BlockSpec((1,) + lse.shape[1:], lambda r: (r, 0, 0))]
        + [whole(b.shape) for b in before],
        out_specs=[own] + [block] * count + [whole(bias.shape)],
        out_shape=[jax.ShapeDtypeStruct((inner, rows * size), BF16)]
        + [jax.ShapeDtypeStruct((rows, depth, size), BF16)] * count
        + [jax.ShapeDtypeStruct(bias.shape, F32)],
        compiler_params=PARAMS,
        name="attend_back",
        cost_estimate=cost(40 * rows * heads * count * size * size * HEAD, 60_000_000),
    )(qt, u, *kv, bias, ot, dot_t, lse, *before)
    return out[0], out[1:-1], out[-1]


def bias_body(heads, slots_ref, buckets_ref, table_ref, bias_ref, buckets_t_ref):
    tables = [jnp.broadcast_to(table_ref[h : h + 1], (8, 128)) for h in range(heads)]
    buckets_t_ref[0] = buckets_ref[...].T
    for i in range(buckets_ref.shape[1] // 8):
        for j in range(buckets_ref.shape[0] // 128):
            at = (slice(i * 8, (i + 1) * 8), slice(j * 128, (j + 1) * 128))
            index = buckets_t_ref[(0,) + at]
            for h in range(heads):
                bias_ref[(h, 0) + at] = jnp.take_along_axis(tables[h], index, axis=1)


def bias_of(slots, buckets, table):
    heads = table.shape[0]
    size, blocks = buckets.shape[0], slots.shape[0]
    spec = pltpu.PrefetchScalarGridSpec(
        num_scalar_prefetch=1,
        grid=(blocks,),
        in_specs=[
            pl.BlockSpec((size, size), lambda s, slots: (0, slots[s])),
            pl.BlockSpec(table.shape, lambda s, slots: (0, 0)),
        ],
        out_specs=[
            pl.BlockSpec((heads, 1, size, size), lambda s, slots: (0, s, 0, 0)),
            pl.BlockSpec((1, size, size), lambda s, slots: (s, 0, 0)),
        ],
    )
    return pl.pallas_call(
        functools.partial(bias_body, heads),
        grid_spec=spec,
        out_shape=[
            jax.ShapeDtypeStruct((heads, blocks, size, size), F32),
            jax.ShapeDtypeStruct((blocks, size, size), jnp.int32),
        ],
        compiler_params=PARAMS,
        name="bias_of",
        cost_estimate=cost(1, 1),
    )(slots, buckets, table)


def sums_body(heads, count, buckets_ref, g_ref, out_ref):
    @pl.when(pl.program_id(0) == 0)
    def _():
        out_ref[...] = jnp.zeros_like(out_ref)

    total = out_ref[...]
    for i in range(buckets_ref.shape[1] // 8):
        at = slice(i * 8, (i + 1) * 8)
        index = buckets_ref[0, at]
        hot = [jnp.where(index == b, 1.0, 0.0) for b in range(count)]
        hot = jnp.concatenate(hot, axis=0).astype(BF16)
        g = jnp.concatenate([g_ref[h, 0, at] for h in range(heads)], axis=0)
        high = g.astype(BF16)
        low = (g - high.astype(F32)).astype(BF16)
        total += dot(jnp.concatenate([high, low], axis=0), hot, 1, 1)
    out_ref[...] = total


def bucket_sums(grad_bias, buckets, count):
    heads, blocks, size, _ = grad_bias.shape
    shape = (2 * heads * 8, count * 8)
    raw = pl.pallas_call(
        functools.partial(sums_body, heads, count),
        grid=(blocks,),
        in_specs=[
            pl.BlockSpec((1, size, size), lambda s: (s, 0, 0)),
            pl.BlockSpec((heads, 1, size, size), lambda s: (0, s, 0, 0)),
        ],
        out_specs=pl.BlockSpec(shape, lambda s: (0, 0)),
        out_shape=jax.ShapeDtypeStruct(shape, F32),
        compiler_params=PARAMS,
        name="bucket_sums",
        cost_estimate=cost(64 * grad_bias.size, 4 * grad_bias.size),
    )(buckets, grad_bias)
    raw = raw.reshape(2, heads, 8, count, 8)
    return jnp.sum(jnp.where(jnp.eye(8, dtype=bool)[None, None, :, None, :], raw, 0.0), (0, 2, 4)).T


def mix_body(x_ref, o_ref, w0, w1, place_ref, gain_ref, mixed_ref, pair_ref, *piece_refs):
    spread = dot(place_ref[...], o_ref[...], 0, 0).astype(BF16)
    mixed = x_ref[0].astype(F32) + back((w0, w1), spread)
    mixed_ref[...] = mixed
    scale = lax.rsqrt(jnp.mean(mixed * mixed, axis=0, keepdims=True) + NORM_EPSILON)
    n = (mixed * scale * gain_ref[...]).astype(BF16)
    pair_ref[0] = n
    put_pieces(piece_refs, n)


def group_specs(shape, count, per, rank):
    def place(g):
        def index(r):
            inside = jnp.clip(r - g * per, 0, per - 1)
            return (0, inside) if rank == 2 else (inside, 0, 0)

        return index

    return [pl.BlockSpec(shape, place(g)) for g in range(count)]


def mix(x, ot, w, place, gain):
    rows, width, size = x.shape
    inner = ot.shape[0]
    here = rows * size
    piece_specs, piece_shapes = pieces_of((width, here), size)
    return pl.pallas_call(
        mix_body,
        grid=(rows,),
        in_specs=[
            pl.BlockSpec((1, width, size), lambda r: (r, 0, 0)),
            pl.BlockSpec((inner, size), lambda r: (0, r)),
        ]
        + picked(w, 1)
        + [whole(place.shape), whole(gain.shape)],
        out_specs=[
            pl.BlockSpec((width, size), lambda r: (0, r)),
            pl.BlockSpec((1, width, size), lambda r: (0, 0, r)),
        ]
        + piece_specs,
        out_shape=[
            jax.ShapeDtypeStruct((width, here), F32),
            jax.ShapeDtypeStruct((2, width, here), BF16),
        ]
        + piece_shapes,
        compiler_params=PARAMS,
        name="mix",
        cost_estimate=cost(1, 1),
    )(x, ot, *w, place, gain)


def units_of(ws):
    return sum(w.shape[0] * w.shape[2] for w in ws)


def entries_of(ws):
    return sum(w.shape[0] for w in ws)


def loads_of(refs, buf, sems, kinds):
    copies, start = [], 0
    for a, ref in enumerate(refs):
        for k, kind in enumerate(kinds):
            inside = buf.at[k, pl.ds(start, ref.shape[0])]
            copies.append(pltpu.make_async_copy(ref.at[:, kind], inside, sems.at[a, k]))
        start += ref.shape[0]
    return copies


def ffn_body(count, masks, me_ref, *refs):
    ws, (n_ref, dy_ref, act_ref), refs = refs[:count], refs[count : count + 3], refs[count + 3 :]
    gs, (buf, acc, in_sems, out_sems) = refs[:-4], refs[-4:]
    t = pl.program_id(0)
    entries, rows, width = buf.shape[1:]
    size = entries * rows
    loads = loads_of(ws, buf, in_sems, range(3))

    @pl.when(t == 0)
    def _():
        for copy in loads:
            copy.start()
        acc[...] = jnp.zeros_like(acc)
        for copy in loads:
            copy.wait()

    norm = n_ref[0]
    dy = dy_ref[0]
    gate = dot(buf[0].reshape(size, width), norm, 1, 0)
    up = dot(buf[1].reshape(size, width), norm, 1, 0)
    dhid = dot(buf[2].reshape(size, width), dy, 1, 0)
    inside = gate * (0.7978845608028654 + 0.035677408136300125 * (gate * gate))
    half = 0.5 + 0.5 * jnp.tanh(inside)
    gelu = gate * half
    slope = half * (1.0 + (1.0 - half) * (6.0 * inside - 3.1915382432114616 * gate))
    dgate = (dhid * up * slope).astype(BF16)
    dup = (dhid * gelu).astype(BF16)
    hidden = (gelu * up).astype(BF16)
    act_ref[0] = dgate
    act_ref[1] = dup
    act_ref[2] = hidden
    acc[0] += dot(dgate, norm, 1, 1)
    acc[1] += dot(dup, norm, 1, 1)
    acc[2] += dot(hidden, dy, 1, 1)

    @pl.when(t == pl.num_programs(0) - 1)
    def _():
        for k in range(3):
            buf[k] = acc[k].astype(BF16).reshape(entries, rows, width)
        stores = []
        if masks is None:
            start = 0
            for g, out in enumerate(gs):
                for k in range(3):
                    inside = buf.at[k, pl.ds(start, out.shape[0])]
                    stores.append(pltpu.make_async_copy(inside, out.at[:, k], out_sems.at[g, k]))
                start += out.shape[0]
        else:
            part = len(masks) // 2
            for s, mask in enumerate(masks):
                for k in range(3):
                    inside, out = buf.at[k, me_ref[0] ^ mask], gs[s // part].at[s % part, k]
                    stores.append(pltpu.make_async_copy(inside, out, out_sems.at[s, k]))
        for copy in stores:
            copy.start()
        for copy in stores:
            copy.wait()


def ffn_group(me, ws, n, dy, tile, masks=None):
    halves, width, tokens = n.shape
    per = tokens // tile
    all_tokens = halves * tokens
    size = units_of(ws)
    inner = (entries_of(ws),) + ws[0].shape[2:]
    column = pl.BlockSpec((1, width, tile), lambda t, me: (t // per, 0, t % per))
    stores = len(ws) if masks is None else len(masks)
    shapes = [w.shape for w in ws]
    if masks is not None:
        shapes = [(inner[0] // 2, 3) + inner[1:]] * 2
    spec = pltpu.PrefetchScalarGridSpec(
        num_scalar_prefetch=1,
        grid=(halves * per,),
        in_specs=[ANY] * len(ws) + [column, column],
        out_specs=[pl.BlockSpec((3, size, tile), lambda t, me: (0, 0, t))] + [ANY] * len(shapes),
        scratch_shapes=[
            pltpu.VMEM((3,) + inner, BF16),
            pltpu.VMEM((3, size, width), F32),
            pltpu.SemaphoreType.DMA((len(ws), 3)),
            pltpu.SemaphoreType.DMA((stores, 3)),
        ],
    )
    out = pl.pallas_call(
        functools.partial(ffn_body, len(ws), masks),
        grid_spec=spec,
        out_shape=[jax.ShapeDtypeStruct((3, size, all_tokens), BF16)]
        + [jax.ShapeDtypeStruct(shape, BF16) for shape in shapes],
        compiler_params=PARAMS,
        name="ffn_group",
        cost_estimate=cost(1, 1),
    )(me, *ws, n, dy)
    return out[0], out[1:]


def ffn_terms(layout, kinds, refs):
    count, total = len(layout), sum(layout)
    ws, acts, refs = refs[:total], refs[total : total + count], refs[total + count :]
    bufs, sems = refs[:count], refs[count]

    @pl.when(pl.program_id(0) == 0)
    def _():
        copies, start = [], 0
        for p, arrays in enumerate(layout):
            copies += loads_of(ws[start : start + arrays], bufs[p], sems.at[p], kinds)
            start += arrays
        for copy in copies:
            copy.start()
        for copy in copies:
            copy.wait()

    out = None
    for act, buf in zip(acts, bufs):
        _, entries, rows, width = buf.shape
        for k in range(len(kinds)):
            term = dot(buf[k].reshape(entries * rows, width), act[k], 0, 0)
            out = term if out is None else out + term
    return out


def layout_of(groups):
    return tuple(len(ws) for ws in groups)


def flat_of(groups):
    return [w for ws in groups for w in ws]


def ffn_specs(groups, acts, kinds, tile, first):
    at = kinds[0] // len(kinds)
    return [ANY] * len(flat_of(groups)) + [
        pl.BlockSpec((len(kinds), a.shape[1], tile), lambda t: (at, 0, first + t)) for a in acts
    ]


def ffn_scratch(groups, kinds):
    return [
        pltpu.VMEM((len(kinds), entries_of(ws)) + ws[0].shape[2:], BF16) for ws in groups
    ] + [pltpu.SemaphoreType.DMA((len(groups), max(layout_of(groups)), len(kinds)))]


def ffn_back_body(layout, kinds, pieces, *refs):
    ins = sum(layout) + len(layout)
    total = ffn_terms(layout, kinds, refs[:ins] + refs[ins + pieces :])
    put_pieces(refs[ins : ins + pieces], total.astype(BF16))


def ffn_back(groups, acts, kinds, start, count, tile, pieces):
    width = groups[0][0].shape[3]
    piece_specs, piece_shapes = pieces_of((width, count), tile, pieces)
    return pl.pallas_call(
        functools.partial(ffn_back_body, layout_of(groups), kinds, pieces),
        grid=(count // tile,),
        in_specs=ffn_specs(groups, acts, kinds, tile, start // tile),
        out_specs=piece_specs,
        out_shape=piece_shapes,
        scratch_shapes=ffn_scratch(groups, kinds),
        compiler_params=PARAMS,
        name="ffn_back",
        cost_estimate=cost(1, 1),
    )(*flat_of(groups), *acts)


def layer_out_body(layout, *refs):
    ins = sum(layout) + len(layout)
    mixed_ref, got_ref, out_ref = refs[ins : ins + 3]
    total = ffn_terms(layout, [2], refs[:ins] + refs[ins + 3 :])
    out_ref[0] = (mixed_ref[...] + total + got_ref[...].astype(F32)).astype(BF16)


def layer_out_of(groups, acts, mixed, got, rows):
    width, here = mixed.shape
    size = here // rows
    col = pl.BlockSpec((width, size), lambda t: (0, t))
    return pl.pallas_call(
        functools.partial(layer_out_body, layout_of(groups)),
        grid=(rows,),
        in_specs=ffn_specs(groups, acts, [2], size, 0) + [col, col],
        out_specs=pl.BlockSpec((1, width, size), lambda t: (t, 0, 0)),
        out_shape=jax.ShapeDtypeStruct((rows, width, size), BF16),
        scratch_shapes=ffn_scratch(groups, [2]),
        compiler_params=PARAMS,
        name="layer_out_of",
        cost_estimate=cost(1, 1),
    )(*flat_of(groups), *acts, mixed, got)


def mix_back_body(layout, *refs):
    ins = sum(layout) + len(layout)
    weights, refs = refs[:ins], refs[ins:]
    pieces, refs = refs[:PIECES], refs[PIECES:]
    mixed_ref, dy_ref, o_ref, w0, w1, place_ref, home_ref, gain_ref = refs[:8]
    refs = refs[8:]
    inside_grad = len(refs) == 5 + len(layout) + 1
    dmixed_ref, do_ref, gg_ref = refs[:3]
    gw_ref, acc = refs[3:5] if inside_grad else (None, None)
    row = pl.program_id(0)
    got = jnp.concatenate([r[...] for r in pieces], axis=0)
    dn = ffn_terms(layout, [0, 1], weights + refs[-len(layout) - 1 :]) + got.astype(F32)
    mixed = mixed_ref[...]
    scale = lax.rsqrt(jnp.mean(mixed * mixed, axis=0, keepdims=True) + NORM_EPSILON)
    unit = mixed * scale
    scaled = dn * gain_ref[...]
    inside = jnp.mean(scaled * unit, axis=0, keepdims=True)
    dmixed = dy_ref[0].astype(F32) + scale * (scaled - unit * inside)
    dmixed_ref[...] = dmixed
    low = dmixed.astype(BF16)
    spread = dot(home_ref[...], o_ref[...], 0, 0).astype(BF16)
    do_ref[...] = dot(place_ref[...], forth((w0, w1), low), 1, 0).astype(BF16)
    both = dn * unit
    gain_part = both[:, :128]
    for j in range(1, both.shape[1] // 128):
        gain_part = gain_part + both[:, j * 128 : (j + 1) * 128]

    @pl.when(row == 0)
    def _():
        gg_ref[...] = gain_part

    @pl.when(row > 0)
    def _():
        gg_ref[...] += gain_part

    if inside_grad:
        product = dot(spread, low, 1, 1)

        @pl.when(row == 0)
        def _():
            acc[...] = product

        @pl.when(row > 0)
        def _():
            acc[...] += product

        @pl.when(row == pl.num_programs(0) - 1)
        def _():
            gw_ref[...] = acc[...].astype(BF16)


def mix_back(groups, acts, mixed, d1, dy, ot, w, place, home, gain):
    rows, width, size = dy.shape
    inner = ot.shape[0]
    here = rows * size
    col = pl.BlockSpec((width, size), lambda r: (0, r))
    head_col = pl.BlockSpec((inner, size), lambda r: (0, r))
    grad = (home.shape[1], width)
    fits = grad[0] <= 1024
    out = pl.pallas_call(
        functools.partial(mix_back_body, layout_of(groups)),
        grid=(rows,),
        in_specs=ffn_specs(groups, acts, [0, 1], size, 0)
        + pieces_of(mixed.shape, size)[0]
        + [col, pl.BlockSpec((1, width, size), lambda r: (r, 0, 0)), head_col]
        + picked(w, 1)
        + [whole(place.shape), whole(home.shape), whole(gain.shape)],
        out_specs=[col, head_col, whole((width, 128))] + [whole(grad)] * fits,
        out_shape=[
            jax.ShapeDtypeStruct((width, here), F32),
            jax.ShapeDtypeStruct((inner, here), BF16),
            jax.ShapeDtypeStruct((width, 128), F32),
        ]
        + [jax.ShapeDtypeStruct(grad, BF16)] * fits,
        scratch_shapes=[pltpu.VMEM(grad, F32)] * fits + ffn_scratch(groups, [0, 1]),
        compiler_params=PARAMS,
        name="mix_back",
        cost_estimate=cost(1, 1),
    )(*flat_of(groups), *acts, *d1, mixed, dy, ot, *w, place, home, gain)
    if not fits:
        spread = dot(home, ot, 0, 0).astype(BF16)
        out = [*out, dot(spread, out[0].astype(BF16), 1, 1).astype(BF16)]
    return out


def grads_body(per, groups, parts, n_ref, *refs):
    d_refs, refs = refs[:groups], refs[groups:]
    places, refs = refs[: len(parts)], refs[len(parts) :]
    outs, (acc, d_scr) = refs[: 2 * len(parts)], refs[2 * len(parts) :]
    row = pl.program_id(0)
    n = n_ref[...]
    for g, d_ref in enumerate(d_refs):

        @pl.when(row // per == g)
        def _():
            d_scr[...] = d_ref[...].reshape(d_scr.shape)

    products = []
    for (start, stop), p_ref in zip(parts, places):
        spread = dot(p_ref[...], d_scr[start:stop], 0, 0).astype(BF16)
        products.append(dot(spread, n, 1, 1))

    @pl.when(row == 0)
    def _():
        for j, product in enumerate(products):
            acc[j] = product

    @pl.when(row > 0)
    def _():
        for j, product in enumerate(products):
            acc[j] += product

    @pl.when(row == pl.num_programs(0) - 1)
    def _():
        half = acc.shape[1] // 2
        for j in range(len(parts)):
            outs[2 * j][...] = acc[j, :half].astype(BF16)
            outs[2 * j + 1][...] = acc[j, half:].astype(BF16)


def projection_grads(n, groups, parts, places, rows):
    if len(parts) > 1 and places[0].shape[1] > 1024:
        return [
            half
            for part, p in zip(parts, places)
            for half in projection_grads(n, groups, [part], [p], rows)
        ]
    width, here = n.shape
    size = here // rows
    per = rows // len(groups)
    rank = groups[0].ndim
    depth = groups[0].shape[-2]
    shape = (depth, size) if rank == 2 else (1, depth, size)
    wide = (places[0].shape[1], width)
    return pl.pallas_call(
        functools.partial(grads_body, per, len(groups), parts),
        grid=(rows,),
        in_specs=[pl.BlockSpec((width, size), lambda r: (0, r))]
        + group_specs(shape, len(groups), per, rank)
        + [whole(p.shape) for p in places],
        out_specs=[whole((wide[0] // 2, width))] * (2 * len(parts)),
        out_shape=[jax.ShapeDtypeStruct((wide[0] // 2, width), BF16)] * (2 * len(parts)),
        scratch_shapes=[pltpu.VMEM((len(parts),) + wide, F32), pltpu.VMEM((depth, size), BF16)],
        compiler_params=PARAMS,
        name="projection_grads",
        cost_estimate=cost(
            2 * len(parts) * wide[0] * width * here, 2 * n.size + 2 * len(parts) * wide[0] * width
        ),
    )(n, *groups, *places)


def last_body(per, groups, x_ref, dm_ref, *refs):
    dq_refs, dkv_refs, refs = refs[:groups], refs[groups : 2 * groups], refs[2 * groups :]
    ws, places, refs = (refs[:2], refs[2:4], refs[4:6]), refs[6:9], refs[9:]
    gain_ref, gx_ref, gg_ref, d_scr = refs
    row = pl.program_id(0)
    inner = dq_refs[0].shape[0]
    for g in range(groups):

        @pl.when(row // per == g)
        def _():
            d_scr[:inner] = dq_refs[g][...]
            d_scr[inner:] = dkv_refs[g][0, : 2 * inner]

    dn = None
    for j in range(3):
        spread = dot(places[j][...], d_scr[j * inner : (j + 1) * inner], 0, 0).astype(BF16)
        term = back(ws[j], spread)
        dn = term if dn is None else dn + term
    x = x_ref[0].astype(F32)
    scale = lax.rsqrt(jnp.mean(x * x, axis=0, keepdims=True) + NORM_EPSILON)
    unit = x * scale
    scaled = dn * gain_ref[...]
    inside = jnp.mean(scaled * unit, axis=0, keepdims=True)
    gx_ref[0] = dm_ref[...] + scale * (scaled - unit * inside)
    both = dn * unit
    gain_part = both[:, :128]
    for j in range(1, both.shape[1] // 128):
        gain_part = gain_part + both[:, j * 128 : (j + 1) * 128]

    @pl.when(row == 0)
    def _():
        gg_ref[...] = gain_part

    @pl.when(row > 0)
    def _():
        gg_ref[...] += gain_part


def last(x, dmixed, dqs, dkvs, ws, places, gain):
    rows, width, size = x.shape
    inner = dqs[0].shape[0]
    per = rows // len(dqs)
    col = pl.BlockSpec((width, size), lambda r: (0, r))
    block = pl.BlockSpec((1, width, size), lambda r: (r, 0, 0))
    return pl.pallas_call(
        functools.partial(last_body, per, len(dqs)),
        grid=(rows,),
        in_specs=[block, col]
        + group_specs((inner, size), len(dqs), per, 2)
        + group_specs((1,) + dkvs[0].shape[1:], len(dkvs), per, 3)
        + [spec for w, index in zip(ws, (1, 0, 0)) for spec in picked(w, index)]
        + [whole(p.shape) for p in places]
        + [whole(gain.shape)],
        out_specs=[block, whole((width, 128))],
        out_shape=[jax.ShapeDtypeStruct(x.shape, F32), jax.ShapeDtypeStruct((width, 128), F32)],
        scratch_shapes=[pltpu.VMEM((3 * inner, size), BF16)],
        compiler_params=PARAMS,
        name="last",
        cost_estimate=cost(1, 1),
    )(x, dmixed, *dqs, *dkvs, *[w for pair in ws for w in pair], *places, gain)


def after(value, *markers):
    return lax.optimization_barrier((value, markers))[0]


def pad_rows(w, rows):
    return jnp.pad(w, ((0, rows - w.shape[0]), (0, 0))) if rows > w.shape[0] else w


class Links:
    def __init__(self, dp, pairs):
        self.sizes = {"dp": dp, "x": pairs, "core": 2}
        self.strides = {"dp": 2 * pairs, "x": 2, "core": 1}
        self.core = ("core", 1)
        self.across = ("x", 1)
        self.near = ("dp", 1)
        self.far_count = dp // 2

    def swap(self, x, step):
        axis, mask = step
        return lax.ppermute(x, axis, [(i, i ^ mask) for i in range(self.sizes[axis])])

    def far_steps(self):
        return [("dp", k << 1) for k in range(1, self.far_count)]

    def far_bits(self):
        return [("dp", 2 << b) for b in range(self.far_count.bit_length() - 1)]

    def masks(self, steps):
        found = [(k << 1) * self.strides["dp"] for k in range(self.far_count)]
        for axis, mask in steps:
            found = found + [f ^ (mask * self.strides[axis]) for f in found]
        return found


def per_device(
    dp, ctx,
    tokens, soft_mask, segment_ids, buckets, gain_attn, gain_ffn, bias_table,
    w_query, w_key, w_value, w_attn_out, w_gate, w_up, w_ffn_out, cotangent,
):
    links = Links(dp, ctx // 2)
    swap, core, across, near = links.swap, links.core, links.across, links.near
    far = links.far_steps()
    rows, size, width = tokens.shape
    here = rows * size
    count, heads = bias_table.shape
    inner = heads * HEAD
    my_dp, my_ctx = lax.axis_index("dp"), lax.axis_index("x") * 2 + lax.axis_index("core")
    me = my_dp * ctx + my_ctx
    tile = min(512, here)
    order_a, order_b = [near, across], [across, near]

    def spread_of(steps):
        real = w_query.shape[0]
        owners = me ^ jnp.asarray(links.masks(steps), dtype=jnp.int32)
        inside = jnp.arange(each)
        feature = owners[:, None] * real + inside[None, :]
        feature = jnp.where(inside[None, :] < real, feature, -1).reshape(-1)
        return (jnp.arange(inner)[:, None] == feature[None, :]).astype(BF16)

    token = []

    def run(work, *args):
        if token:
            args = lax.optimization_barrier((args, tuple(token)))[0]
        out = work(*args)
        token[:] = jax.tree.leaves(out)
        return out

    each = -(-w_query.shape[0] // ROW_TILE) * ROW_TILE
    slot = lambda w: pad_rows(w, each)[None]
    flat = lambda w: w.reshape(-1, width)
    far_bits = links.far_bits()
    ab, ba = (near, across), (across, near)

    def exchange(arrays, steps):
        return [(a, swap(a, step)) for a, step in zip(arrays, steps)]

    def swap_core(value):
        return [swap(v, core) for v in value]

    def close(value):
        return run(lambda v: v, value)

    class Gather:
        def __init__(self, array, cuts, direct=False, mark=None, paths=(ab, ba)):
            if mark is not None:
                array = after(array, mark)
            self.cuts, self.stage, self.paths = cuts, 0, paths
            self.hops = 1 if direct else len(far_bits)
            steps = far if direct else far_bits[:1]
            self.held = [array] + [swap(array, step) for step in steps]

        def go(self):
            self.stage += 1
            if self.stage < self.hops:
                (array,) = run(lambda *p: join([p]), *self.held)
                self.held = [array, swap(array, far_bits[self.stage])]
            elif self.stage == self.hops:
                parts = run(lambda *p: cut_join(list(p), self.cuts), *self.held)
                self.held = exchange(parts, self.paths[0])
            elif self.stage == self.hops + 1:
                self.held = exchange(run(join, self.held), self.paths[1])

        def start_of(self):
            first = self.held[0]
            return first[0] if isinstance(first, tuple) else first

        def core_go(self):
            self.held = exchange(run(join, self.held), (core, core))

        def core_end(self):
            return close([list(pair) for pair in self.held])

    attn_w = Gather(
        jnp.concatenate([slot(w) for w in (w_key, w_attn_out, w_value, w_query)], axis=1)[:, None],
        [(0, 2 * each), (2 * each, 2 * each)],
        direct=True,
    )
    units = -(-w_gate.shape[0] // ROW_TILE)
    ffn_own = after((w_gate, w_up, w_ffn_out), attn_w.held[0])
    padded = [pad_rows(w, units * ROW_TILE) for w in ffn_own]
    marks = [0, 3, 5, 7] if units == 7 else list(range(units + 1))
    shards = [
        jnp.stack([w[low * ROW_TILE : high * ROW_TILE] for w in padded])
        for low, high in zip(marks, marks[1:])
    ]
    same_core = ("dp", "x")
    by_hops = units == 7
    last_group = len(shards) - 1

    x = jnp.transpose(tokens, (0, 2, 1))
    dy = jnp.transpose(cotangent, (0, 2, 1))
    gain_one, gain_two = gain_attn[:, None], gain_ffn[:, None]
    place_a, place_b = spread_of(order_a + [core]), spread_of(order_b + [core])
    real = w_query.shape[0]
    segs = lax.dynamic_slice_in_dim(segment_ids, my_ctx * size, size, 1)
    same = segs[:, None, :] == jnp.arange(DOCS, dtype=segs.dtype)[None, :, None]
    ones = jnp.ones((rows, 1, size), BF16)
    rest = AUG - 1 - DOCS
    aug = jnp.concatenate(
        [soft_mask[:, None, :], same.astype(BF16)] + [ones] * 3
        + [jnp.zeros((rows, rest - 3, size), BF16)],
        axis=1,
    )
    query_aug = jnp.concatenate(
        [ones, jnp.where(same, 0.0, MASK_VALUE).astype(BF16), jnp.zeros((rows, rest, size), BF16)],
        axis=1,
    )
    normed, dy_pair, *dy_own = run(first_norm, x, dy, gain_one)
    place_a, place_b, aug, query_aug, shards = close((place_a, place_b, aug, query_aug, shards))

    attn_w.go()
    ffn_w = [
        [lax.all_gather(after(shard, attn_w.start_of()), same_core)]
        for shard in (shards[:-1] if by_hops else shards)
    ]
    slots = jnp.array([0, 2, 1, 3], jnp.int32) ^ my_ctx
    bias, buckets_t = run(
        bias_of, slots, buckets, jnp.pad(bias_table.T, ((0, 0), (0, 128 - count)))
    )
    dy_parts = swap_core(dy_own)
    attn_w.go()
    if by_hops:
        last_w = Gather(
            shards[-1][None],
            [(0, shards[-1].shape[1])],
            mark=attn_w.start_of(),
            paths=((near,), (across,)),
        )
    dy_pair = run(fill, dy_pair, dy_parts)
    if by_hops:
        last_w.go()
    attn_w.core_go()
    wko, wvq = attn_w.core_end()
    kv_own = run(lambda *a: key_value(*a, 0, rows), normed, wko, wvq, place_a, place_b, aug)
    kv_across = swap(kv_own, across)
    kv_core = swap(kv_own, core)
    queries = run(lambda n, w, p: project(n, w, p, tile), normed, wvq, place_b)
    kv_core = close(kv_core)
    if by_hops:
        last_w.go()

    kv = run(lambda *k: list(k), kv_own, kv_across, kv_core)
    kv.append(close(jnp.concatenate([swap(k, core) for k in jnp.split(kv[1], min(2, rows))])))
    attended, lse = run(lambda *a: attend(*a, heads, 0), queries, query_aug, kv, bias)
    if by_hops:
        last_w.go()
    mixed, n_pair, *normed_two = run(mix, x, attended, wko, place_a, gain_two)
    n_parts = close(swap_core(normed_two))
    n_pair = run(fill, n_pair, n_parts)

    class Sums:
        def __init__(self, grads, paths, direct=False):
            self.paths, self.direct = paths[: len(grads)], direct
            self.stage = 0
            self.send(grads)

        def send(self, halves):
            self.keep = [h[0] for h in halves]
            self.got = [swap(h[1], p[self.stage]) for h, p in zip(halves, self.paths)]

        def go(self):
            near_hops = len(self.paths[0])
            hops = near_hops + (1 if self.direct else len(far_bits))
            self.stage += 1
            if self.stage > hops:
                return
            if self.stage < near_hops:
                self.send(run(add_halves, self.keep, self.got))
                return
            if self.stage == near_hops:
                rows_of = [k.shape[-2] for k in self.keep]
                self.edges = [sum(rows_of[:k]) for k in range(len(rows_of) + 1)]
                if self.direct:
                    piles = run(lambda k, r: add_piles(k, r, self.edges), self.keep, self.got)
                    self.keep = [piles[0]]
                    self.got = [swap(pile, step) for pile, step in zip(piles[1:], far)]
                    return
                halves = run(lambda k, r: add_merge(k, r, self.edges), self.keep, self.got)
            elif self.stage < hops:
                halves = run(add_halves, self.keep, self.got)[0]
            else:
                got = after(self.got, *token)
                self.out = add_last(self.keep[0], got, self.edges)
                return
            self.keep = [halves[0]]
            self.got = [swap(halves[1], far_bits[hops - 1 - self.stage])]

    acts, sums = [], []
    me_same = (my_dp * (ctx // 2) + lax.axis_index("x")).reshape(1)
    masks = [[m >> 1 for m in links.masks(steps)] for steps in (ab, ba)]
    ffn_grads = {}
    if by_hops:
        ffn_w.append(None)
    sequence = [0, 2, 1] if by_hops else range(len(ffn_w))
    by_group = {}
    for i in sequence:
        ws = ffn_w[i]
        if i == last_group and by_hops:
            ws = ffn_w[i] = last_ws
        some = tile if units_of(ws) <= 768 else tile // 2
        mask = masks[1] if by_hops and i == last_group - 1 else None
        act, grads = run(
            lambda m, w, n, d: ffn_group(m, w, n, d, some, mask), me_same, ws, n_pair, dy_pair
        )
        by_group[i] = act
        if by_hops and i == 0:
            last_ws = close(list(last_w.held[0]))
            grads = [after(g, last_ws) for g in grads]
        ffn_grads[i] = grads if by_hops and i else lax.psum_scatter(grads[0], same_core)
    ffn_grads = [ffn_grads[i] for i in range(len(ffn_w))]
    acts = [by_group[i] for i in range(len(ffn_w))]
    if by_hops:
        sums = [Sums(ffn_grads[-2:], [ab, ba])]

    def tick():
        for s in sums:
            s.go()

    back = run(lambda p, a: ffn_back(p, a, [0, 1], here, here, tile, PIECES), ffn_w, acts)
    dn_got = swap_core(back)
    (out_other,) = run(lambda p, a: ffn_back(p, a, [2], here, here, tile, 1), ffn_w, acts)
    dn_got = close(dn_got)
    out_got = swap(out_other, core)

    dmixed, dattended, gain_two_part, gwo = run(
        mix_back, ffn_w, acts, mixed, dn_got, dy, attended, wko, place_a, place_b, gain_two
    )
    tick()
    out_got = close(out_got)
    dq, dkv, grad_bias = run(
        lambda *a: attend_back(*a, heads, 0, []),
        queries, query_aug, kv, bias, attended, dattended, lse,
    )
    by_core = [(dkv[0], swap(dkv[2], core)), (dkv[1], swap(dkv[3], core))]
    tick()
    entries = lambda g: tuple(v.reshape(-1, each, width) for v in g)
    home_a, home_b = (core,) + ba, (core,) + ab
    own, other = run(add_pairs, by_core)
    other = swap(other, across)
    gwq = run(
        lambda n, d, p: projection_grads(n, [d], [(0, inner)], [p], rows), normed, dq, place_b
    )
    if by_hops:
        ffn_grads[0] = close(ffn_grads[0])
    part = gwo.shape[0] // 2
    query_sum = Sums([entries((gwo[:part], gwo[part:])), entries(gwq)], [home_b, home_b])
    grad_table = run(lambda g, b: bucket_sums(g, b, count), grad_bias, buckets_t)
    query_sum.go()
    out = run(lambda *a: layer_out_of(*a, rows), ffn_w, acts, mixed, out_got)
    query_sum.go()
    (dkv,) = run(add_pairs, [(own, other)])
    gkv = run(
        lambda n, d, pa, pb: projection_grads(n, [d], [(0, inner), (inner, 2 * inner)], [pa, pb], rows),
        normed, dkv, place_a, place_b,
    )
    value_sum = Sums([entries(gkv[:2]), entries(gkv[2:])], [home_a, home_b], direct=dp <= 8)
    tick()
    query_sum.go()
    value_sum.go()
    gx, gain_one_part = run(
        lambda *a: last(a[0], a[1], [a[2]], [a[3]], a[4:7], a[7:10], a[10]),
        x, dmixed, dq, dkv, wvq, wko, wvq, place_b, place_a, place_b, gain_one,
    )
    value_sum.go()
    tick()
    query_sum.go()
    small = jnp.concatenate(
        [jnp.sum(gain_one_part, 1), jnp.sum(gain_two_part, 1), grad_table.reshape(-1)]
    )
    length = small.shape[0]
    small = jnp.pad(small, (0, -length % 1024)).reshape(-1, 128)
    bits = [core, across] + [("dp", 1 << b) for b in range(dp.bit_length() - 1)]
    for k, one in enumerate(bits):
        got = swap(small, one)
        if k == 1:
            value_sum.go()
        if k == 3:
            value_sum.got = close(value_sum.got)
        small = run(lambda a, b: a + b, small, got)
    for _ in range(len(far_bits) + 4):
        for s in [query_sum, value_sum] + sums:
            s.go()
    small = small.reshape(-1)
    if by_hops:
        ffn_grads[-2:] = sums[0].out
    grad_gate, grad_up, grad_ffn_out = (
        jnp.concatenate([g[j].astype(F32) for g in ffn_grads])[: w_gate.shape[0]] for j in range(3)
    )
    return (
        jnp.transpose(out, (0, 2, 1)),
        jnp.transpose(gx, (0, 2, 1)),
        dkv[:, 2 * inner].astype(F32),
        small[:width],
        small[width : 2 * width],
        small[2 * width : length].reshape(count, heads),
        query_sum.out[1][:real],
        value_sum.out[0][:real],
        value_sum.out[1][:real],
        query_sum.out[0][:real],
        grad_gate,
        grad_up,
        grad_ffn_out,
    )


def solution(mesh):
    dp, ctx = mesh.shape["dp"], mesh.shape["ctx"]
    by_core = Mesh(mesh.devices.reshape(dp, ctx // 2, 2), ("dp", "x", "core"))
    ctx_axes = ("x", "core")
    split = P(("dp", "x", "core"), None)
    act = P("dp", ctx_axes, None)
    in_specs = (
        (act, P("dp", ctx_axes), P("dp", None), P(ctx_axes, None), P(), P(), P()) + (split,) * 7 + (act,)
    )
    out_specs = (act, act, P("dp", ctx_axes), P(), P(), P()) + (split,) * 7
    return jax.shard_map(
        functools.partial(per_device, dp, ctx),
        mesh=by_core,
        in_specs=in_specs,
        out_specs=out_specs,
        check_vma=False,
    )
```

```python
import functools

import jax
import jax.numpy as jnp
import numpy as np
from jax import lax
from jax.experimental import pallas as pl
from jax.experimental.pallas import tpu as pltpu
from jax.sharding import Mesh, PartitionSpec as P

NORM_EPSILON = 1e-06
MASK_VALUE = -1e30
F32, BF16 = jnp.float32, jnp.bfloat16
HEAD = 64
ROW_TILE = 16
AUG = 16
DOCS = 5
ONES = 1 + DOCS
VMEM_LIMIT = 58 * 1024 * 1024
PARAMS = pltpu.CompilerParams(vmem_limit_bytes=VMEM_LIMIT)


def dot(a, b, ca, cb):
    return lax.dot_general(a, b, (((ca,), (cb,)), ((), ())), preferred_element_type=F32)


def whole(shape):
    return pl.BlockSpec(shape, lambda t: (0,) * len(shape), pipeline_mode=pl.Buffered(1))


def cost(flops, nbytes):
    return pl.CostEstimate(flops=1, bytes_accessed=1, transcendentals=0)


ANY = pl.BlockSpec(memory_space=pl.ANY)


def join(pairs):
    return [jnp.concatenate(list(pair), axis=0) for pair in pairs]


def cut_join(parts, cuts):
    out = []
    for cut in cuts:
        at = np.s_[:, :, cut[0] : cut[0] + cut[1]] if isinstance(cut, tuple) else np.s_[:, cut]
        out.append(jnp.concatenate([p[at] for p in parts], axis=0))
    return out


def fill(pair, parts):
    start = 0
    for part in parts:
        pair = pair.at[1, start : start + part.shape[0]].set(part)
        start += part.shape[0]
    return pair


def add_halves(keep, got):
    out = []
    for k, r in zip(keep, got):
        part = k.shape[0] // 2
        out.append((k[:part] + r[:part], k[part:] + r[part:]))
    return out


def add_merge(keep, got, edges):
    part = keep[0].shape[0] // 2
    ends = [slice(None, part), slice(part, None)]
    return [jnp.concatenate([k[e] + r[e] for k, r in zip(keep, got)], axis=-2) for e in ends]


def add_piles(keep, got, edges):
    return [
        jnp.concatenate([k[i : i + 1] + r[i : i + 1] for k, r in zip(keep, got)], axis=-2)
        for i in range(keep[0].shape[0])
    ]


def add_last(keep, got, edges):
    total = keep[0].astype(F32)
    for r in got:
        total = total + r[0].astype(F32)
    return [total[..., a:b, :] for a, b in zip(edges, edges[1:])]


def add_pairs(pairs):
    return [a + b for a, b in pairs]


PIECES = 2


def pieces_of(shape, tile, pieces=PIECES):
    rows, columns = shape
    piece = (rows // pieces, columns)
    specs = [pl.BlockSpec((piece[0], tile), lambda t: (0, t)) for _ in range(pieces)]
    return specs, [jax.ShapeDtypeStruct(piece, BF16)] * pieces


def put_pieces(refs, value):
    step = refs[0].shape[0]
    for k, ref in enumerate(refs):
        ref[...] = value[k * step : (k + 1) * step]


def norm_body(x_ref, dy_ref, gain_ref, n_ref, pair_ref, *piece_refs):
    x = x_ref[0].astype(F32)
    scale = lax.rsqrt(jnp.mean(x * x, axis=0, keepdims=True) + NORM_EPSILON)
    n_ref[...] = (x * scale * gain_ref[...]).astype(BF16)
    pair_ref[0] = dy_ref[0]
    put_pieces(piece_refs, dy_ref[0])


def first_norm(x, dy, gain):
    rows, width, size = x.shape
    block = pl.BlockSpec((1, width, size), lambda r: (r, 0, 0))
    col = pl.BlockSpec((width, size), lambda r: (0, r))
    here = rows * size
    piece_specs, piece_shapes = pieces_of((width, here), size)
    return pl.pallas_call(
        norm_body,
        grid=(rows,),
        in_specs=[block, block, whole(gain.shape)],
        out_specs=[col, pl.BlockSpec((1, width, size), lambda r: (0, 0, r))] + piece_specs,
        out_shape=[
            jax.ShapeDtypeStruct((width, here), BF16),
            jax.ShapeDtypeStruct((2, width, here), BF16),
        ]
        + piece_shapes,
        compiler_params=PARAMS,
        name="first_norm",
        cost_estimate=cost(4 * x.size, 10 * x.size),
    )(x, dy, gain)


def picked(pair, index):
    return [
        pl.BlockSpec(
            (w.shape[0], 1, w.shape[2] // 2, w.shape[3]),
            lambda t: (0, 0, index, 0),
            pipeline_mode=pl.Buffered(1),
        )
        for w in pair
    ]


def flat_rows(w_ref):
    entries, _, each, width = w_ref.shape
    return w_ref[...].reshape(entries * each, width)


def forth(refs, x):
    return jnp.concatenate([dot(flat_rows(w), x, 1, 0).astype(BF16) for w in refs], axis=0)


def back(refs, x):
    part = x.shape[0] // 2
    return dot(flat_rows(refs[0]), x[:part], 0, 0) + dot(flat_rows(refs[1]), x[part:], 0, 0)


def key_value_body(inner, n_ref, wk0, wk1, wv0, wv1, pk_ref, pv_ref, aug_ref, out_ref):
    n = n_ref[...]
    for start, refs, p_ref in ((0, (wk0, wk1), pk_ref), (inner, (wv0, wv1), pv_ref)):
        out_ref[0, start : start + inner] = dot(p_ref[...], forth(refs, n), 1, 0).astype(BF16)
    out_ref[0, 2 * inner :] = aug_ref[0]


def key_value(n, wk, wv, place_k, place_v, aug, first, rows):
    size = aug.shape[2]
    inner = place_k.shape[0]
    width = n.shape[0]
    return pl.pallas_call(
        functools.partial(key_value_body, inner),
        grid=(rows,),
        in_specs=[pl.BlockSpec((width, size), lambda r: (0, first + r))]
        + picked(wk, 0)
        + picked(wv, 0)
        + [
            whole(place_k.shape),
            whole(place_v.shape),
            pl.BlockSpec((1, AUG, size), lambda r: (first + r, 0, 0)),
        ],
        out_specs=pl.BlockSpec((1, 2 * inner + AUG, size), lambda r: (r, 0, 0)),
        out_shape=jax.ShapeDtypeStruct((rows, 2 * inner + AUG, size), BF16),
        compiler_params=PARAMS,
        name="key_value",
        cost_estimate=cost(1, 1),
    )(n, *wk, *wv, place_k, place_v, aug)


def project_body(n_ref, w0, w1, p_ref, out_ref):
    out_ref[...] = dot(p_ref[...], forth((w0, w1), n_ref[...]), 1, 0).astype(BF16)


def project(n, w, place, tile):
    width, here = n.shape
    inner = place.shape[0]
    return pl.pallas_call(
        project_body,
        grid=(here // tile,),
        in_specs=[pl.BlockSpec((width, tile), lambda t: (0, t))] + picked(w, 1) + [whole(place.shape)],
        out_specs=pl.BlockSpec((inner, tile), lambda t: (0, t)),
        out_shape=jax.ShapeDtypeStruct((inner, here), BF16),
        compiler_params=PARAMS,
        name="project",
        cost_estimate=cost(1, 1),
    )(n, *w, place)


def attend_body(heads, inner, q_ref, u_ref, *refs):
    *blocks, bias_ref, o_ref, lse_ref, s_ref = refs
    for h in range(heads):
        part = slice(h * HEAD, (h + 1) * HEAD)
        q = jnp.concatenate([q_ref[part], u_ref[0]], axis=0)
        top = None
        for s, k_ref in enumerate(blocks):
            k = jnp.concatenate([k_ref[0, part], k_ref[0, 2 * inner :]], axis=0)
            logits = dot(k, q, 0, 0) + bias_ref[h, s]
            s_ref[s] = logits
            peak = jnp.max(logits, axis=0, keepdims=True)
            top = peak if top is None else jnp.maximum(top, peak)
        total, out = None, None
        for s, k_ref in enumerate(blocks):
            e = jnp.exp(s_ref[s] - top)
            part_sum = jnp.sum(e, axis=0, keepdims=True)
            total = part_sum if total is None else total + part_sum
            value = k_ref[0, slice(inner + h * HEAD, inner + (h + 1) * HEAD)]
            term = dot(value, e.astype(BF16), 1, 0)
            out = term if out is None else out + term
        o_ref[part] = (out / total).astype(BF16)
        lse_ref[0, h : h + 1] = top + jnp.log(total)
    pad = lse_ref.shape[1] - heads
    if pad:
        lse_ref[0, heads:] = jnp.zeros((pad, lse_ref.shape[2]), F32)


def attend(qt, u, kv, bias, heads, first):
    rows, depth, size = kv[0].shape
    inner = heads * HEAD
    pad = -(-heads // 8) * 8
    return pl.pallas_call(
        functools.partial(attend_body, heads, inner),
        grid=(rows,),
        in_specs=[
            pl.BlockSpec((inner, size), lambda r: (0, first + r)),
            pl.BlockSpec((1, AUG, size), lambda r: (first + r, 0, 0)),
        ]
        + [pl.BlockSpec((1, depth, size), lambda r: (r, 0, 0))] * len(kv)
        + [whole(bias.shape)],
        out_specs=[
            pl.BlockSpec((inner, size), lambda r: (0, r)),
            pl.BlockSpec((1, pad, size), lambda r: (r, 0, 0)),
        ],
        out_shape=[
            jax.ShapeDtypeStruct((inner, rows * size), BF16),
            jax.ShapeDtypeStruct((rows, pad, size), F32),
        ],
        scratch_shapes=[pltpu.VMEM((len(kv), size, size), F32)],
        compiler_params=PARAMS,
        name="attend",
        cost_estimate=cost(16 * rows * heads * len(kv) * size * size * HEAD, 40_000_000),
    )(qt, u, *kv, bias)


def three(x):
    a = x.astype(BF16).astype(F32)
    rest = x - a
    b = rest.astype(BF16).astype(F32)
    return a, b, rest - b


def attend_back_body(heads, inner, count, more, q_ref, u_ref, *refs):
    blocks = refs[:count]
    bias_ref, o_ref, do_ref, lse_ref = refs[count : count + 4]
    refs = refs[count + 4 :]
    before_ref, refs = (refs[0], refs[1:]) if more else (None, refs)
    dq_ref = refs[0]
    grads = refs[1 : count + 1]
    gb_ref = refs[count + 1]
    size = bias_ref.shape[3]
    row = pl.program_id(0)
    mask_grad = [None] * count
    extra = u_ref[0].astype(F32)
    place = lax.broadcasted_iota(jnp.int32, (AUG, size), 0)

    def pick(parts, base):
        for i, value in enumerate(parts):
            base = jnp.where(place == ONES + i, value, base)
        return base.astype(BF16)

    for h in range(heads):
        part = slice(h * HEAD, (h + 1) * HEAD)
        vpart = slice(inner + h * HEAD, inner + (h + 1) * HEAD)
        q = q_ref[part]
        do = do_ref[part]
        delta = jnp.sum(do.astype(F32) * o_ref[part].astype(F32), axis=0, keepdims=True)
        q_aug = jnp.concatenate([q, pick(three(-lse_ref[0, h : h + 1]), extra)], axis=0)
        do_aug = jnp.concatenate([do, pick(three(-delta), jnp.zeros_like(extra))], axis=0)
        dq = None
        for s, k_ref in enumerate(blocks):
            k = k_ref[0, part]
            aug = k_ref[0, 2 * inner :]
            logits = dot(jnp.concatenate([k, aug], axis=0), q_aug, 0, 0) + bias_ref[h, s]
            p = jnp.exp(logits)
            dp = dot(jnp.concatenate([k_ref[0, vpart], aug], axis=0), do_aug, 0, 0)
            ds = p * dp

            @pl.when(row == 0)
            def _():
                gb_ref[h, s] = before_ref[h, s] + ds if more else ds

            @pl.when(row > 0)
            def _():
                gb_ref[h, s] += ds

            low = ds.astype(BF16)
            grads[s][0, vpart] = dot(do, p.astype(BF16), 1, 1).astype(BF16)
            both = dot(q_aug, low, 1, 1)
            grads[s][0, part] = both[:HEAD].astype(BF16)
            g = both[HEAD : HEAD + 1]
            mask_grad[s] = g if mask_grad[s] is None else mask_grad[s] + g
            term = dot(k, low, 1, 0)
            dq = term if dq is None else dq + term
        dq_ref[part] = dq.astype(BF16)
    for s in range(count):
        grads[s][0, 2 * inner :] = jnp.broadcast_to(mask_grad[s], (AUG, size)).astype(BF16)


def attend_back(qt, u, kv, bias, ot, dot_t, lse, heads, first, before):
    rows, depth, size = kv[0].shape
    inner = heads * HEAD
    count = len(kv)
    own = pl.BlockSpec((inner, size), lambda r: (0, r))
    col = pl.BlockSpec((inner, size), lambda r: (0, first + r))
    block = pl.BlockSpec((1, depth, size), lambda r: (r, 0, 0))
    out = pl.pallas_call(
        functools.partial(attend_back_body, heads, inner, count, len(before)),
        grid=(rows,),
        in_specs=[col, pl.BlockSpec((1, AUG, size), lambda r: (first + r, 0, 0))]
        + [block] * count
        + [whole(bias.shape), own, col]
        + [pl.BlockSpec((1,) + lse.shape[1:], lambda r: (r, 0, 0))]
        + [whole(b.shape) for b in before],
        out_specs=[own] + [block] * count + [whole(bias.shape)],
        out_shape=[jax.ShapeDtypeStruct((inner, rows * size), BF16)]
        + [jax.ShapeDtypeStruct((rows, depth, size), BF16)] * count
        + [jax.ShapeDtypeStruct(bias.shape, F32)],
        compiler_params=PARAMS,
        name="attend_back",
        cost_estimate=cost(40 * rows * heads * count * size * size * HEAD, 60_000_000),
    )(qt, u, *kv, bias, ot, dot_t, lse, *before)
    return out[0], out[1:-1], out[-1]


def bias_body(heads, slots_ref, buckets_ref, table_ref, bias_ref, buckets_t_ref):
    tables = [jnp.broadcast_to(table_ref[h : h + 1], (8, 128)) for h in range(heads)]
    buckets_t_ref[0] = buckets_ref[...].T
    for i in range(buckets_ref.shape[1] // 8):
        for j in range(buckets_ref.shape[0] // 128):
            at = (slice(i * 8, (i + 1) * 8), slice(j * 128, (j + 1) * 128))
            index = buckets_t_ref[(0,) + at]
            for h in range(heads):
                bias_ref[(h, 0) + at] = jnp.take_along_axis(tables[h], index, axis=1)


def bias_of(slots, buckets, table):
    heads = table.shape[0]
    size, blocks = buckets.shape[0], slots.shape[0]
    spec = pltpu.PrefetchScalarGridSpec(
        num_scalar_prefetch=1,
        grid=(blocks,),
        in_specs=[
            pl.BlockSpec((size, size), lambda s, slots: (0, slots[s])),
            pl.BlockSpec(table.shape, lambda s, slots: (0, 0)),
        ],
        out_specs=[
            pl.BlockSpec((heads, 1, size, size), lambda s, slots: (0, s, 0, 0)),
            pl.BlockSpec((1, size, size), lambda s, slots: (s, 0, 0)),
        ],
    )
    return pl.pallas_call(
        functools.partial(bias_body, heads),
        grid_spec=spec,
        out_shape=[
            jax.ShapeDtypeStruct((heads, blocks, size, size), F32),
            jax.ShapeDtypeStruct((blocks, size, size), jnp.int32),
        ],
        compiler_params=PARAMS,
        name="bias_of",
        cost_estimate=cost(1, 1),
    )(slots, buckets, table)


def sums_body(heads, count, buckets_ref, g_ref, out_ref):
    @pl.when(pl.program_id(0) == 0)
    def _():
        out_ref[...] = jnp.zeros_like(out_ref)

    total = out_ref[...]
    for i in range(buckets_ref.shape[1] // 8):
        at = slice(i * 8, (i + 1) * 8)
        index = buckets_ref[0, at]
        hot = [jnp.where(index == b, 1.0, 0.0) for b in range(count)]
        hot = jnp.concatenate(hot, axis=0).astype(BF16)
        g = jnp.concatenate([g_ref[h, 0, at] for h in range(heads)], axis=0)
        high = g.astype(BF16)
        low = (g - high.astype(F32)).astype(BF16)
        total += dot(jnp.concatenate([high, low], axis=0), hot, 1, 1)
    out_ref[...] = total


def bucket_sums(grad_bias, buckets, count):
    heads, blocks, size, _ = grad_bias.shape
    shape = (2 * heads * 8, count * 8)
    raw = pl.pallas_call(
        functools.partial(sums_body, heads, count),
        grid=(blocks,),
        in_specs=[
            pl.BlockSpec((1, size, size), lambda s: (s, 0, 0)),
            pl.BlockSpec((heads, 1, size, size), lambda s: (0, s, 0, 0)),
        ],
        out_specs=pl.BlockSpec(shape, lambda s: (0, 0)),
        out_shape=jax.ShapeDtypeStruct(shape, F32),
        compiler_params=PARAMS,
        name="bucket_sums",
        cost_estimate=cost(64 * grad_bias.size, 4 * grad_bias.size),
    )(buckets, grad_bias)
    raw = raw.reshape(2, heads, 8, count, 8)
    return jnp.sum(jnp.where(jnp.eye(8, dtype=bool)[None, None, :, None, :], raw, 0.0), (0, 2, 4)).T


def mix_body(x_ref, o_ref, w0, w1, place_ref, gain_ref, mixed_ref, pair_ref, *piece_refs):
    spread = dot(place_ref[...], o_ref[...], 0, 0).astype(BF16)
    mixed = x_ref[0].astype(F32) + back((w0, w1), spread)
    mixed_ref[...] = mixed
    scale = lax.rsqrt(jnp.mean(mixed * mixed, axis=0, keepdims=True) + NORM_EPSILON)
    n = (mixed * scale * gain_ref[...]).astype(BF16)
    pair_ref[0] = n
    put_pieces(piece_refs, n)


def group_specs(shape, count, per, rank):
    def place(g):
        def index(r):
            inside = jnp.clip(r - g * per, 0, per - 1)
            return (0, inside) if rank == 2 else (inside, 0, 0)

        return index

    return [pl.BlockSpec(shape, place(g)) for g in range(count)]


def mix(x, ot, w, place, gain):
    rows, width, size = x.shape
    inner = ot.shape[0]
    here = rows * size
    piece_specs, piece_shapes = pieces_of((width, here), size)
    return pl.pallas_call(
        mix_body,
        grid=(rows,),
        in_specs=[
            pl.BlockSpec((1, width, size), lambda r: (r, 0, 0)),
            pl.BlockSpec((inner, size), lambda r: (0, r)),
        ]
        + picked(w, 1)
        + [whole(place.shape), whole(gain.shape)],
        out_specs=[
            pl.BlockSpec((width, size), lambda r: (0, r)),
            pl.BlockSpec((1, width, size), lambda r: (0, 0, r)),
        ]
        + piece_specs,
        out_shape=[
            jax.ShapeDtypeStruct((width, here), F32),
            jax.ShapeDtypeStruct((2, width, here), BF16),
        ]
        + piece_shapes,
        compiler_params=PARAMS,
        name="mix",
        cost_estimate=cost(1, 1),
    )(x, ot, *w, place, gain)


def units_of(ws):
    return sum(w.shape[0] * w.shape[2] for w in ws)


def entries_of(ws):
    return sum(w.shape[0] for w in ws)


def loads_of(refs, buf, sems, kinds):
    copies, start = [], 0
    for a, ref in enumerate(refs):
        for k, kind in enumerate(kinds):
            inside = buf.at[k, pl.ds(start, ref.shape[0])]
            copies.append(pltpu.make_async_copy(ref.at[:, kind], inside, sems.at[a, k]))
        start += ref.shape[0]
    return copies


def ffn_body(count, masks, me_ref, *refs):
    ws, (n_ref, dy_ref, act_ref), refs = refs[:count], refs[count : count + 3], refs[count + 3 :]
    gs, (buf, acc, in_sems, out_sems) = refs[:-4], refs[-4:]
    t = pl.program_id(0)
    entries, rows, width = buf.shape[1:]
    size = entries * rows
    loads = loads_of(ws, buf, in_sems, range(3))

    @pl.when(t == 0)
    def _():
        for copy in loads:
            copy.start()
        acc[...] = jnp.zeros_like(acc)
        for copy in loads:
            copy.wait()

    norm = n_ref[0]
    dy = dy_ref[0]
    gate = dot(buf[0].reshape(size, width), norm, 1, 0)
    up = dot(buf[1].reshape(size, width), norm, 1, 0)
    dhid = dot(buf[2].reshape(size, width), dy, 1, 0)
    inside = gate * (0.7978845608028654 + 0.035677408136300125 * (gate * gate))
    half = 0.5 + 0.5 * jnp.tanh(inside)
    gelu = gate * half
    slope = half * (1.0 + (1.0 - half) * (6.0 * inside - 3.1915382432114616 * gate))
    dgate = (dhid * up * slope).astype(BF16)
    dup = (dhid * gelu).astype(BF16)
    hidden = (gelu * up).astype(BF16)
    act_ref[0] = dgate
    act_ref[1] = dup
    act_ref[2] = hidden
    acc[0] += dot(dgate, norm, 1, 1)
    acc[1] += dot(dup, norm, 1, 1)
    acc[2] += dot(hidden, dy, 1, 1)

    @pl.when(t == pl.num_programs(0) - 1)
    def _():
        for k in range(3):
            buf[k] = acc[k].astype(BF16).reshape(entries, rows, width)
        stores = []
        if masks is None:
            start = 0
            for g, out in enumerate(gs):
                for k in range(3):
                    inside = buf.at[k, pl.ds(start, out.shape[0])]
                    stores.append(pltpu.make_async_copy(inside, out.at[:, k], out_sems.at[g, k]))
                start += out.shape[0]
        else:
            part = len(masks) // 2
            for s, mask in enumerate(masks):
                for k in range(3):
                    inside, out = buf.at[k, me_ref[0] ^ mask], gs[s // part].at[s % part, k]
                    stores.append(pltpu.make_async_copy(inside, out, out_sems.at[s, k]))
        for copy in stores:
            copy.start()
        for copy in stores:
            copy.wait()


def ffn_group(me, ws, n, dy, tile, masks=None):
    halves, width, tokens = n.shape
    per = tokens // tile
    all_tokens = halves * tokens
    size = units_of(ws)
    inner = (entries_of(ws),) + ws[0].shape[2:]
    column = pl.BlockSpec((1, width, tile), lambda t, me: (t // per, 0, t % per))
    stores = len(ws) if masks is None else len(masks)
    shapes = [w.shape for w in ws]
    if masks is not None:
        shapes = [(inner[0] // 2, 3) + inner[1:]] * 2
    spec = pltpu.PrefetchScalarGridSpec(
        num_scalar_prefetch=1,
        grid=(halves * per,),
        in_specs=[ANY] * len(ws) + [column, column],
        out_specs=[pl.BlockSpec((3, size, tile), lambda t, me: (0, 0, t))] + [ANY] * len(shapes),
        scratch_shapes=[
            pltpu.VMEM((3,) + inner, BF16),
            pltpu.VMEM((3, size, width), F32),
            pltpu.SemaphoreType.DMA((len(ws), 3)),
            pltpu.SemaphoreType.DMA((stores, 3)),
        ],
    )
    out = pl.pallas_call(
        functools.partial(ffn_body, len(ws), masks),
        grid_spec=spec,
        out_shape=[jax.ShapeDtypeStruct((3, size, all_tokens), BF16)]
        + [jax.ShapeDtypeStruct(shape, BF16) for shape in shapes],
        compiler_params=PARAMS,
        name="ffn_group",
        cost_estimate=cost(1, 1),
    )(me, *ws, n, dy)
    return out[0], out[1:]


def ffn_terms(layout, kinds, refs):
    count, total = len(layout), sum(layout)
    ws, acts, refs = refs[:total], refs[total : total + count], refs[total + count :]
    bufs, sems = refs[:count], refs[count]

    @pl.when(pl.program_id(0) == 0)
    def _():
        copies, start = [], 0
        for p, arrays in enumerate(layout):
            copies += loads_of(ws[start : start + arrays], bufs[p], sems.at[p], kinds)
            start += arrays
        for copy in copies:
            copy.start()
        for copy in copies:
            copy.wait()

    out = None
    for act, buf in zip(acts, bufs):
        _, entries, rows, width = buf.shape
        for k in range(len(kinds)):
            term = dot(buf[k].reshape(entries * rows, width), act[k], 0, 0)
            out = term if out is None else out + term
    return out


def layout_of(groups):
    return tuple(len(ws) for ws in groups)


def flat_of(groups):
    return [w for ws in groups for w in ws]


def ffn_specs(groups, acts, kinds, tile, first):
    at = kinds[0] // len(kinds)
    return [ANY] * len(flat_of(groups)) + [
        pl.BlockSpec((len(kinds), a.shape[1], tile), lambda t: (at, 0, first + t)) for a in acts
    ]


def ffn_scratch(groups, kinds):
    return [
        pltpu.VMEM((len(kinds), entries_of(ws)) + ws[0].shape[2:], BF16) for ws in groups
    ] + [pltpu.SemaphoreType.DMA((len(groups), max(layout_of(groups)), len(kinds)))]


def ffn_back_body(layout, kinds, pieces, *refs):
    ins = sum(layout) + len(layout)
    total = ffn_terms(layout, kinds, refs[:ins] + refs[ins + pieces :])
    put_pieces(refs[ins : ins + pieces], total.astype(BF16))


def ffn_back(groups, acts, kinds, start, count, tile, pieces):
    width = groups[0][0].shape[3]
    piece_specs, piece_shapes = pieces_of((width, count), tile, pieces)
    return pl.pallas_call(
        functools.partial(ffn_back_body, layout_of(groups), kinds, pieces),
        grid=(count // tile,),
        in_specs=ffn_specs(groups, acts, kinds, tile, start // tile),
        out_specs=piece_specs,
        out_shape=piece_shapes,
        scratch_shapes=ffn_scratch(groups, kinds),
        compiler_params=PARAMS,
        name="ffn_back",
        cost_estimate=cost(1, 1),
    )(*flat_of(groups), *acts)


def layer_out_body(layout, *refs):
    ins = sum(layout) + len(layout)
    mixed_ref, got_ref, out_ref = refs[ins : ins + 3]
    total = ffn_terms(layout, [2], refs[:ins] + refs[ins + 3 :])
    out_ref[0] = (mixed_ref[...] + total + got_ref[...].astype(F32)).astype(BF16)


def layer_out_of(groups, acts, mixed, got, rows):
    width, here = mixed.shape
    size = here // rows
    col = pl.BlockSpec((width, size), lambda t: (0, t))
    return pl.pallas_call(
        functools.partial(layer_out_body, layout_of(groups)),
        grid=(rows,),
        in_specs=ffn_specs(groups, acts, [2], size, 0) + [col, col],
        out_specs=pl.BlockSpec((1, width, size), lambda t: (t, 0, 0)),
        out_shape=jax.ShapeDtypeStruct((rows, width, size), BF16),
        scratch_shapes=ffn_scratch(groups, [2]),
        compiler_params=PARAMS,
        name="layer_out_of",
        cost_estimate=cost(1, 1),
    )(*flat_of(groups), *acts, mixed, got)


def mix_back_body(layout, *refs):
    ins = sum(layout) + len(layout)
    weights, refs = refs[:ins], refs[ins:]
    pieces, refs = refs[:PIECES], refs[PIECES:]
    mixed_ref, dy_ref, o_ref, w0, w1, place_ref, home_ref, gain_ref = refs[:8]
    refs = refs[8:]
    inside_grad = len(refs) == 5 + len(layout) + 1
    dmixed_ref, do_ref, gg_ref = refs[:3]
    gw_ref, acc = refs[3:5] if inside_grad else (None, None)
    row = pl.program_id(0)
    got = jnp.concatenate([r[...] for r in pieces], axis=0)
    dn = ffn_terms(layout, [0, 1], weights + refs[-len(layout) - 1 :]) + got.astype(F32)
    mixed = mixed_ref[...]
    scale = lax.rsqrt(jnp.mean(mixed * mixed, axis=0, keepdims=True) + NORM_EPSILON)
    unit = mixed * scale
    scaled = dn * gain_ref[...]
    inside = jnp.mean(scaled * unit, axis=0, keepdims=True)
    dmixed = dy_ref[0].astype(F32) + scale * (scaled - unit * inside)
    dmixed_ref[...] = dmixed
    low = dmixed.astype(BF16)
    spread = dot(home_ref[...], o_ref[...], 0, 0).astype(BF16)
    do_ref[...] = dot(place_ref[...], forth((w0, w1), low), 1, 0).astype(BF16)
    both = dn * unit
    gain_part = both[:, :128]
    for j in range(1, both.shape[1] // 128):
        gain_part = gain_part + both[:, j * 128 : (j + 1) * 128]

    @pl.when(row == 0)
    def _():
        gg_ref[...] = gain_part

    @pl.when(row > 0)
    def _():
        gg_ref[...] += gain_part

    if inside_grad:
        product = dot(spread, low, 1, 1)

        @pl.when(row == 0)
        def _():
            acc[...] = product

        @pl.when(row > 0)
        def _():
            acc[...] += product

        @pl.when(row == pl.num_programs(0) - 1)
        def _():
            gw_ref[...] = acc[...].astype(BF16)


def mix_back(groups, acts, mixed, d1, dy, ot, w, place, home, gain):
    rows, width, size = dy.shape
    inner = ot.shape[0]
    here = rows * size
    col = pl.BlockSpec((width, size), lambda r: (0, r))
    head_col = pl.BlockSpec((inner, size), lambda r: (0, r))
    grad = (home.shape[1], width)
    fits = grad[0] <= 1024
    out = pl.pallas_call(
        functools.partial(mix_back_body, layout_of(groups)),
        grid=(rows,),
        in_specs=ffn_specs(groups, acts, [0, 1], size, 0)
        + pieces_of(mixed.shape, size)[0]
        + [col, pl.BlockSpec((1, width, size), lambda r: (r, 0, 0)), head_col]
        + picked(w, 1)
        + [whole(place.shape), whole(home.shape), whole(gain.shape)],
        out_specs=[col, head_col, whole((width, 128))] + [whole(grad)] * fits,
        out_shape=[
            jax.ShapeDtypeStruct((width, here), F32),
            jax.ShapeDtypeStruct((inner, here), BF16),
            jax.ShapeDtypeStruct((width, 128), F32),
        ]
        + [jax.ShapeDtypeStruct(grad, BF16)] * fits,
        scratch_shapes=[pltpu.VMEM(grad, F32)] * fits + ffn_scratch(groups, [0, 1]),
        compiler_params=PARAMS,
        name="mix_back",
        cost_estimate=cost(1, 1),
    )(*flat_of(groups), *acts, *d1, mixed, dy, ot, *w, place, home, gain)
    if not fits:
        spread = dot(home, ot, 0, 0).astype(BF16)
        out = [*out, dot(spread, out[0].astype(BF16), 1, 1).astype(BF16)]
    return out


def grads_body(per, groups, parts, n_ref, *refs):
    d_refs, refs = refs[:groups], refs[groups:]
    places, refs = refs[: len(parts)], refs[len(parts) :]
    outs, (acc, d_scr) = refs[: 2 * len(parts)], refs[2 * len(parts) :]
    row = pl.program_id(0)
    n = n_ref[...]
    for g, d_ref in enumerate(d_refs):

        @pl.when(row // per == g)
        def _():
            d_scr[...] = d_ref[...].reshape(d_scr.shape)

    products = []
    for (start, stop), p_ref in zip(parts, places):
        spread = dot(p_ref[...], d_scr[start:stop], 0, 0).astype(BF16)
        products.append(dot(spread, n, 1, 1))

    @pl.when(row == 0)
    def _():
        for j, product in enumerate(products):
            acc[j] = product

    @pl.when(row > 0)
    def _():
        for j, product in enumerate(products):
            acc[j] += product

    @pl.when(row == pl.num_programs(0) - 1)
    def _():
        half = acc.shape[1] // 2
        for j in range(len(parts)):
            outs[2 * j][...] = acc[j, :half].astype(BF16)
            outs[2 * j + 1][...] = acc[j, half:].astype(BF16)


def projection_grads(n, groups, parts, places, rows):
    if len(parts) > 1 and places[0].shape[1] > 1024:
        return [
            half
            for part, p in zip(parts, places)
            for half in projection_grads(n, groups, [part], [p], rows)
        ]
    width, here = n.shape
    size = here // rows
    per = rows // len(groups)
    rank = groups[0].ndim
    depth = groups[0].shape[-2]
    shape = (depth, size) if rank == 2 else (1, depth, size)
    wide = (places[0].shape[1], width)
    return pl.pallas_call(
        functools.partial(grads_body, per, len(groups), parts),
        grid=(rows,),
        in_specs=[pl.BlockSpec((width, size), lambda r: (0, r))]
        + group_specs(shape, len(groups), per, rank)
        + [whole(p.shape) for p in places],
        out_specs=[whole((wide[0] // 2, width))] * (2 * len(parts)),
        out_shape=[jax.ShapeDtypeStruct((wide[0] // 2, width), BF16)] * (2 * len(parts)),
        scratch_shapes=[pltpu.VMEM((len(parts),) + wide, F32), pltpu.VMEM((depth, size), BF16)],
        compiler_params=PARAMS,
        name="projection_grads",
        cost_estimate=cost(
            2 * len(parts) * wide[0] * width * here, 2 * n.size + 2 * len(parts) * wide[0] * width
        ),
    )(n, *groups, *places)


def last_body(per, groups, x_ref, dm_ref, *refs):
    dq_refs, dkv_refs, refs = refs[:groups], refs[groups : 2 * groups], refs[2 * groups :]
    ws, places, refs = (refs[:2], refs[2:4], refs[4:6]), refs[6:9], refs[9:]
    gain_ref, gx_ref, gg_ref, d_scr = refs
    row = pl.program_id(0)
    inner = dq_refs[0].shape[0]
    for g in range(groups):

        @pl.when(row // per == g)
        def _():
            d_scr[:inner] = dq_refs[g][...]
            d_scr[inner:] = dkv_refs[g][0, : 2 * inner]

    dn = None
    for j in range(3):
        spread = dot(places[j][...], d_scr[j * inner : (j + 1) * inner], 0, 0).astype(BF16)
        term = back(ws[j], spread)
        dn = term if dn is None else dn + term
    x = x_ref[0].astype(F32)
    scale = lax.rsqrt(jnp.mean(x * x, axis=0, keepdims=True) + NORM_EPSILON)
    unit = x * scale
    scaled = dn * gain_ref[...]
    inside = jnp.mean(scaled * unit, axis=0, keepdims=True)
    gx_ref[0] = dm_ref[...] + scale * (scaled - unit * inside)
    both = dn * unit
    gain_part = both[:, :128]
    for j in range(1, both.shape[1] // 128):
        gain_part = gain_part + both[:, j * 128 : (j + 1) * 128]

    @pl.when(row == 0)
    def _():
        gg_ref[...] = gain_part

    @pl.when(row > 0)
    def _():
        gg_ref[...] += gain_part


def last(x, dmixed, dqs, dkvs, ws, places, gain):
    rows, width, size = x.shape
    inner = dqs[0].shape[0]
    per = rows // len(dqs)
    col = pl.BlockSpec((width, size), lambda r: (0, r))
    block = pl.BlockSpec((1, width, size), lambda r: (r, 0, 0))
    return pl.pallas_call(
        functools.partial(last_body, per, len(dqs)),
        grid=(rows,),
        in_specs=[block, col]
        + group_specs((inner, size), len(dqs), per, 2)
        + group_specs((1,) + dkvs[0].shape[1:], len(dkvs), per, 3)
        + [spec for w, index in zip(ws, (1, 0, 0)) for spec in picked(w, index)]
        + [whole(p.shape) for p in places]
        + [whole(gain.shape)],
        out_specs=[block, whole((width, 128))],
        out_shape=[jax.ShapeDtypeStruct(x.shape, F32), jax.ShapeDtypeStruct((width, 128), F32)],
        scratch_shapes=[pltpu.VMEM((3 * inner, size), BF16)],
        compiler_params=PARAMS,
        name="last",
        cost_estimate=cost(1, 1),
    )(x, dmixed, *dqs, *dkvs, *[w for pair in ws for w in pair], *places, gain)


def after(value, *markers):
    return lax.optimization_barrier((value, markers))[0]


def pad_rows(w, rows):
    return jnp.pad(w, ((0, rows - w.shape[0]), (0, 0))) if rows > w.shape[0] else w


class Links:
    def __init__(self, dp, pairs):
        self.sizes = {"dp": dp, "x": pairs, "core": 2}
        self.strides = {"dp": 2 * pairs, "x": 2, "core": 1}
        self.core = ("core", 1)
        self.across = ("x", 1)
        self.near = ("dp", 1)
        self.far_count = dp // 2

    def swap(self, x, step):
        axis, mask = step
        return lax.ppermute(x, axis, [(i, i ^ mask) for i in range(self.sizes[axis])])

    def far_steps(self):
        return [("dp", k << 1) for k in range(1, self.far_count)]

    def far_bits(self):
        return [("dp", 2 << b) for b in range(self.far_count.bit_length() - 1)]

    def masks(self, steps):
        found = [(k << 1) * self.strides["dp"] for k in range(self.far_count)]
        for axis, mask in steps:
            found = found + [f ^ (mask * self.strides[axis]) for f in found]
        return found


def per_device(
    dp, ctx,
    tokens, soft_mask, segment_ids, buckets, gain_attn, gain_ffn, bias_table,
    w_query, w_key, w_value, w_attn_out, w_gate, w_up, w_ffn_out, cotangent,
):
    links = Links(dp, ctx // 2)
    swap, core, across, near = links.swap, links.core, links.across, links.near
    far = links.far_steps()
    rows, size, width = tokens.shape
    here = rows * size
    count, heads = bias_table.shape
    inner = heads * HEAD
    my_dp, my_ctx = lax.axis_index("dp"), lax.axis_index("x") * 2 + lax.axis_index("core")
    me = my_dp * ctx + my_ctx
    tile = min(512, here)
    order_a, order_b = [near, across], [across, near]

    def spread_of(steps):
        real = w_query.shape[0]
        owners = me ^ jnp.asarray(links.masks(steps), dtype=jnp.int32)
        inside = jnp.arange(each)
        feature = owners[:, None] * real + inside[None, :]
        feature = jnp.where(inside[None, :] < real, feature, -1).reshape(-1)
        return (jnp.arange(inner)[:, None] == feature[None, :]).astype(BF16)

    token = []

    def run(work, *args):
        if token:
            args = lax.optimization_barrier((args, tuple(token)))[0]
        out = work(*args)
        token[:] = jax.tree.leaves(out)
        return out

    each = -(-w_query.shape[0] // ROW_TILE) * ROW_TILE
    slot = lambda w: pad_rows(w, each)[None]
    flat = lambda w: w.reshape(-1, width)
    far_bits = links.far_bits()
    ab, ba = (near, across), (across, near)

    def exchange(arrays, steps):
        return [(a, swap(a, step)) for a, step in zip(arrays, steps)]

    def swap_core(value):
        return [swap(v, core) for v in value]

    def close(value):
        return run(lambda v: v, value)

    class Gather:
        def __init__(self, array, cuts, direct=False, mark=None, paths=(ab, ba)):
            if mark is not None:
                array = after(array, mark)
            self.cuts, self.stage, self.paths = cuts, 0, paths
            self.hops = 1 if direct else len(far_bits)
            steps = far if direct else far_bits[:1]
            self.held = [array] + [swap(array, step) for step in steps]

        def go(self):
            self.stage += 1
            if self.stage < self.hops:
                (array,) = run(lambda *p: join([p]), *self.held)
                self.held = [array, swap(array, far_bits[self.stage])]
            elif self.stage == self.hops:
                parts = run(lambda *p: cut_join(list(p), self.cuts), *self.held)
                self.held = exchange(parts, self.paths[0])
            elif self.stage == self.hops + 1:
                self.held = exchange(run(join, self.held), self.paths[1])

        def start_of(self):
            first = self.held[0]
            return first[0] if isinstance(first, tuple) else first

        def core_go(self):
            self.held = exchange(run(join, self.held), (core, core))

        def core_end(self):
            return close([list(pair) for pair in self.held])

    attn_w = Gather(
        jnp.concatenate([slot(w) for w in (w_key, w_attn_out, w_value, w_query)], axis=1)[:, None],
        [(0, 2 * each), (2 * each, 2 * each)],
        direct=True,
    )
    units = -(-w_gate.shape[0] // ROW_TILE)
    ffn_own = after((w_gate, w_up, w_ffn_out), attn_w.held[0])
    padded = [pad_rows(w, units * ROW_TILE) for w in ffn_own]
    marks = [0, 3, 5, 7] if units == 7 else list(range(units + 1))
    shards = [
        jnp.stack([w[low * ROW_TILE : high * ROW_TILE] for w in padded])
        for low, high in zip(marks, marks[1:])
    ]
    same_core = ("dp", "x")
    by_hops = units == 7
    last_group = len(shards) - 1

    x = jnp.transpose(tokens, (0, 2, 1))
    dy = jnp.transpose(cotangent, (0, 2, 1))
    gain_one, gain_two = gain_attn[:, None], gain_ffn[:, None]
    place_a, place_b = spread_of(order_a + [core]), spread_of(order_b + [core])
    real = w_query.shape[0]
    segs = lax.dynamic_slice_in_dim(segment_ids, my_ctx * size, size, 1)
    same = segs[:, None, :] == jnp.arange(DOCS, dtype=segs.dtype)[None, :, None]
    ones = jnp.ones((rows, 1, size), BF16)
    rest = AUG - 1 - DOCS
    aug = jnp.concatenate(
        [soft_mask[:, None, :], same.astype(BF16)] + [ones] * 3
        + [jnp.zeros((rows, rest - 3, size), BF16)],
        axis=1,
    )
    query_aug = jnp.concatenate(
        [ones, jnp.where(same, 0.0, MASK_VALUE).astype(BF16), jnp.zeros((rows, rest, size), BF16)],
        axis=1,
    )
    normed, dy_pair, *dy_own = run(first_norm, x, dy, gain_one)
    place_a, place_b, aug, query_aug, shards = close((place_a, place_b, aug, query_aug, shards))

    attn_w.go()
    ffn_w = [
        [lax.all_gather(after(shard, attn_w.start_of()), same_core)]
        for shard in (shards[:-1] if by_hops else shards)
    ]
    slots = jnp.array([0, 2, 1, 3], jnp.int32) ^ my_ctx
    bias, buckets_t = run(
        bias_of, slots, buckets, jnp.pad(bias_table.T, ((0, 0), (0, 128 - count)))
    )
    dy_parts = swap_core(dy_own)
    attn_w.go()
    if by_hops:
        last_w = Gather(
            shards[-1][None],
            [(0, shards[-1].shape[1])],
            mark=attn_w.start_of(),
            paths=((near,), (across,)),
        )
    dy_pair = run(fill, dy_pair, dy_parts)
    if by_hops:
        last_w.go()
    attn_w.core_go()
    wko, wvq = attn_w.core_end()
    kv_own = run(lambda *a: key_value(*a, 0, rows), normed, wko, wvq, place_a, place_b, aug)
    kv_across = swap(kv_own, across)
    kv_core = swap(kv_own, core)
    queries = run(lambda n, w, p: project(n, w, p, tile), normed, wvq, place_b)
    kv_core = close(kv_core)
    if by_hops:
        last_w.go()

    kv = run(lambda *k: list(k), kv_own, kv_across, kv_core)
    kv.append(close(jnp.concatenate([swap(k, core) for k in jnp.split(kv[1], min(2, rows))])))
    attended, lse = run(lambda *a: attend(*a, heads, 0), queries, query_aug, kv, bias)
    if by_hops:
        last_w.go()
    mixed, n_pair, *normed_two = run(mix, x, attended, wko, place_a, gain_two)
    n_parts = close(swap_core(normed_two))
    n_pair = run(fill, n_pair, n_parts)

    class Sums:
        def __init__(self, grads, paths, direct=False):
            self.paths, self.direct = paths[: len(grads)], direct
            self.stage = 0
            self.send(grads)

        def send(self, halves):
            self.keep = [h[0] for h in halves]
            self.got = [swap(h[1], p[self.stage]) for h, p in zip(halves, self.paths)]

        def go(self):
            near_hops = len(self.paths[0])
            hops = near_hops + (1 if self.direct else len(far_bits))
            self.stage += 1
            if self.stage > hops:
                return
            if self.stage < near_hops:
                self.send(run(add_halves, self.keep, self.got))
                return
            if self.stage == near_hops:
                rows_of = [k.shape[-2] for k in self.keep]
                self.edges = [sum(rows_of[:k]) for k in range(len(rows_of) + 1)]
                if self.direct:
                    piles = run(lambda k, r: add_piles(k, r, self.edges), self.keep, self.got)
                    self.keep = [piles[0]]
                    self.got = [swap(pile, step) for pile, step in zip(piles[1:], far)]
                    return
                halves = run(lambda k, r: add_merge(k, r, self.edges), self.keep, self.got)
            elif self.stage < hops:
                halves = run(add_halves, self.keep, self.got)[0]
            else:
                got = after(self.got, *token)
                self.out = add_last(self.keep[0], got, self.edges)
                return
            self.keep = [halves[0]]
            self.got = [swap(halves[1], far_bits[hops - 1 - self.stage])]

    acts, sums = [], []
    me_same = (my_dp * (ctx // 2) + lax.axis_index("x")).reshape(1)
    masks = [[m >> 1 for m in links.masks(steps)] for steps in (ab, ba)]
    ffn_grads = {}
    if by_hops:
        ffn_w.append(None)
    sequence = [0, 2, 1] if by_hops else range(len(ffn_w))
    by_group = {}
    for i in sequence:
        ws = ffn_w[i]
        if i == last_group and by_hops:
            ws = ffn_w[i] = last_ws
        some = tile if units_of(ws) <= 768 else tile // 2
        mask = masks[1] if by_hops and i == last_group - 1 else None
        act, grads = run(
            lambda m, w, n, d: ffn_group(m, w, n, d, some, mask), me_same, ws, n_pair, dy_pair
        )
        by_group[i] = act
        if by_hops and i == 0:
            last_ws = close(list(last_w.held[0]))
            grads = [after(g, last_ws) for g in grads]
        ffn_grads[i] = grads if by_hops and i else lax.psum_scatter(grads[0], same_core)
    ffn_grads = [ffn_grads[i] for i in range(len(ffn_w))]
    acts = [by_group[i] for i in range(len(ffn_w))]
    if by_hops:
        sums = [Sums(ffn_grads[-2:], [ab, ba])]

    def tick():
        for s in sums:
            s.go()

    back = run(lambda p, a: ffn_back(p, a, [0, 1], here, here, tile, PIECES), ffn_w, acts)
    dn_got = swap_core(back)
    (out_other,) = run(lambda p, a: ffn_back(p, a, [2], here, here, tile, 1), ffn_w, acts)
    dn_got = close(dn_got)
    out_got = swap(out_other, core)

    dmixed, dattended, gain_two_part, gwo = run(
        mix_back, ffn_w, acts, mixed, dn_got, dy, attended, wko, place_a, place_b, gain_two
    )
    tick()
    out_got = close(out_got)
    dq, dkv, grad_bias = run(
        lambda *a: attend_back(*a, heads, 0, []),
        queries, query_aug, kv, bias, attended, dattended, lse,
    )
    by_core = [(dkv[0], swap(dkv[2], core)), (dkv[1], swap(dkv[3], core))]
    tick()
    entries = lambda g: tuple(v.reshape(-1, each, width) for v in g)
    home_a, home_b = (core,) + ba, (core,) + ab
    own, other = run(add_pairs, by_core)
    other = swap(other, across)
    gwq = run(
        lambda n, d, p: projection_grads(n, [d], [(0, inner)], [p], rows), normed, dq, place_b
    )
    if by_hops:
        ffn_grads[0] = close(ffn_grads[0])
    part = gwo.shape[0] // 2
    query_sum = Sums([entries((gwo[:part], gwo[part:])), entries(gwq)], [home_b, home_b])
    grad_table = run(lambda g, b: bucket_sums(g, b, count), grad_bias, buckets_t)
    out = run(lambda *a: layer_out_of(*a, rows), ffn_w, acts, mixed, out_got)
    tick()
    query_sum.go()
    (dkv,) = run(add_pairs, [(own, other)])
    gkv = run(
        lambda n, d, pa, pb: projection_grads(n, [d], [(0, inner), (inner, 2 * inner)], [pa, pb], rows),
        normed, dkv, place_a, place_b,
    )
    value_sum = Sums([entries(gkv[:2]), entries(gkv[2:])], [home_a, home_b], direct=dp <= 8)
    query_sum.go()
    value_sum.go()
    gx, gain_one_part = run(
        lambda *a: last(a[0], a[1], [a[2]], [a[3]], a[4:7], a[7:10], a[10]),
        x, dmixed, dq, dkv, wvq, wko, wvq, place_b, place_a, place_b, gain_one,
    )
    value_sum.go()
    tick()
    query_sum.go()
    small = jnp.concatenate(
        [jnp.sum(gain_one_part, 1), jnp.sum(gain_two_part, 1), grad_table.reshape(-1)]
    )
    length = small.shape[0]
    small = jnp.pad(small, (0, -length % 1024)).reshape(-1, 128)
    bits = [core, across] + [("dp", 1 << b) for b in range(dp.bit_length() - 1)]
    for k, one in enumerate(bits):
        got = swap(small, one)
        if k == 1:
            value_sum.go()
            query_sum.go()
        if k == 3:
            value_sum.got = close(value_sum.got)
        small = run(lambda a, b: a + b, small, got)
    for _ in range(len(far_bits) + 4):
        for s in [query_sum, value_sum] + sums:
            s.go()
    small = small.reshape(-1)
    if by_hops:
        ffn_grads[-2:] = sums[0].out
    grad_gate, grad_up, grad_ffn_out = (
        jnp.concatenate([g[j].astype(F32) for g in ffn_grads])[: w_gate.shape[0]] for j in range(3)
    )
    return (
        jnp.transpose(out, (0, 2, 1)),
        jnp.transpose(gx, (0, 2, 1)),
        dkv[:, 2 * inner].astype(F32),
        small[:width],
        small[width : 2 * width],
        small[2 * width : length].reshape(count, heads),
        query_sum.out[1][:real],
        value_sum.out[0][:real],
        value_sum.out[1][:real],
        query_sum.out[0][:real],
        grad_gate,
        grad_up,
        grad_ffn_out,
    )


def solution(mesh):
    dp, ctx = mesh.shape["dp"], mesh.shape["ctx"]
    by_core = Mesh(mesh.devices.reshape(dp, ctx // 2, 2), ("dp", "x", "core"))
    ctx_axes = ("x", "core")
    split = P(("dp", "x", "core"), None)
    act = P("dp", ctx_axes, None)
    in_specs = (
        (act, P("dp", ctx_axes), P("dp", None), P(ctx_axes, None), P(), P(), P()) + (split,) * 7 + (act,)
    )
    out_specs = (act, act, P("dp", ctx_axes), P(), P(), P()) + (split,) * 7
    return jax.shard_map(
        functools.partial(per_device, dp, ctx),
        mesh=by_core,
        in_specs=in_specs,
        out_specs=out_specs,
        check_vma=False,
    )
```
